32 devices in a mesh: gx: 16 (over z, y, x), ta: 2 (over core).
Axes of the slice: x: 2, y: 2, z: 4, core: 2. Of those that a mesh axis runs over, the one named last changes fastest.
Arguments:
- query_vecs: bfloat16 [256, 16, 5120], P('gx', None, 'ta'), may hold values from -32 to 32
- key_vecs: bfloat16 [256, 16, 5120], P('gx', None, 'ta'), may hold values from -6 to 6
- value_vecs: bfloat16 [256, 16, 5120], P('gx', None, 'ta'), may hold values from -6 to 6
- slot_map: int32 [16, 16], replicated, may hold values from 0 to 15, each once within a row
- edge_list: int32 [64, 2], replicated, may hold values from 0 to 15
- edge_types: int32 [64], replicated, may hold values from 0 to 2
- type_gain: float32 [2, 3, 5120], P(None, None, 'ta'), may hold values from 0.25 to 2
- norm_gain: float32 [2, 5120], P(None, 'ta'), may hold values from 0.5 to 2
- gate_proj: bfloat16 [2, 5120, 20480], P(None, 'ta', 'gx'), may hold values from -0.078125 to 0.078125
- up_proj: bfloat16 [2, 5120, 20480], P(None, 'ta', 'gx'), may hold values from -0.078125 to 0.078125
- down_proj: bfloat16 [2, 20480, 5120], P(None, 'gx', 'ta'), may hold values from -0.0390625 to 0.0390625
Outputs:
- node_states: bfloat16 [128, 5120], P('gx', 'ta')
The draws below stay inside these ranges and needn't reach their ends.
All inputs are finite; a program needn't handle non-finite values.
Results may differ from the reference program's by a relative error of at most 0.04.
Values may be sent and summed in bfloat16 or wider, within the bound.
No kernel may reach another device: no remote copies, remote signals or barrier semaphores. Data moves between devices by JAX's collectives and lax.ppermute only.
A program may use at most 128 MiB of HBM per device.

```python
import math
import jax
import jax.numpy as jnp
import numpy as np
from jax import lax

D = 5120
HEAD_DIM = 128
FF = 20480
VENUES = 16
STEPS = 16
NODE_STEPS = 8
ROUNDS = 2
ETYPES = 3
INST_DEV = 1
INST = 16
PAIRS = 256
EDGES = 64
N_GX = 16


def paired_draw(key):
    shape_full = (VENUES, STEPS, INST, D)
    key_one = jax.random.fold_in(key, 101)
    key_two = jax.random.fold_in(key, 202)
    keyset = jax.random.truncated_normal(key_one, -6.0, 6.0, shape_full, jnp.float32)
    queries = jax.random.truncated_normal(key_two, -6.0, 6.0, shape_full, jnp.float32)
    return (queries.reshape(VENUES * STEPS, INST, D), keyset.reshape(VENUES * STEPS, INST, D))


def draw_query_vecs(key, part):
    return paired_draw(key)[0].astype(jnp.bfloat16)


def draw_key_vecs(key, part):
    return paired_draw(key)[1].astype(jnp.bfloat16)


def plant(entries, stream_key, smallest, high):
    longest = entries.shape.index(max(entries.shape))
    spots = []
    for shift in (0, 1):
        where = [jax.random.randint(jax.random.fold_in(stream_key, axis), (), 0, length) for axis, length in enumerate(entries.shape)]
        where[longest] = (where[longest] + shift) % entries.shape[longest]
        spots.append(tuple(where))
    return entries.at[spots[0]].set(smallest).at[spots[1]].set(high)


def block_levels(own_key, extent, split, smallest, high):
    factor_of = 1.0
    for dim, blocks in split:
        steps = jax.random.uniform(jax.random.fold_in(jax.random.fold_in(own_key, 6), dim), (blocks,), jnp.float32, smallest / len(split), high / len(split))
        factor_of = factor_of * jnp.repeat(jnp.exp(steps), extent[dim] // blocks).reshape((-1,) + (1,) * (len(extent) - 1 - dim))
    return factor_of


def rank_table(number_of, lean):
    loads = [(1 << 20) // math.isqrt(rank ** lean) + 1 for rank in range(1, number_of + 1)]
    spread = 1 + sum(loads) // (1 << 30)
    return np.cumsum(np.array([max(1, weight // spread) for weight in loads]))


def skewed_ids(stream_key, dims, number_of, slope):
    listing = rank_table(number_of, slope)
    ticket = jax.random.randint(jax.random.fold_in(stream_key, 1), dims, 0, int(listing[number_of - 1]))
    standing = jnp.searchsorted(jnp.asarray(listing, jnp.int32), ticket, side="right")
    return jax.random.permutation(jax.random.fold_in(stream_key, 2), number_of)[standing].astype(jnp.int32)


def scatter_about(key, shape, deviation, most, split=(), held_as=jnp.bfloat16):
    values = deviation * jax.random.normal(key, shape, jnp.float32)
    if split:
        values = values * block_levels(key, shape, split, -0.22, 0.18)
    return jnp.clip(values, -most, most).astype(held_as)


def setup_inputs(seed: int = 0) -> dict:
    streams_of = jax.random.split(jax.random.key(seed), 12)
    return {
        "query_vecs": draw_query_vecs(jax.random.fold_in(streams_of[11], 71), 0),
        "key_vecs": draw_key_vecs(jax.random.fold_in(streams_of[11], 71), 0),
        "value_vecs": scatter_about(streams_of[2], (PAIRS, INST, D), 1.0, 6.0, ((0, 16), (2, 2))),
        "slot_map": jax.vmap(lambda own: jax.random.permutation(own, INST))(jax.random.split(streams_of[3], VENUES)).reshape((VENUES, INST)).astype(jnp.int32),
        "edge_list": plant(skewed_ids(streams_of[4], (EDGES, 2), INST, 2), jax.random.fold_in(streams_of[4], 3), 0, INST - 1).astype(jnp.int32),
        "edge_types": plant(jax.random.randint(streams_of[5], (EDGES,), 0, ETYPES), jax.random.fold_in(streams_of[5], 1), 0, ETYPES - 1).astype(jnp.int32),
        "type_gain": jnp.clip(jnp.exp(math.log(2.0) - 2.0794415 * jax.random.uniform(streams_of[6], (ROUNDS, ETYPES, D), jnp.float32) ** block_levels(streams_of[6], (ROUNDS, ETYPES, D), ((2, 2),), -0.2, 0.2)), 0.25, 2.0),
        "norm_gain": jnp.clip(jnp.exp(math.log(2.0) - 1.3862944 * jax.random.uniform(streams_of[7], (ROUNDS, D), jnp.float32) ** block_levels(streams_of[7], (ROUNDS, D), ((1, 2),), -0.2, 0.2)), 0.5, 2.0),
        "gate_proj": scatter_about(streams_of[8], (ROUNDS, D, FF), D ** -0.5, 0.078125, ((1, 2), (2, 16))),
        "up_proj": scatter_about(streams_of[9], (ROUNDS, D, FF), D ** -0.5, 0.078125, ((1, 2), (2, 16))),
        "down_proj": scatter_about(streams_of[10], (ROUNDS, FF, D), FF ** -0.5, 0.0390625, ((1, 16), (2, 2))),
    }


def reference(query_vecs, key_vecs, value_vecs, slot_map, edge_list, edge_types, type_gain, norm_gain, gate_proj, up_proj, down_proj):
    pair_total = VENUES * STEPS
    inst_total = INST_DEV * N_GX
    head_count = D // HEAD_DIM
    score_scale = 1.0 / HEAD_DIM ** 0.5
    pair_ids = jnp.arange(pair_total).astype(jnp.int32)
    venue_of = (pair_ids // STEPS).astype(jnp.int32)
    slot_order = slot_map[venue_of]
    query_steps = jnp.arange(VENUES * NODE_STEPS) % NODE_STEPS + (STEPS - NODE_STEPS)
    key_steps = jnp.arange(pair_total) % STEPS
    allowed = key_steps[None, :] <= query_steps[:, None]

    def attend_one(inst_idx):
        columns = slot_order[:, inst_idx].astype(jnp.int32)
        queries = query_vecs[pair_ids, columns]
        keyset = key_vecs[pair_ids, columns]
        valueset = value_vecs[pair_ids, columns]
        queries = queries.reshape(VENUES, STEPS, head_count, HEAD_DIM)[:, STEPS - NODE_STEPS:]
        queries = queries.reshape(VENUES * NODE_STEPS, head_count, HEAD_DIM)
        keyset = keyset.reshape(pair_total, head_count, HEAD_DIM)
        valueset = valueset.reshape(pair_total, head_count, HEAD_DIM)
        scores = jnp.einsum('qhd,khd->hqk', queries.astype(jnp.float32), keyset.astype(jnp.float32)) * score_scale
        scores = jnp.where(allowed[None], scores, jnp.float32(-1e+30))
        row_max = lax.optimization_barrier(jnp.max(scores, axis=-1, keepdims=True))
        expd = jnp.exp(scores - row_max)
        probs = (expd / lax.optimization_barrier(jnp.sum(expd, axis=-1, keepdims=True))).astype(jnp.bfloat16)
        attended = jnp.einsum('hqk,khd->qhd', probs.astype(jnp.float32), valueset.astype(jnp.float32))
        return lax.optimization_barrier(jnp.mean(attended.reshape(VENUES, NODE_STEPS, D), axis=0)).astype(jnp.bfloat16)
    nodes = lax.map(attend_one, jnp.arange(inst_total).astype(jnp.int32))
    nodes = nodes.reshape(inst_total * NODE_STEPS, D)
    node_ids = jnp.arange(inst_total).astype(jnp.int32)
    type_ids = jnp.arange(ETYPES).astype(jnp.int32)
    at_source = (edge_list[:, 0][:, None] == node_ids[None, :]).astype(jnp.float32)
    at_target = (edge_list[:, 1][:, None] == node_ids[None, :]).astype(jnp.float32)
    of_type = (edge_types[:, None] == type_ids[None, :]).astype(jnp.float32)
    adjacency = jnp.einsum('et,ei,ej->tij', of_type, at_target, at_source)
    degree = jnp.maximum(lax.optimization_barrier(jnp.sum(at_target, axis=0)), 1.0)
    adj_rows = adjacency.reshape(ETYPES * inst_total, inst_total).astype(jnp.bfloat16)
    for layer_idx in range(ROUNDS):
        flat_nodes = nodes.reshape(inst_total, NODE_STEPS * D)
        gathered = jnp.dot(adj_rows, flat_nodes, preferred_element_type=jnp.float32)
        gathered = gathered.reshape(ETYPES, inst_total, NODE_STEPS, D)
        message = lax.optimization_barrier(jnp.sum(gathered * type_gain[layer_idx][:, None, None, :], axis=0)) / degree[:, None, None]
        pre_norm = nodes.astype(jnp.float32) + message.reshape(inst_total * NODE_STEPS, D)
        row_scale = lax.rsqrt(lax.optimization_barrier(jnp.mean(pre_norm * pre_norm, axis=-1, keepdims=True)) + 1e-05)
        normed = (pre_norm * row_scale * norm_gain[layer_idx][None, :]).astype(jnp.bfloat16)
        gate_sum = jnp.dot(normed, gate_proj[layer_idx], preferred_element_type=jnp.float32)
        up_sum = jnp.dot(normed, up_proj[layer_idx], preferred_element_type=jnp.float32)
        hidden = (jax.nn.silu(gate_sum) * up_sum).astype(jnp.bfloat16)
        update = jnp.dot(hidden, down_proj[layer_idx], preferred_element_type=jnp.float32)
        nodes = (nodes.astype(jnp.float32) + update).astype(jnp.bfloat16)
    return nodes
```

```python
import jax
import jax.numpy as jnp
from jax import lax
from jax.sharding import PartitionSpec as P

D = 5120
HEAD_DIM = 128
VENUES = 16
STEPS = 16
NODE_STEPS = 8
ROUNDS = 2
ETYPES = 3


def flip_pairs(count, bit):
    return [(i, i ^ (1 << bit)) for i in range(count)]


def stage_bits(count):
    return list(range(count.bit_length() - 1))


def scatter_rows(partial, gx_count):
    me = lax.axis_index("gx")
    held = partial.astype(jnp.float32)
    for bit in stage_bits(gx_count):
        half = held.shape[0] // 2
        side = (me >> bit) & 1
        keep = lax.dynamic_slice_in_dim(held, side * half, half, 0)
        give = lax.dynamic_slice_in_dim(held, (1 - side) * half, half, 0).astype(jnp.bfloat16)
        held = keep + lax.ppermute(give, "gx", flip_pairs(gx_count, bit)).astype(jnp.float32)
    return held


def gather_rows(own, gx_count):
    me = lax.axis_index("gx")
    held = own
    for bit in reversed(stage_bits(gx_count)):
        side = (me >> bit) & 1
        other = lax.ppermute(held, "gx", flip_pairs(gx_count, bit))
        held = jnp.where(
            side == 0,
            jnp.concatenate([held, other], axis=0),
            jnp.concatenate([other, held], axis=0),
        )
    return held


def sum_over_ta(part, ta_count):
    if ta_count == 2:
        return part.astype(jnp.float32) + lax.ppermute(part, "ta", [(0, 1), (1, 0)]).astype(
            jnp.float32
        )
    return lax.psum(part, "ta").astype(jnp.float32)


def per_device(
    query_vecs,
    key_vecs,
    value_vecs,
    slot_map,
    edge_list,
    edge_types,
    type_gain,
    norm_gain,
    gate_proj,
    up_proj,
    down_proj,
):
    pairs_dev, inst_total, feat_width = query_vecs.shape
    head_count = feat_width // HEAD_DIM
    gx_count = lax.axis_size("gx")
    ta_count = lax.axis_size("ta")
    inst_local = inst_total // gx_count
    score_scale = 1.0 / HEAD_DIM**0.5
    venue_idx = lax.axis_index("gx") * pairs_dev // STEPS
    slot_order = lax.dynamic_index_in_dim(slot_map, venue_idx, 0, keepdims=False)

    def by_instrument(vecs):
        pairs = vecs.shape[0]
        rows = pairs * inst_total
        row = jnp.arange(rows)
        source = (row % pairs) * inst_total + slot_order[row // pairs]
        pick = (source[:, None] == row[None, :]).astype(jnp.bfloat16)
        return jnp.dot(
            pick, vecs.reshape(rows, feat_width), preferred_element_type=jnp.float32
        ).astype(jnp.bfloat16)

    def to_instrument(vecs):
        rows = by_instrument(vecs)
        return lax.all_to_all(rows, "gx", split_axis=0, concat_axis=0, tiled=True)

    whole_venue = pairs_dev == STEPS
    if whole_venue:
        query_vecs = query_vecs[STEPS - NODE_STEPS :]
    queries = to_instrument(query_vecs)
    keyset = to_instrument(key_vecs)
    valueset = to_instrument(value_vecs)
    pair_total = VENUES * STEPS
    if whole_venue:
        queries = queries.reshape(VENUES * NODE_STEPS, head_count, HEAD_DIM)
    else:
        queries = queries.reshape(VENUES, STEPS, head_count, HEAD_DIM)[:, STEPS - NODE_STEPS :]
        queries = queries.reshape(VENUES * NODE_STEPS, head_count, HEAD_DIM)
    keyset = keyset.reshape(pair_total, head_count, HEAD_DIM)
    valueset = valueset.reshape(pair_total, head_count, HEAD_DIM)
    query_steps = jnp.arange(VENUES * NODE_STEPS) % NODE_STEPS + (STEPS - NODE_STEPS)
    key_steps = jnp.arange(pair_total) % STEPS
    allowed = key_steps[None, :] <= query_steps[:, None]
    scores = (
        jnp.einsum("qhd,khd->hqk", queries, keyset, preferred_element_type=jnp.float32)
        * score_scale
    )
    scores = jnp.where(allowed[None], scores, jnp.float32(-1e30))
    row_max = jnp.max(scores, axis=-1, keepdims=True)
    expd = jnp.exp(scores - row_max)
    probs = (expd / jnp.sum(expd, axis=-1, keepdims=True)).astype(jnp.bfloat16)
    attended = jnp.einsum("hqk,khd->qhd", probs, valueset, preferred_element_type=jnp.float32)
    attended = attended.reshape(VENUES, NODE_STEPS, feat_width)
    own_rows = jnp.mean(attended, axis=0).astype(jnp.bfloat16)

    bits = stage_bits(gx_count)
    place = jnp.arange(inst_total)
    inst_at = sum((((place >> b) & 1) << (len(bits) - 1 - b)) for b in bits)
    at_source = (edge_list[:, 0][:, None] == inst_at[None, :]).astype(jnp.float32)
    at_target = (edge_list[:, 1][:, None] == inst_at[None, :]).astype(jnp.float32)
    of_type = (edge_types[:, None] == jnp.arange(ETYPES)[None, :]).astype(jnp.float32)
    adjacency = jnp.einsum("et,ei,ej->tij", of_type, at_target, at_source)
    degree = jnp.maximum(jnp.sum(at_target, axis=0), 1.0)
    adj_rows = adjacency.reshape(ETYPES * inst_total, inst_total).astype(jnp.bfloat16)
    row_total = inst_total * NODE_STEPS
    ff_dev = gate_proj.shape[2]
    for layer_idx in range(ROUNDS):
        nodes = gather_rows(own_rows, gx_count)
        flat_nodes = nodes.reshape(inst_total, NODE_STEPS * feat_width)
        gathered = jnp.dot(adj_rows, flat_nodes, preferred_element_type=jnp.float32)
        gathered = gathered.reshape(ETYPES, inst_total, NODE_STEPS, feat_width)
        message = (
            jnp.sum(gathered * type_gain[layer_idx][:, None, None, :], axis=0)
            / degree[:, None, None]
        )
        pre_norm = nodes.astype(jnp.float32) + message.reshape(row_total, feat_width)
        squares = lax.psum(jnp.sum(pre_norm * pre_norm, axis=-1), "ta")
        row_scale = lax.rsqrt(squares / D + 1e-05)[:, None]
        normed = (pre_norm * row_scale * norm_gain[layer_idx][None, :]).astype(jnp.bfloat16)
        gate_part = jnp.dot(normed, gate_proj[layer_idx], preferred_element_type=jnp.float32)
        up_part = jnp.dot(normed, up_proj[layer_idx], preferred_element_type=jnp.float32)
        both = jnp.concatenate(
            [gate_part.astype(jnp.bfloat16), up_part.astype(jnp.bfloat16)], axis=1
        )
        both = sum_over_ta(both, ta_count)
        hidden = (jax.nn.silu(both[:, :ff_dev]) * both[:, ff_dev:]).astype(jnp.bfloat16)
        update = jnp.dot(hidden, down_proj[layer_idx], preferred_element_type=jnp.float32)
        own_rows = (own_rows.astype(jnp.float32) + scatter_rows(update, gx_count)).astype(
            jnp.bfloat16
        )
    return own_rows


def solution(mesh):
    placed = (
        P("gx", None, "ta"),
        P("gx", None, "ta"),
        P("gx", None, "ta"),
        P(),
        P(),
        P(),
        P(None, None, "ta"),
        P(None, "ta"),
        P(None, "ta", "gx"),
        P(None, "ta", "gx"),
        P(None, "gx", "ta"),
    )
    return jax.shard_map(
        per_device, mesh=mesh, in_specs=placed, out_specs=P("gx", "ta"), check_vma=False
    )
```

```python
import jax
import jax.numpy as jnp
from jax import lax
from jax.experimental import pallas as pl
from jax.experimental.pallas import tpu as pltpu
from jax.sharding import PartitionSpec as P

D = 5120
HEAD_DIM = 128
VENUES = 16
STEPS = 16
NODE_STEPS = 8
ROUNDS = 2
ETYPES = 3
HALF_VENUES = VENUES // 2
HEADS_STEP = 5
COLS_STEP = HEADS_STEP * HEAD_DIM
ROWS_HALF = HALF_VENUES * NODE_STEPS
KEYS_HALF = HALF_VENUES * STEPS


def flip_pairs(count, bit):
    return [(i, i ^ (1 << bit)) for i in range(count)]


def stage_bits(count):
    return list(range(count.bit_length() - 1))


def scatter_rows(partial, gx_count):
    me = lax.axis_index("gx")
    held = partial.astype(jnp.float32)
    for bit in stage_bits(gx_count):
        half = held.shape[0] // 2
        side = (me >> bit) & 1
        keep = lax.dynamic_slice_in_dim(held, side * half, half, 0)
        give = lax.dynamic_slice_in_dim(held, (1 - side) * half, half, 0).astype(jnp.bfloat16)
        held = keep + lax.ppermute(give, "gx", flip_pairs(gx_count, bit)).astype(jnp.float32)
    return held


def gather_rows(own, gx_count, bits):
    me = lax.axis_index("gx")
    held = own
    for bit in reversed(bits):
        side = (me >> bit) & 1
        other = lax.ppermute(held, "gx", flip_pairs(gx_count, bit))
        held = jnp.where(
            side == 0,
            jnp.concatenate([held, other], axis=0),
            jnp.concatenate([other, held], axis=0),
        )
    return held


def sum_over_ta(part, ta_count):
    if ta_count == 2:
        return part.astype(jnp.float32) + lax.ppermute(part, "ta", [(0, 1), (1, 0)]).astype(
            jnp.float32
        )
    return lax.psum(part, "ta").astype(jnp.float32)


def arrange_body(pick_ref, key_ref, value_ref, out_ref):
    chunks, rows, cols = out_ref.shape
    pick = pick_ref[...]
    for side, ref in enumerate((key_ref, value_ref)):
        moved = jnp.dot(pick, ref[...], preferred_element_type=jnp.float32)
        moved = moved.reshape(chunks, rows // 2, cols).astype(jnp.bfloat16)
        out_ref[:, side * (rows // 2) : (side + 1) * (rows // 2), :] = moved


def arrange(pick, keys, values, chunks):
    rows, width = keys.shape
    per_chunk = 2 * rows // chunks
    return pl.pallas_call(
        arrange_body,
        grid=(width // COLS_STEP,),
        in_specs=[
            pl.BlockSpec((rows, rows), lambda j: (0, 0)),
            pl.BlockSpec((rows, COLS_STEP), lambda j: (0, j)),
            pl.BlockSpec((rows, COLS_STEP), lambda j: (0, j)),
        ],
        out_specs=pl.BlockSpec((chunks, per_chunk, COLS_STEP), lambda j: (0, 0, j)),
        out_shape=jax.ShapeDtypeStruct((chunks, per_chunk, width), jnp.bfloat16),
        compiler_params=pltpu.CompilerParams(vmem_limit_bytes=24 << 20),
        name="arrange",
    )(pick, keys, values)


def score_body(own_ref, far_ref, kv_ref, probs_ref, lse_ref):
    step = pl.program_id(0)

    @pl.when(step == 0)
    def _():
        lse_ref[...] = jnp.zeros_like(lse_ref)

    shape = (HALF_VENUES, 2, NODE_STEPS, COLS_STEP)
    own = own_ref[...].astype(jnp.float32).reshape(shape)
    far = far_ref[...].astype(jnp.float32).reshape(shape)
    full = (2 * ROWS_HALF, KEYS_HALF)
    query_step = lax.broadcasted_iota(jnp.int32, full, 0) % NODE_STEPS + (STEPS - NODE_STEPS)
    key_step = lax.broadcasted_iota(jnp.int32, full, 1) % STEPS
    allowed = key_step <= query_step
    lane = lax.broadcasted_iota(jnp.int32, lse_ref.shape, 1)
    lse = lse_ref[...]
    for item in range(2):
        queries = jnp.concatenate(
            [
                own[:, item].reshape(ROWS_HALF, COLS_STEP),
                far[:, item].reshape(ROWS_HALF, COLS_STEP),
            ],
            axis=0,
        ).astype(jnp.bfloat16)
        keys = kv_ref[:, item].reshape(KEYS_HALF, COLS_STEP)
        for head in range(HEADS_STEP):
            span = slice(head * HEAD_DIM, (head + 1) * HEAD_DIM)
            scores = lax.dot_general(
                queries[:, span],
                keys[:, span],
                (((1,), (1,)), ((), ())),
                preferred_element_type=jnp.float32,
            ) * (1.0 / HEAD_DIM**0.5)
            scores = jnp.where(allowed, scores, -1e30)
            top = jnp.max(scores, axis=1, keepdims=True)
            expd = jnp.exp(scores - top)
            total = jnp.sum(expd, axis=1, keepdims=True)
            probs_ref[head, item] = (expd * (1.0 / total)).astype(jnp.bfloat16)
            column = (step * HEADS_STEP + head) * 2 + item
            lse = jnp.where(lane == column, top + jnp.log(total), lse)
    lse_ref[...] = lse


def half_scores(own, far, kv):
    width = own.shape[1]
    rows = own.shape[0]
    heads = width // HEAD_DIM
    return pl.pallas_call(
        score_body,
        grid=(width // COLS_STEP,),
        in_specs=[
            pl.BlockSpec((rows, COLS_STEP), lambda j: (0, j)),
            pl.BlockSpec((rows, COLS_STEP), lambda j: (0, j)),
            pl.BlockSpec((HALF_VENUES, 2, STEPS, COLS_STEP), lambda j: (0, 0, 0, j)),
        ],
        out_specs=[
            pl.BlockSpec((HEADS_STEP, 2, 2 * ROWS_HALF, KEYS_HALF), lambda j: (j, 0, 0, 0)),
            pl.BlockSpec((2 * ROWS_HALF, 128), lambda j: (0, 0)),
        ],
        out_shape=[
            jax.ShapeDtypeStruct((heads, 2, 2 * ROWS_HALF, KEYS_HALF), jnp.bfloat16),
            jax.ShapeDtypeStruct((2 * ROWS_HALF, 128), jnp.float32),
        ],
        compiler_params=pltpu.CompilerParams(vmem_limit_bytes=24 << 20),
        name="half_scores",
    )(own, far, kv)


def pool_body(probs_ref, lse_ref, far_ref, kv_ref, out_ref):
    step = pl.program_id(0)
    far = jnp.concatenate([far_ref[ROWS_HALF:, :], far_ref[:ROWS_HALF, :]], axis=0)
    share = 1.0 / (1.0 + jnp.exp(far - lse_ref[...])) * (1.0 / VENUES)
    lane = lax.broadcasted_iota(jnp.int32, lse_ref.shape, 1)
    for head in range(HEADS_STEP):
        span = slice(head * HEAD_DIM, (head + 1) * HEAD_DIM)
        pooled = []
        for item in range(2):
            column = (step * HEADS_STEP + head) * 2 + item
            factor = jnp.sum(jnp.where(lane == column, share, 0.0), axis=1, keepdims=True)
            weights = probs_ref[head, item].astype(jnp.float32) * factor
            weights = jnp.sum(weights.reshape(VENUES, NODE_STEPS, KEYS_HALF), axis=0)
            values = kv_ref[:, item, :, span].reshape(KEYS_HALF, HEAD_DIM)
            pooled.append(
                jnp.dot(
                    weights.astype(jnp.bfloat16), values, preferred_element_type=jnp.float32
                )
            )
        out_ref[:, span] = jnp.concatenate(pooled, axis=0).astype(jnp.bfloat16)


def half_pool(probs, lse, far_lse, kv):
    width = kv.shape[3]
    return pl.pallas_call(
        pool_body,
        grid=(width // COLS_STEP,),
        in_specs=[
            pl.BlockSpec((HEADS_STEP, 2, 2 * ROWS_HALF, KEYS_HALF), lambda j: (j, 0, 0, 0)),
            pl.BlockSpec((2 * ROWS_HALF, 128), lambda j: (0, 0)),
            pl.BlockSpec((2 * ROWS_HALF, 128), lambda j: (0, 0)),
            pl.BlockSpec((HALF_VENUES, 2, STEPS, COLS_STEP), lambda j: (0, 1, 0, j)),
        ],
        out_specs=pl.BlockSpec((2 * NODE_STEPS, COLS_STEP), lambda j: (0, j)),
        out_shape=jax.ShapeDtypeStruct((2 * NODE_STEPS, width), jnp.bfloat16),
        compiler_params=pltpu.CompilerParams(vmem_limit_bytes=24 << 20),
        name="half_pool",
    )(probs, lse, far_lse, kv)


def per_device(
    query_vecs,
    key_vecs,
    value_vecs,
    slot_map,
    edge_list,
    edge_types,
    type_gain,
    norm_gain,
    gate_proj,
    up_proj,
    down_proj,
):
    pairs_dev, inst_total, feat_width = query_vecs.shape
    gx_count = lax.axis_size("gx")
    ta_count = lax.axis_size("ta")
    me = lax.axis_index("gx")
    bits = stage_bits(gx_count)
    chunks = gx_count // 2
    groups = [list(range(chunks)), list(range(chunks, gx_count))]
    far_half = flip_pairs(gx_count, bits[-1])
    venue_idx = me * pairs_dev // STEPS
    slot_order = lax.dynamic_index_in_dim(slot_map, venue_idx, 0, keepdims=False)

    def picker(pairs):
        rows = pairs * inst_total
        row = lax.broadcasted_iota(jnp.int32, (rows, inst_total), 0)
        inst = (row // pairs % 2) * chunks + row // (2 * pairs)
        hit = inst == lax.broadcasted_iota(jnp.int32, (rows, inst_total), 1)
        slot = jnp.sum(jnp.where(hit, slot_order[None, :], 0), axis=1, keepdims=True)
        line = lax.broadcasted_iota(jnp.int32, (rows, rows), 0)
        source = line % pairs * inst_total + slot
        return (source == lax.broadcasted_iota(jnp.int32, (rows, rows), 1)).astype(jnp.bfloat16)

    whole_venue = pairs_dev == STEPS
    if whole_venue:
        query_vecs = query_vecs[STEPS - NODE_STEPS :]
    query_pairs = query_vecs.shape[0]
    query_rows = query_pairs * inst_total
    queries = jnp.dot(
        picker(query_pairs),
        query_vecs.reshape(query_rows, feat_width),
        preferred_element_type=jnp.float32,
    ).astype(jnp.bfloat16)
    queries = lax.all_to_all(queries, "gx", 0, 0, axis_index_groups=groups, tiled=True)
    kv_rows = pairs_dev * inst_total
    kv = arrange(
        picker(pairs_dev),
        key_vecs.reshape(kv_rows, feat_width),
        value_vecs.reshape(kv_rows, feat_width),
        chunks,
    )
    kv, queries = lax.optimization_barrier((kv, queries))
    if not whole_venue:
        queries = queries.reshape(HALF_VENUES, STEPS // pairs_dev, 2, pairs_dev, feat_width)
        queries = queries[:, (STEPS - NODE_STEPS) // pairs_dev :].transpose(0, 2, 1, 3, 4)
        queries = queries.reshape(2 * ROWS_HALF, feat_width)
    far_queries = lax.ppermute(queries, "gx", far_half)
    kv = lax.all_to_all(kv, "gx", 0, 0, axis_index_groups=groups, tiled=True)
    kv = kv.reshape(HALF_VENUES, STEPS // pairs_dev, 4, pairs_dev, feat_width)
    kv = kv.transpose(0, 2, 1, 3, 4).reshape(HALF_VENUES, 4, STEPS, feat_width)
    probs, lse = half_scores(queries, far_queries, kv)
    far_lse = lax.ppermute(lse, "gx", far_half)
    pooled = half_pool(probs, lse, far_lse, kv)
    far_pooled = lax.ppermute(pooled, "gx", far_half)
    pooled = (pooled.astype(jnp.float32) + far_pooled.astype(jnp.float32)).astype(jnp.bfloat16)
    own_rows = lax.dynamic_slice_in_dim(pooled, me // chunks * NODE_STEPS, NODE_STEPS, 0)

    place = jnp.arange(inst_total)
    inst_at = sum((((place >> b) & 1) << (len(bits) - 1 - b)) for b in bits)
    at_source = (edge_list[:, 0][:, None] == inst_at[None, :]).astype(jnp.float32)
    at_target = (edge_list[:, 1][:, None] == inst_at[None, :]).astype(jnp.float32)
    of_type = (edge_types[:, None] == jnp.arange(ETYPES)[None, :]).astype(jnp.float32)
    adjacency = jnp.einsum("et,ei,ej->tij", of_type, at_target, at_source)
    degree = jnp.maximum(jnp.sum(at_target, axis=0), 1.0)
    adj_rows = adjacency.reshape(ETYPES * inst_total, inst_total).astype(jnp.bfloat16)
    row_total = inst_total * NODE_STEPS
    ff_dev = gate_proj.shape[2]
    for layer_idx in range(ROUNDS):
        if layer_idx == 0:
            nodes = gather_rows(pooled, gx_count, bits[:-1])
        else:
            nodes = gather_rows(own_rows, gx_count, bits)
        flat_nodes = nodes.reshape(inst_total, NODE_STEPS * feat_width)
        gathered = jnp.dot(adj_rows, flat_nodes, preferred_element_type=jnp.float32)
        gathered = gathered.reshape(ETYPES, inst_total, NODE_STEPS, feat_width)
        message = (
            jnp.sum(gathered * type_gain[layer_idx][:, None, None, :], axis=0)
            / degree[:, None, None]
        )
        pre_norm = nodes.astype(jnp.float32) + message.reshape(row_total, feat_width)
        squares = lax.psum(jnp.sum(pre_norm * pre_norm, axis=-1), "ta")
        row_scale = lax.rsqrt(squares / D + 1e-05)[:, None]
        normed = (pre_norm * row_scale * norm_gain[layer_idx][None, :]).astype(jnp.bfloat16)
        gate_part = jnp.dot(normed, gate_proj[layer_idx], preferred_element_type=jnp.float32)
        up_part = jnp.dot(normed, up_proj[layer_idx], preferred_element_type=jnp.float32)
        both = jnp.concatenate(
            [gate_part.astype(jnp.bfloat16), up_part.astype(jnp.bfloat16)], axis=1
        )
        both = sum_over_ta(both, ta_count)
        hidden = (jax.nn.silu(both[:, :ff_dev]) * both[:, ff_dev:]).astype(jnp.bfloat16)
        update = jnp.dot(hidden, down_proj[layer_idx], preferred_element_type=jnp.float32)
        own_rows = (own_rows.astype(jnp.float32) + scatter_rows(update, gx_count)).astype(
            jnp.bfloat16
        )
    return own_rows


def solution(mesh):
    placed = (
        P("gx", None, "ta"),
        P("gx", None, "ta"),
        P("gx", None, "ta"),
        P(),
        P(),
        P(),
        P(None, None, "ta"),
        P(None, "ta"),
        P(None, "ta", "gx"),
        P(None, "ta", "gx"),
        P(None, "gx", "ta"),
    )
    return jax.shard_map(
        per_device, mesh=mesh, in_specs=placed, out_specs=P("gx", "ta"), check_vma=False
    )
```

```python
import functools

import jax
import jax.numpy as jnp
from jax import lax
from jax.experimental import pallas as pl
from jax.experimental.pallas import tpu as pltpu
from jax.sharding import PartitionSpec as P

D = 5120
HEAD_DIM = 128
VENUES = 16
STEPS = 16
NODE_STEPS = 8
ROUNDS = 2
ETYPES = 3
HALF_VENUES = VENUES // 2
HEADS_STEP = 5
COLS_STEP = HEADS_STEP * HEAD_DIM
ROWS_HALF = HALF_VENUES * NODE_STEPS
KEYS_HALF = HALF_VENUES * STEPS
LSE_ITEM = 64


def stage_bits(count):
    return list(range(count.bit_length() - 1))


def bit_orders(gx_count, ta_count):
    plain = stage_bits(gx_count)
    if ta_count != 2:
        return [plain] * ta_count
    return [plain, [plain[1], plain[0]] + plain[2:]]


def swap_stage(block, orders, stage):
    gx_count, ta_count = lax.axis_size("gx"), lax.axis_size("ta")
    pairs = [
        (g * ta_count + t, (g ^ (1 << orders[t][stage])) * ta_count + t)
        for g in range(gx_count)
        for t in range(ta_count)
    ]
    return lax.ppermute(block, ("gx", "ta"), pairs)


def scatter_rows(keep, give, orders):
    held = keep + swap_stage(give, orders, 0).astype(jnp.float32)
    for stage in range(1, len(orders[0])):
        half = held.shape[0] // 2
        give = held[half:].astype(jnp.bfloat16)
        held = held[:half] + swap_stage(give, orders, stage).astype(jnp.float32)
    return held


def gather_rows(held, orders, stages):
    for stage in reversed(range(1, stages)):
        held = jnp.concatenate([held, swap_stage(held, orders, stage)], axis=0)
    return held, swap_stage(held, orders, 0)


def arrange_body(pick_ref, key_ref, value_ref, out_ref):
    chunks, rows, cols = out_ref.shape
    pick = pick_ref[...]
    for side, ref in enumerate((key_ref, value_ref)):
        moved = jnp.dot(pick, ref[...], preferred_element_type=jnp.float32)
        moved = moved.reshape(chunks, rows // 2, cols).astype(jnp.bfloat16)
        out_ref[:, side * (rows // 2) : (side + 1) * (rows // 2), :] = moved


def arrange(pick, keys, values, chunks):
    rows, width = keys.shape
    per_chunk = 2 * rows // chunks
    return pl.pallas_call(
        arrange_body,
        grid=(width // COLS_STEP,),
        in_specs=[
            pl.BlockSpec((rows, rows), lambda j: (0, 0)),
            pl.BlockSpec((rows, COLS_STEP), lambda j: (0, j)),
            pl.BlockSpec((rows, COLS_STEP), lambda j: (0, j)),
        ],
        out_specs=pl.BlockSpec((chunks, per_chunk, COLS_STEP), lambda j: (0, 0, j)),
        out_shape=jax.ShapeDtypeStruct((chunks, per_chunk, width), jnp.bfloat16),
        compiler_params=pltpu.CompilerParams(vmem_limit_bytes=24 << 20),
        name="arrange",
    )(pick, keys, values)


def score_body(own_ref, far_ref, kv_ref, probs_ref, lse_ref):
    step = pl.program_id(0)

    @pl.when(step == 0)
    def _():
        lse_ref[...] = jnp.zeros_like(lse_ref)

    shape = (HALF_VENUES, 2, NODE_STEPS, COLS_STEP)
    own = own_ref[...].astype(jnp.float32).reshape(shape)
    far = far_ref[...].astype(jnp.float32).reshape(shape)
    full = (2 * ROWS_HALF, KEYS_HALF)
    query_step = lax.broadcasted_iota(jnp.int32, full, 0) % NODE_STEPS + (STEPS - NODE_STEPS)
    key_step = lax.broadcasted_iota(jnp.int32, full, 1) % STEPS
    allowed = key_step <= query_step
    lane = lax.broadcasted_iota(jnp.int32, lse_ref.shape, 1)
    lse = lse_ref[...]
    for item in range(2):
        queries = jnp.concatenate(
            [
                own[:, item].reshape(ROWS_HALF, COLS_STEP),
                far[:, 1 - item].reshape(ROWS_HALF, COLS_STEP),
            ],
            axis=0,
        ).astype(jnp.bfloat16)
        keys = kv_ref[:, item].reshape(KEYS_HALF, COLS_STEP)
        for head in range(HEADS_STEP):
            span = slice(head * HEAD_DIM, (head + 1) * HEAD_DIM)
            scores = lax.dot_general(
                queries[:, span],
                keys[:, span],
                (((1,), (1,)), ((), ())),
                preferred_element_type=jnp.float32,
            ) * (1.0 / HEAD_DIM**0.5)
            scores = jnp.where(allowed, scores, -1e30)
            top = jnp.max(scores, axis=1, keepdims=True)
            expd = jnp.exp(scores - top)
            total = jnp.sum(expd, axis=1, keepdims=True)
            probs_ref[head, item] = (expd * (1.0 / total)).astype(jnp.bfloat16)
            column = step * HEADS_STEP + head + item * LSE_ITEM
            lse = jnp.where(lane == column, top + jnp.log(total), lse)
    lse_ref[...] = lse


def half_scores(own, far, kv):
    width = own.shape[1]
    rows = own.shape[0]
    heads = width // HEAD_DIM
    return pl.pallas_call(
        score_body,
        grid=(width // COLS_STEP,),
        in_specs=[
            pl.BlockSpec((rows, COLS_STEP), lambda j: (0, j)),
            pl.BlockSpec((rows, COLS_STEP), lambda j: (0, j)),
            pl.BlockSpec((HALF_VENUES, 2, STEPS, COLS_STEP), lambda j: (0, 0, 0, j)),
        ],
        out_specs=[
            pl.BlockSpec((HEADS_STEP, 2, 2 * ROWS_HALF, KEYS_HALF), lambda j: (j, 0, 0, 0)),
            pl.BlockSpec((2 * ROWS_HALF, 128), lambda j: (0, 0)),
        ],
        out_shape=[
            jax.ShapeDtypeStruct((heads, 2, 2 * ROWS_HALF, KEYS_HALF), jnp.bfloat16),
            jax.ShapeDtypeStruct((2 * ROWS_HALF, 128), jnp.float32),
        ],
        compiler_params=pltpu.CompilerParams(vmem_limit_bytes=24 << 20),
        name="half_scores",
    )(own, far, kv)


def pool_body(probs_ref, lse_ref, far_ref, kv_ref, out_ref):
    step = pl.program_id(0)
    far = jnp.concatenate([far_ref[ROWS_HALF:, :], far_ref[:ROWS_HALF, :]], axis=0)
    far = jnp.concatenate([far[:, LSE_ITEM:], far[:, :LSE_ITEM]], axis=1)
    share = 1.0 / (1.0 + jnp.exp(far - lse_ref[...])) * (1.0 / VENUES)
    lane = lax.broadcasted_iota(jnp.int32, lse_ref.shape, 1)
    for head in range(HEADS_STEP):
        span = slice(head * HEAD_DIM, (head + 1) * HEAD_DIM)
        pooled = []
        for item in range(2):
            column = step * HEADS_STEP + head + item * LSE_ITEM
            factor = jnp.sum(jnp.where(lane == column, share, 0.0), axis=1, keepdims=True)
            weights = probs_ref[head, item].astype(jnp.float32) * factor
            weights = jnp.sum(weights.reshape(VENUES, NODE_STEPS, KEYS_HALF), axis=0)
            values = kv_ref[:, item, :, span].reshape(KEYS_HALF, HEAD_DIM)
            pooled.append(
                jnp.dot(
                    weights.astype(jnp.bfloat16), values, preferred_element_type=jnp.float32
                )
            )
        out_ref[:, span] = jnp.concatenate(pooled, axis=0).astype(jnp.bfloat16)


def half_pool(probs, lse, far_lse, kv):
    width = kv.shape[3]
    return pl.pallas_call(
        pool_body,
        grid=(width // COLS_STEP,),
        in_specs=[
            pl.BlockSpec((HEADS_STEP, 2, 2 * ROWS_HALF, KEYS_HALF), lambda j: (j, 0, 0, 0)),
            pl.BlockSpec((2 * ROWS_HALF, 128), lambda j: (0, 0)),
            pl.BlockSpec((2 * ROWS_HALF, 128), lambda j: (0, 0)),
            pl.BlockSpec((HALF_VENUES, 2, STEPS, COLS_STEP), lambda j: (0, 1, 0, j)),
        ],
        out_specs=pl.BlockSpec((2 * NODE_STEPS, COLS_STEP), lambda j: (0, j)),
        out_shape=jax.ShapeDtypeStruct((2 * NODE_STEPS, width), jnp.bfloat16),
        compiler_params=pltpu.CompilerParams(vmem_limit_bytes=24 << 20),
        name="half_pool",
    )(probs, lse, far_lse, kv)


def pad_lanes(width):
    return -(-width // 128) * 128


def expand_body(near_ref, far_ref, mix_ref, inv_ref, gain_ref, norm_ref, gate_ref, up_ref, out_ref, total_ref, square_ref):
    step = pl.program_id(0)
    steps = pl.num_programs(0)
    width = gate_ref.shape[1]
    padded = pad_lanes(width)

    @pl.when(step == 0)
    def _():
        total_ref[...] = jnp.zeros_like(total_ref)
        square_ref[...] = jnp.zeros_like(square_ref)

    nodes = jnp.concatenate([near_ref[...], far_ref[...]], axis=0)
    message = 0.0
    for kind in range(ETYPES):
        message += gain_ref[kind : kind + 1, :] * jnp.dot(
            mix_ref[kind], nodes, preferred_element_type=jnp.float32
        )
    pre = nodes.astype(jnp.float32) + message * inv_ref[...]
    square_ref[...] += jnp.sum(pre * pre, axis=1, keepdims=True)
    scaled = (pre * norm_ref[...]).astype(jnp.bfloat16)
    total_ref[:, :width] += jnp.dot(scaled, gate_ref[...], preferred_element_type=jnp.float32)
    total_ref[:, padded : padded + width] += jnp.dot(
        scaled, up_ref[...], preferred_element_type=jnp.float32
    )

    @pl.when(step == steps - 1)
    def _():
        out_ref[:, : 2 * padded] = total_ref[...].astype(jnp.bfloat16)
        squares = square_ref[...]
        high = squares.astype(jnp.bfloat16).astype(jnp.float32)
        lane = lax.broadcasted_iota(jnp.int32, (squares.shape[0], 128), 1)
        parts = jnp.where(lane == 0, high, jnp.where(lane == 1, squares - high, 0.0))
        out_ref[:, 2 * padded :] = parts.astype(jnp.bfloat16)

def expand(near, far, mix, inv, gain, norm, gate, up, layer, tile):
    half, feat = near.shape
    rows = 2 * half
    width = gate.shape[2]
    padded = pad_lanes(width)
    return pl.pallas_call(
        expand_body,
        grid=(feat // tile,),
        in_specs=[
            pl.BlockSpec((half, tile), lambda k: (0, k)),
            pl.BlockSpec((half, tile), lambda k: (0, k)),
            pl.BlockSpec((ETYPES, rows, rows), lambda k: (0, 0, 0)),
            pl.BlockSpec((rows, 1), lambda k: (0, 0)),
            pl.BlockSpec((None, ETYPES, tile), lambda k: (layer, 0, k)),
            pl.BlockSpec((None, 1, tile), lambda k: (layer, 0, k)),
            pl.BlockSpec((None, tile, width), lambda k: (layer, k, 0)),
            pl.BlockSpec((None, tile, width), lambda k: (layer, k, 0)),
        ],
        out_specs=pl.BlockSpec((rows, 2 * padded + 128), lambda k: (0, 0)),
        out_shape=jax.ShapeDtypeStruct((rows, 2 * padded + 128), jnp.bfloat16),
        scratch_shapes=[
            pltpu.VMEM((rows, 2 * padded), jnp.float32),
            pltpu.VMEM((rows, 1), jnp.float32),
        ],
        compiler_params=pltpu.CompilerParams(vmem_limit_bytes=24 << 20),
        name="expand",
    )(near, far, mix, inv, gain, norm, gate, up)

def contract_body(near_ref, far_ref, down_ref, keep_ref, give_ref, hidden_ref, total_ref, *, swap):
    step = pl.program_id(0)
    steps = pl.num_programs(0)
    rows, width = hidden_ref.shape
    padded = pad_lanes(width)
    tile = down_ref.shape[0]

    @pl.when(step == 0)
    def _():
        far = far_ref[...].astype(jnp.float32)
        if swap:
            part = rows // 4
            far = jnp.concatenate(
                [far[:part], far[2 * part : 3 * part], far[part : 2 * part], far[3 * part :]], axis=0
            )
        both = near_ref[...].astype(jnp.float32) + far
        squares = jnp.sum(both[:, 2 * padded :], axis=1, keepdims=True)
        scale = lax.rsqrt(squares * (1.0 / D) + 1e-05)
        gate = both[:, :width] * scale
        up = both[:, padded : padded + width] * scale
        hidden_ref[...] = (gate * (1.0 / (1.0 + jnp.exp(-gate))) * up).astype(jnp.bfloat16)
        total_ref[...] = jnp.zeros_like(total_ref)

    if tile == width:
        hidden = hidden_ref[...]
    else:
        hidden = hidden_ref[:, pl.ds(pl.multiple_of(step * tile, 128), tile)]
    total_ref[...] += jnp.dot(hidden, down_ref[...], preferred_element_type=jnp.float32)

    @pl.when(step == steps - 1)
    def _():
        keep_ref[...] = total_ref[: rows // 2, :]
        give_ref[...] = total_ref[rows // 2 :, :].astype(jnp.bfloat16)


def contract(near, far, down, layer, swap, tile):
    rows = near.shape[0]
    width, feat = down.shape[1:]
    half = rows // 2
    return pl.pallas_call(
        functools.partial(contract_body, swap=swap),
        grid=(width // tile,),
        in_specs=[
            pl.BlockSpec(near.shape, lambda k: (0, 0)),
            pl.BlockSpec(far.shape, lambda k: (0, 0)),
            pl.BlockSpec((None, tile, feat), lambda k: (layer, k, 0)),
        ],
        out_specs=[
            pl.BlockSpec((half, feat), lambda k: (0, 0)),
            pl.BlockSpec((half, feat), lambda k: (0, 0)),
        ],
        out_shape=[
            jax.ShapeDtypeStruct((half, feat), jnp.float32),
            jax.ShapeDtypeStruct((half, feat), jnp.bfloat16),
        ],
        scratch_shapes=[
            pltpu.VMEM((rows, width), jnp.bfloat16),
            pltpu.VMEM((rows, feat), jnp.float32),
        ],
        compiler_params=pltpu.CompilerParams(vmem_limit_bytes=24 << 20),
        name="contract",
    )(near, far, down)


def per_device(
    query_vecs,
    key_vecs,
    value_vecs,
    slot_map,
    edge_list,
    edge_types,
    type_gain,
    norm_gain,
    gate_proj,
    up_proj,
    down_proj,
):
    pairs_dev, inst_total, feat_width = query_vecs.shape
    gx_count = lax.axis_size("gx")
    ta_count = lax.axis_size("ta")
    me = lax.axis_index("gx")
    orders = bit_orders(gx_count, ta_count)
    last = len(orders[0]) - 1
    chunks = gx_count // 2
    groups = [list(range(chunks)), list(range(chunks, gx_count))]
    venue_idx = me * pairs_dev // STEPS
    slot_order = lax.dynamic_index_in_dim(slot_map, venue_idx, 0, keepdims=False)

    def picker(pairs):
        rows = pairs * inst_total
        row = lax.broadcasted_iota(jnp.int32, (rows, inst_total), 0)
        inst = (row // pairs % 2 ^ me // chunks) * chunks + row // (2 * pairs)
        hit = inst == lax.broadcasted_iota(jnp.int32, (rows, inst_total), 1)
        slot = jnp.sum(jnp.where(hit, slot_order[None, :], 0), axis=1, keepdims=True)
        line = lax.broadcasted_iota(jnp.int32, (rows, rows), 0)
        source = line % pairs * inst_total + slot
        return (source == lax.broadcasted_iota(jnp.int32, (rows, rows), 1)).astype(jnp.bfloat16)

    whole_venue = pairs_dev == STEPS
    if whole_venue:
        query_vecs = query_vecs[STEPS - NODE_STEPS :]
    query_pairs = query_vecs.shape[0]
    query_rows = query_pairs * inst_total
    queries = jnp.dot(
        picker(query_pairs),
        query_vecs.reshape(query_rows, feat_width),
        preferred_element_type=jnp.float32,
    ).astype(jnp.bfloat16)
    queries = lax.all_to_all(queries, "gx", 0, 0, axis_index_groups=groups, tiled=True)
    kv_rows = pairs_dev * inst_total
    kv = arrange(
        picker(pairs_dev),
        key_vecs.reshape(kv_rows, feat_width),
        value_vecs.reshape(kv_rows, feat_width),
        chunks,
    )
    kv, queries = lax.optimization_barrier((kv, queries))
    if not whole_venue:
        queries = queries.reshape(HALF_VENUES, STEPS // pairs_dev, 2, pairs_dev, feat_width)
        queries = queries[:, (STEPS - NODE_STEPS) // pairs_dev :].transpose(0, 2, 1, 3, 4)
        queries = queries.reshape(2 * ROWS_HALF, feat_width)
    far_queries = swap_stage(queries, orders, last)
    kv = lax.all_to_all(kv, "gx", 0, 0, axis_index_groups=groups, tiled=True)
    kv = kv.reshape(HALF_VENUES, STEPS // pairs_dev, 4, pairs_dev, feat_width)
    kv = kv.transpose(0, 2, 1, 3, 4).reshape(HALF_VENUES, 4, STEPS, feat_width)
    probs, lse = half_scores(queries, far_queries, kv)
    far_lse = swap_stage(lse, orders, last)
    pooled = half_pool(probs, lse, far_lse, kv)
    far_pooled = swap_stage(pooled, orders, last)
    far_pooled = jnp.concatenate([far_pooled[NODE_STEPS:], far_pooled[:NODE_STEPS]], axis=0)
    pooled = (pooled.astype(jnp.float32) + far_pooled.astype(jnp.float32)).astype(jnp.bfloat16)
    own_rows = pooled[:NODE_STEPS]

    row_total = inst_total * NODE_STEPS
    row = jnp.arange(row_total)
    place = row // NODE_STEPS
    inst_at = [
        me ^ sum((place >> (last - stage) & 1) << bit for stage, bit in enumerate(order))
        for order in orders[:2]
    ]
    inst_at = jnp.where(lax.axis_index("ta") % 2 == 0, inst_at[0], inst_at[1])
    at_source = (edge_list[:, 0][:, None] == inst_at[None, :]).astype(jnp.bfloat16)
    at_target = edge_list[:, 1][:, None] == inst_at[None, :]
    same_step = row[:, None] % NODE_STEPS == row[None, :] % NODE_STEPS
    typed = at_target[None] & (edge_types[None, :] == jnp.arange(ETYPES)[:, None])[:, :, None]
    mix = jnp.einsum(
        "ter,ec->trc", typed.astype(jnp.bfloat16), at_source, preferred_element_type=jnp.float32
    )
    mix = jnp.where(same_step[None], mix, 0.0).astype(jnp.bfloat16)
    degree = jnp.maximum(jnp.sum(at_target.astype(jnp.float32), axis=0), 1.0)
    inverse = (1.0 / degree)[:, None]
    norm_rows = norm_gain[:, None, :]
    down_tile = 640 if down_proj.shape[1] % 640 == 0 else down_proj.shape[1]
    expand_tile = 512 if feat_width % 512 == 0 else 128
    for layer_idx in range(ROUNDS):
        if layer_idx == 0:
            near, far = gather_rows(pooled, orders, last)
        else:
            near, far = gather_rows(own_rows, orders, last + 1)
        near_sums = expand(
            near, far, mix, inverse, type_gain, norm_rows, gate_proj, up_proj, layer_idx, expand_tile
        )
        if ta_count == 2:
            far_sums = lax.ppermute(near_sums, "ta", [(0, 1), (1, 0)])
        else:
            far_sums = lax.psum(near_sums.astype(jnp.float32), "ta") - near_sums.astype(jnp.float32)
        keep, give = contract(near_sums, far_sums, down_proj, layer_idx, ta_count == 2, down_tile)
        own_rows = (own_rows.astype(jnp.float32) + scatter_rows(keep, give, orders)).astype(
            jnp.bfloat16
        )
    return own_rows


def solution(mesh):
    placed = (
        P("gx", None, "ta"),
        P("gx", None, "ta"),
        P("gx", None, "ta"),
        P(),
        P(),
        P(),
        P(None, None, "ta"),
        P(None, "ta"),
        P(None, "ta", "gx"),
        P(None, "ta", "gx"),
        P(None, "gx", "ta"),
    )
    return jax.shard_map(
        per_device, mesh=mesh, in_specs=placed, out_specs=P("gx", "ta"), check_vma=False
    )
```

```python
import functools

import jax
import jax.numpy as jnp
from jax import lax
from jax.experimental import pallas as pl
from jax.experimental.pallas import tpu as pltpu
from jax.sharding import PartitionSpec as P

D = 5120
HEAD_DIM = 128
VENUES = 16
STEPS = 16
NODE_STEPS = 8
ROUNDS = 2
ETYPES = 3
HALF_VENUES = VENUES // 2
HEADS_STEP = 5
COLS_STEP = HEADS_STEP * HEAD_DIM
ROWS_HALF = HALF_VENUES * NODE_STEPS
KEYS_HALF = HALF_VENUES * STEPS
LSE_ITEM = 64
VMEM_LIMIT = 56 << 20


def stage_bits(count):
    return list(range(count.bit_length() - 1))


def bit_orders(gx_count, ta_count):
    plain = stage_bits(gx_count)
    if ta_count != 2:
        return [plain] * ta_count
    return [plain, [plain[1], plain[0]] + plain[2:]]


def swap_stage(block, orders, stage):
    gx_count, ta_count = lax.axis_size("gx"), lax.axis_size("ta")
    pairs = [
        (g * ta_count + t, (g ^ (1 << orders[t][stage])) * ta_count + t)
        for g in range(gx_count)
        for t in range(ta_count)
    ]
    return lax.ppermute(block, ("gx", "ta"), pairs)


def scatter_rows(keep, give, orders):
    held = keep + swap_stage(give, orders, 0).astype(jnp.float32)
    for stage in range(1, len(orders[0])):
        half = held.shape[0] // 2
        give = held[half:].astype(jnp.bfloat16)
        held = held[:half] + swap_stage(give, orders, stage).astype(jnp.float32)
    return held


def gather_rows(held, orders, stages):
    for stage in reversed(range(1, stages)):
        held = jnp.concatenate([held, swap_stage(held, orders, stage)], axis=0)
    return held, swap_stage(held, orders, 0)


def arrange_body(pick_ref, *refs):
    sources, out_ref = refs[:-1], refs[-1]
    chunks, rows, cols = out_ref.shape
    part = rows // len(sources)
    pick = pick_ref[...]
    for side, ref in enumerate(sources):
        moved = jnp.dot(pick, ref[...], preferred_element_type=jnp.float32)
        moved = moved.reshape(chunks, part, cols).astype(jnp.bfloat16)
        out_ref[:, side * part : (side + 1) * part, :] = moved


def arrange(pick, sources, chunks):
    rows = pick.shape[0]
    total, width = sources[0].shape
    per_chunk = len(sources) * rows // chunks
    last = total // rows - 1
    return pl.pallas_call(
        arrange_body,
        grid=(width // COLS_STEP,),
        in_specs=[pl.BlockSpec((rows, rows), lambda j: (0, 0))]
        + [pl.BlockSpec((rows, COLS_STEP), lambda j: (last, j)) for _ in sources],
        out_specs=pl.BlockSpec((chunks, per_chunk, COLS_STEP), lambda j: (0, 0, j)),
        out_shape=jax.ShapeDtypeStruct((chunks, per_chunk, width), jnp.bfloat16),
        compiler_params=pltpu.CompilerParams(vmem_limit_bytes=VMEM_LIMIT),
        name="arrange",
    )(pick, *sources)


def score_body(own_ref, far_ref, kv_ref, probs_ref, lse_ref):
    step = pl.program_id(0)

    @pl.when(step == 0)
    def _():
        lse_ref[...] = jnp.zeros_like(lse_ref)

    shape = (HALF_VENUES, 2, NODE_STEPS, COLS_STEP)
    own = own_ref[...].astype(jnp.float32).reshape(shape)
    far = far_ref[...].astype(jnp.float32).reshape(shape)
    full = (2 * ROWS_HALF, KEYS_HALF)
    query_step = lax.broadcasted_iota(jnp.int32, full, 0) % NODE_STEPS + (STEPS - NODE_STEPS)
    key_step = lax.broadcasted_iota(jnp.int32, full, 1) % STEPS
    allowed = key_step <= query_step
    lane = lax.broadcasted_iota(jnp.int32, lse_ref.shape, 1)
    lse = lse_ref[...]
    for item in range(2):
        queries = jnp.concatenate(
            [
                own[:, item].reshape(ROWS_HALF, COLS_STEP),
                far[:, 1 - item].reshape(ROWS_HALF, COLS_STEP),
            ],
            axis=0,
        ).astype(jnp.bfloat16)
        keys = kv_ref[:, item].reshape(KEYS_HALF, COLS_STEP)
        for head in range(HEADS_STEP):
            span = slice(head * HEAD_DIM, (head + 1) * HEAD_DIM)
            scores = lax.dot_general(
                queries[:, span],
                keys[:, span],
                (((1,), (1,)), ((), ())),
                preferred_element_type=jnp.float32,
            ) * (1.0 / HEAD_DIM**0.5)
            scores = jnp.where(allowed, scores, -1e30)
            top = jnp.max(scores, axis=1, keepdims=True)
            expd = jnp.exp(scores - top)
            total = jnp.sum(expd, axis=1, keepdims=True)
            probs_ref[head, item] = (expd * (1.0 / total)).astype(jnp.bfloat16)
            column = step * HEADS_STEP + head + item * LSE_ITEM
            lse = jnp.where(lane == column, top + jnp.log(total), lse)
    lse_ref[...] = lse


def half_scores(own, far, kv):
    width = own.shape[1]
    rows = own.shape[0]
    heads = width // HEAD_DIM
    return pl.pallas_call(
        score_body,
        grid=(width // COLS_STEP,),
        in_specs=[
            pl.BlockSpec((rows, COLS_STEP), lambda j: (0, j)),
            pl.BlockSpec((rows, COLS_STEP), lambda j: (0, j)),
            pl.BlockSpec((HALF_VENUES, 2, STEPS, COLS_STEP), lambda j: (0, 0, 0, j)),
        ],
        out_specs=[
            pl.BlockSpec((HEADS_STEP, 2, 2 * ROWS_HALF, KEYS_HALF), lambda j: (j, 0, 0, 0)),
            pl.BlockSpec((2 * ROWS_HALF, 128), lambda j: (0, 0)),
        ],
        out_shape=[
            jax.ShapeDtypeStruct((heads, 2, 2 * ROWS_HALF, KEYS_HALF), jnp.bfloat16),
            jax.ShapeDtypeStruct((2 * ROWS_HALF, 128), jnp.float32),
        ],
        compiler_params=pltpu.CompilerParams(vmem_limit_bytes=VMEM_LIMIT),
        name="half_scores",
    )(own, far, kv)


def pool_body(probs_ref, lse_ref, far_ref, kv_ref, out_ref):
    step = pl.program_id(0)
    far = jnp.concatenate([far_ref[ROWS_HALF:, :], far_ref[:ROWS_HALF, :]], axis=0)
    far = jnp.concatenate([far[:, LSE_ITEM:], far[:, :LSE_ITEM]], axis=1)
    share = 1.0 / (1.0 + jnp.exp(far - lse_ref[...])) * (1.0 / VENUES)
    lane = lax.broadcasted_iota(jnp.int32, lse_ref.shape, 1)
    for head in range(HEADS_STEP):
        span = slice(head * HEAD_DIM, (head + 1) * HEAD_DIM)
        pooled = []
        for item in range(2):
            column = step * HEADS_STEP + head + item * LSE_ITEM
            factor = jnp.sum(jnp.where(lane == column, share, 0.0), axis=1, keepdims=True)
            weights = probs_ref[head, item].astype(jnp.float32) * factor
            weights = jnp.sum(weights.reshape(VENUES, NODE_STEPS, KEYS_HALF), axis=0)
            values = kv_ref[:, item, :, span].reshape(KEYS_HALF, HEAD_DIM)
            pooled.append(
                jnp.dot(
                    weights.astype(jnp.bfloat16), values, preferred_element_type=jnp.float32
                )
            )
        out_ref[:, span] = jnp.concatenate(pooled, axis=0).astype(jnp.bfloat16)


def half_pool(probs, lse, far_lse, kv):
    width = kv.shape[3]
    return pl.pallas_call(
        pool_body,
        grid=(width // COLS_STEP,),
        in_specs=[
            pl.BlockSpec((HEADS_STEP, 2, 2 * ROWS_HALF, KEYS_HALF), lambda j: (j, 0, 0, 0)),
            pl.BlockSpec((2 * ROWS_HALF, 128), lambda j: (0, 0)),
            pl.BlockSpec((2 * ROWS_HALF, 128), lambda j: (0, 0)),
            pl.BlockSpec((HALF_VENUES, 2, STEPS, COLS_STEP), lambda j: (0, 1, 0, j)),
        ],
        out_specs=pl.BlockSpec((2 * NODE_STEPS, COLS_STEP), lambda j: (0, j)),
        out_shape=jax.ShapeDtypeStruct((2 * NODE_STEPS, width), jnp.bfloat16),
        compiler_params=pltpu.CompilerParams(vmem_limit_bytes=VMEM_LIMIT),
        name="half_pool",
    )(probs, lse, far_lse, kv)


def pad_lanes(width):
    return -(-width // 128) * 128


def expand_body(near_ref, far_ref, mix_ref, inv_ref, gain_ref, norm_ref, gate_ref, up_ref, out_ref, total_ref, square_ref):
    step = pl.program_id(0)
    steps = pl.num_programs(0)
    width = gate_ref.shape[1]
    padded = pad_lanes(width)

    @pl.when(step == 0)
    def _():
        total_ref[...] = jnp.zeros_like(total_ref)
        square_ref[...] = jnp.zeros_like(square_ref)

    nodes = jnp.concatenate([near_ref[...], far_ref[...]], axis=0)
    message = 0.0
    for kind in range(ETYPES):
        message += gain_ref[kind : kind + 1, :] * jnp.dot(
            mix_ref[kind], nodes, preferred_element_type=jnp.float32
        )
    pre = nodes.astype(jnp.float32) + message * inv_ref[...]
    square_ref[...] += jnp.sum(pre * pre, axis=1, keepdims=True)
    scaled = (pre * norm_ref[...]).astype(jnp.bfloat16)
    total_ref[:, :width] += jnp.dot(scaled, gate_ref[...], preferred_element_type=jnp.float32)
    total_ref[:, padded : padded + width] += jnp.dot(
        scaled, up_ref[...], preferred_element_type=jnp.float32
    )

    @pl.when(step == steps - 1)
    def _():
        out_ref[:, : 2 * padded] = total_ref[...].astype(jnp.bfloat16)
        squares = square_ref[...]
        high = squares.astype(jnp.bfloat16).astype(jnp.float32)
        lane = lax.broadcasted_iota(jnp.int32, (squares.shape[0], 128), 1)
        parts = jnp.where(lane == 0, high, jnp.where(lane == 1, squares - high, 0.0))
        out_ref[:, 2 * padded :] = parts.astype(jnp.bfloat16)

def expand(near, far, mix, inv, gain, norm, gate, up, layer, tile):
    half, feat = near.shape
    rows = 2 * half
    width = gate.shape[2]
    padded = pad_lanes(width)
    return pl.pallas_call(
        expand_body,
        grid=(feat // tile,),
        in_specs=[
            pl.BlockSpec((half, tile), lambda k: (0, k)),
            pl.BlockSpec((half, tile), lambda k: (0, k)),
            pl.BlockSpec((ETYPES, rows, rows), lambda k: (0, 0, 0)),
            pl.BlockSpec((rows, 1), lambda k: (0, 0)),
            pl.BlockSpec((None, ETYPES, tile), lambda k: (layer, 0, k)),
            pl.BlockSpec((None, 1, tile), lambda k: (layer, 0, k)),
            pl.BlockSpec((None, tile, width), lambda k: (layer, k, 0)),
            pl.BlockSpec((None, tile, width), lambda k: (layer, k, 0)),
        ],
        out_specs=pl.BlockSpec((rows, 2 * padded + 128), lambda k: (0, 0)),
        out_shape=jax.ShapeDtypeStruct((rows, 2 * padded + 128), jnp.bfloat16),
        scratch_shapes=[
            pltpu.VMEM((rows, 2 * padded), jnp.float32),
            pltpu.VMEM((rows, 1), jnp.float32),
        ],
        compiler_params=pltpu.CompilerParams(vmem_limit_bytes=VMEM_LIMIT),
        name="expand",
    )(near, far, mix, inv, gain, norm, gate, up)

def contract_body(near_ref, far_ref, down_ref, keep_ref, give_ref, hidden_ref, total_ref, *, swap):
    step = pl.program_id(0)
    steps = pl.num_programs(0)
    rows, width = hidden_ref.shape
    padded = pad_lanes(width)
    tile = down_ref.shape[0]

    @pl.when(step == 0)
    def _():
        far = far_ref[...].astype(jnp.float32)
        if swap:
            part = rows // 4
            far = jnp.concatenate(
                [far[:part], far[2 * part : 3 * part], far[part : 2 * part], far[3 * part :]], axis=0
            )
        both = near_ref[...].astype(jnp.float32) + far
        squares = jnp.sum(both[:, 2 * padded :], axis=1, keepdims=True)
        scale = lax.rsqrt(squares * (1.0 / D) + 1e-05)
        gate = both[:, :width] * scale
        up = both[:, padded : padded + width] * scale
        hidden_ref[...] = (gate * (1.0 / (1.0 + jnp.exp(-gate))) * up).astype(jnp.bfloat16)
        total_ref[...] = jnp.zeros_like(total_ref)

    if tile == width:
        hidden = hidden_ref[...]
    else:
        hidden = hidden_ref[:, pl.ds(pl.multiple_of(step * tile, 128), tile)]
    total_ref[...] += jnp.dot(hidden, down_ref[...], preferred_element_type=jnp.float32)

    @pl.when(step == steps - 1)
    def _():
        keep_ref[...] = total_ref[: rows // 2, :]
        give_ref[...] = total_ref[rows // 2 :, :].astype(jnp.bfloat16)


def contract(near, far, down, layer, swap, tile):
    rows = near.shape[0]
    width, feat = down.shape[1:]
    half = rows // 2
    return pl.pallas_call(
        functools.partial(contract_body, swap=swap),
        grid=(width // tile,),
        in_specs=[
            pl.BlockSpec(near.shape, lambda k: (0, 0)),
            pl.BlockSpec(far.shape, lambda k: (0, 0)),
            pl.BlockSpec((None, tile, feat), lambda k: (layer, k, 0)),
        ],
        out_specs=[
            pl.BlockSpec((half, feat), lambda k: (0, 0)),
            pl.BlockSpec((half, feat), lambda k: (0, 0)),
        ],
        out_shape=[
            jax.ShapeDtypeStruct((half, feat), jnp.float32),
            jax.ShapeDtypeStruct((half, feat), jnp.bfloat16),
        ],
        scratch_shapes=[
            pltpu.VMEM((rows, width), jnp.bfloat16),
            pltpu.VMEM((rows, feat), jnp.float32),
        ],
        compiler_params=pltpu.CompilerParams(vmem_limit_bytes=VMEM_LIMIT),
        name="contract",
    )(near, far, down)


def per_device(
    query_vecs,
    key_vecs,
    value_vecs,
    slot_map,
    edge_list,
    edge_types,
    type_gain,
    norm_gain,
    gate_proj,
    up_proj,
    down_proj,
):
    pairs_dev, inst_total, feat_width = query_vecs.shape
    gx_count = lax.axis_size("gx")
    ta_count = lax.axis_size("ta")
    me = lax.axis_index("gx")
    orders = bit_orders(gx_count, ta_count)
    last = len(orders[0]) - 1
    chunks = gx_count // 2
    groups = [list(range(chunks)), list(range(chunks, gx_count))]
    venue_idx = me * pairs_dev // STEPS
    slot_order = lax.dynamic_index_in_dim(slot_map, venue_idx, 0, keepdims=False)

    def picker(pairs):
        rows = pairs * inst_total
        row = lax.broadcasted_iota(jnp.int32, (rows, inst_total), 0)
        inst = (row // pairs % 2 ^ me // chunks) * chunks + row // (2 * pairs)
        hit = inst == lax.broadcasted_iota(jnp.int32, (rows, inst_total), 1)
        slot = jnp.sum(jnp.where(hit, slot_order[None, :], 0), axis=1, keepdims=True)
        line = lax.broadcasted_iota(jnp.int32, (rows, rows), 0)
        source = line % pairs * inst_total + slot
        return (source == lax.broadcasted_iota(jnp.int32, (rows, rows), 1)).astype(jnp.bfloat16)

    whole_venue = pairs_dev == STEPS
    query_pairs = NODE_STEPS if whole_venue else pairs_dev
    rows = pairs_dev * inst_total
    queries = arrange(picker(query_pairs), [query_vecs.reshape(rows, feat_width)], chunks)
    queries = lax.all_to_all(queries, "gx", 0, 0, axis_index_groups=groups, tiled=True)
    queries = queries.reshape(query_pairs * inst_total, feat_width)
    kv = arrange(
        picker(pairs_dev),
        [key_vecs.reshape(rows, feat_width), value_vecs.reshape(rows, feat_width)],
        chunks,
    )
    kv, queries = lax.optimization_barrier((kv, queries))
    if not whole_venue:
        queries = queries.reshape(HALF_VENUES, STEPS // pairs_dev, 2, pairs_dev, feat_width)
        queries = queries[:, (STEPS - NODE_STEPS) // pairs_dev :].transpose(0, 2, 1, 3, 4)
        queries = queries.reshape(2 * ROWS_HALF, feat_width)
    far_queries = swap_stage(queries, orders, last)
    kv = lax.all_to_all(kv, "gx", 0, 0, axis_index_groups=groups, tiled=True)
    kv = kv.reshape(HALF_VENUES, STEPS // pairs_dev, 4, pairs_dev, feat_width)
    kv = kv.transpose(0, 2, 1, 3, 4).reshape(HALF_VENUES, 4, STEPS, feat_width)
    probs, lse = half_scores(queries, far_queries, kv)
    far_lse = swap_stage(lse, orders, last)
    pooled = half_pool(probs, lse, far_lse, kv)
    far_pooled = swap_stage(pooled, orders, last)
    far_pooled = jnp.concatenate([far_pooled[NODE_STEPS:], far_pooled[:NODE_STEPS]], axis=0)
    pooled = (pooled.astype(jnp.float32) + far_pooled.astype(jnp.float32)).astype(jnp.bfloat16)
    own_rows = pooled[:NODE_STEPS]

    row_total = inst_total * NODE_STEPS
    row = jnp.arange(row_total)
    place = row // NODE_STEPS
    inst_at = [
        me ^ sum((place >> (last - stage) & 1) << bit for stage, bit in enumerate(order))
        for order in orders[:2]
    ]
    inst_at = jnp.where(lax.axis_index("ta") % 2 == 0, inst_at[0], inst_at[1])
    at_source = (edge_list[:, 0][:, None] == inst_at[None, :]).astype(jnp.bfloat16)
    at_target = edge_list[:, 1][:, None] == inst_at[None, :]
    same_step = row[:, None] % NODE_STEPS == row[None, :] % NODE_STEPS
    typed = at_target[None] & (edge_types[None, :] == jnp.arange(ETYPES)[:, None])[:, :, None]
    mix = jnp.einsum(
        "ter,ec->trc", typed.astype(jnp.bfloat16), at_source, preferred_element_type=jnp.float32
    )
    mix = jnp.where(same_step[None], mix, 0.0).astype(jnp.bfloat16)
    degree = jnp.maximum(jnp.sum(at_target.astype(jnp.float32), axis=0), 1.0)
    inverse = (1.0 / degree)[:, None]
    norm_rows = norm_gain[:, None, :]
    down_tile = 640 if down_proj.shape[1] % 640 == 0 else down_proj.shape[1]
    expand_tile = 512 if feat_width % 512 == 0 else 128
    for layer_idx in range(ROUNDS):
        if layer_idx == 0:
            near, far = gather_rows(pooled, orders, last)
        else:
            near, far = gather_rows(own_rows, orders, last + 1)
        near_sums = expand(
            near, far, mix, inverse, type_gain, norm_rows, gate_proj, up_proj, layer_idx, expand_tile
        )
        if ta_count == 2:
            far_sums = lax.ppermute(near_sums, "ta", [(0, 1), (1, 0)])
        else:
            far_sums = lax.psum(near_sums.astype(jnp.float32), "ta") - near_sums.astype(jnp.float32)
        keep, give = contract(near_sums, far_sums, down_proj, layer_idx, ta_count == 2, down_tile)
        own_rows = (own_rows.astype(jnp.float32) + scatter_rows(keep, give, orders)).astype(
            jnp.bfloat16
        )
    return own_rows


def solution(mesh):
    placed = (
        P("gx", None, "ta"),
        P("gx", None, "ta"),
        P("gx", None, "ta"),
        P(),
        P(),
        P(),
        P(None, None, "ta"),
        P(None, "ta"),
        P(None, "ta", "gx"),
        P(None, "ta", "gx"),
        P(None, "gx", "ta"),
    )
    return jax.shard_map(
        per_device, mesh=mesh, in_specs=placed, out_specs=P("gx", "ta"), check_vma=False
    )
```

```python
import functools

import jax
import jax.numpy as jnp
from jax import lax
from jax.experimental import pallas as pl
from jax.experimental.pallas import tpu as pltpu
from jax.sharding import PartitionSpec as P

D = 5120
HEAD_DIM = 128
VENUES = 16
STEPS = 16
NODE_STEPS = 8
ROUNDS = 2
ETYPES = 3
HALF_VENUES = VENUES // 2
HEADS_STEP = 5
COLS_STEP = HEADS_STEP * HEAD_DIM
ROWS_HALF = HALF_VENUES * NODE_STEPS
KEYS_HALF = HALF_VENUES * STEPS
LSE_ITEM = 64
VMEM_LIMIT = 8 << 20


def stage_bits(count):
    return list(range(count.bit_length() - 1))


def bit_orders(gx_count, ta_count):
    plain = stage_bits(gx_count)
    if ta_count != 2:
        return [plain] * ta_count
    return [plain, [plain[1], plain[0]] + plain[2:]]


def swap_stage(block, orders, stage):
    gx_count, ta_count = lax.axis_size("gx"), lax.axis_size("ta")
    pairs = [
        (g * ta_count + t, (g ^ (1 << orders[t][stage])) * ta_count + t)
        for g in range(gx_count)
        for t in range(ta_count)
    ]
    return lax.ppermute(block, ("gx", "ta"), pairs)


def gather_rows(held, orders, stages):
    for stage in reversed(range(1, stages)):
        held = jnp.concatenate([held, swap_stage(held, orders, stage)], axis=0)
    return held, swap_stage(held, orders, 0)


def arrange_body(pick_ref, *refs):
    sources, out_ref = refs[:-1], refs[-1]
    chunks, rows, cols = out_ref.shape
    part = rows // len(sources)
    pick = pick_ref[...]
    for side, ref in enumerate(sources):
        moved = jnp.dot(pick, ref[...], preferred_element_type=jnp.float32)
        moved = moved.reshape(chunks, part, cols).astype(jnp.bfloat16)
        out_ref[:, side * part : (side + 1) * part, :] = moved


def arrange(pick, sources, chunks):
    rows = pick.shape[0]
    total, width = sources[0].shape
    per_chunk = len(sources) * rows // chunks
    last = total // rows - 1
    cols = 1280 if width % 1280 == 0 else COLS_STEP
    return pl.pallas_call(
        arrange_body,
        grid=(width // cols,),
        in_specs=[pl.BlockSpec((rows, rows), lambda j: (0, 0))]
        + [pl.BlockSpec((rows, cols), lambda j: (last, j)) for _ in sources],
        out_specs=pl.BlockSpec((chunks, per_chunk, cols), lambda j: (0, 0, j)),
        out_shape=jax.ShapeDtypeStruct((chunks, per_chunk, width), jnp.bfloat16),
        compiler_params=pltpu.CompilerParams(vmem_limit_bytes=VMEM_LIMIT),
        name="arrange",
    )(pick, *sources)


def score_body(own_ref, far_ref, kv_ref, probs_ref, lse_ref):
    step = pl.program_id(0)

    @pl.when(step == 0)
    def _():
        lse_ref[...] = jnp.zeros_like(lse_ref)

    shape = (HALF_VENUES, 2, NODE_STEPS, COLS_STEP)
    own = own_ref[...].astype(jnp.float32).reshape(shape)
    far = far_ref[...].astype(jnp.float32).reshape(shape)
    full = (2 * ROWS_HALF, KEYS_HALF)
    query_step = lax.broadcasted_iota(jnp.int32, full, 0) % NODE_STEPS + (STEPS - NODE_STEPS)
    key_step = lax.broadcasted_iota(jnp.int32, full, 1) % STEPS
    allowed = key_step <= query_step
    lane = lax.broadcasted_iota(jnp.int32, lse_ref.shape, 1)
    lse = lse_ref[...]
    for item in range(2):
        queries = jnp.concatenate(
            [
                own[:, item].reshape(ROWS_HALF, COLS_STEP),
                far[:, 1 - item].reshape(ROWS_HALF, COLS_STEP),
            ],
            axis=0,
        ).astype(jnp.bfloat16)
        keys = kv_ref[:, item].reshape(KEYS_HALF, COLS_STEP)
        for head in range(HEADS_STEP):
            span = slice(head * HEAD_DIM, (head + 1) * HEAD_DIM)
            scores = lax.dot_general(
                queries[:, span],
                keys[:, span],
                (((1,), (1,)), ((), ())),
                preferred_element_type=jnp.float32,
            ) * (1.0 / HEAD_DIM**0.5)
            scores = jnp.where(allowed, scores, -1e30)
            top = jnp.max(scores, axis=1, keepdims=True)
            expd = jnp.exp(scores - top)
            total = jnp.sum(expd, axis=1, keepdims=True)
            probs_ref[head, item] = (expd * (1.0 / total)).astype(jnp.bfloat16)
            column = step * HEADS_STEP + head + item * LSE_ITEM
            lse = jnp.where(lane == column, top + jnp.log(total), lse)
    lse_ref[...] = lse


def half_scores(own, far, kv):
    width = own.shape[1]
    rows = own.shape[0]
    heads = width // HEAD_DIM
    return pl.pallas_call(
        score_body,
        grid=(width // COLS_STEP,),
        in_specs=[
            pl.BlockSpec((rows, COLS_STEP), lambda j: (0, j)),
            pl.BlockSpec((rows, COLS_STEP), lambda j: (0, j)),
            pl.BlockSpec((HALF_VENUES, 2, STEPS, COLS_STEP), lambda j: (0, 0, 0, j)),
        ],
        out_specs=[
            pl.BlockSpec((HEADS_STEP, 2, 2 * ROWS_HALF, KEYS_HALF), lambda j: (j, 0, 0, 0)),
            pl.BlockSpec((2 * ROWS_HALF, 128), lambda j: (0, 0)),
        ],
        out_shape=[
            jax.ShapeDtypeStruct((heads, 2, 2 * ROWS_HALF, KEYS_HALF), jnp.bfloat16),
            jax.ShapeDtypeStruct((2 * ROWS_HALF, 128), jnp.float32),
        ],
        compiler_params=pltpu.CompilerParams(vmem_limit_bytes=VMEM_LIMIT),
        name="half_scores",
    )(own, far, kv)


def pool_body(probs_ref, lse_ref, far_ref, kv_ref, token_ref, out_ref):
    del token_ref
    step = pl.program_id(0)
    far = jnp.concatenate([far_ref[ROWS_HALF:, :], far_ref[:ROWS_HALF, :]], axis=0)
    far = jnp.concatenate([far[:, LSE_ITEM:], far[:, :LSE_ITEM]], axis=1)
    share = 1.0 / (1.0 + jnp.exp(far - lse_ref[...])) * (1.0 / VENUES)
    lane = lax.broadcasted_iota(jnp.int32, lse_ref.shape, 1)
    for head in range(HEADS_STEP):
        span = slice(head * HEAD_DIM, (head + 1) * HEAD_DIM)
        pooled = []
        for item in range(2):
            column = step * HEADS_STEP + head + item * LSE_ITEM
            factor = jnp.sum(jnp.where(lane == column, share, 0.0), axis=1, keepdims=True)
            weights = probs_ref[head, item].astype(jnp.float32) * factor
            weights = jnp.sum(weights.reshape(VENUES, NODE_STEPS, KEYS_HALF), axis=0)
            values = kv_ref[:, item, :, span].reshape(KEYS_HALF, HEAD_DIM)
            pooled.append(
                jnp.dot(
                    weights.astype(jnp.bfloat16), values, preferred_element_type=jnp.float32
                )
            )
        out_ref[:, span] = jnp.concatenate(pooled, axis=0).astype(jnp.bfloat16)


def half_pool(probs, lse, far_lse, kv, token):
    width = kv.shape[3]
    return pl.pallas_call(
        pool_body,
        grid=(width // COLS_STEP,),
        in_specs=[
            pl.BlockSpec((HEADS_STEP, 2, 2 * ROWS_HALF, KEYS_HALF), lambda j: (j, 0, 0, 0)),
            pl.BlockSpec((2 * ROWS_HALF, 128), lambda j: (0, 0)),
            pl.BlockSpec((2 * ROWS_HALF, 128), lambda j: (0, 0)),
            pl.BlockSpec((HALF_VENUES, 2, STEPS, COLS_STEP), lambda j: (0, 1, 0, j)),
            pl.BlockSpec(memory_space=pl.ANY),
        ],
        out_specs=pl.BlockSpec((2 * NODE_STEPS, COLS_STEP), lambda j: (0, j)),
        out_shape=jax.ShapeDtypeStruct((2 * NODE_STEPS, width), jnp.bfloat16),
        compiler_params=pltpu.CompilerParams(vmem_limit_bytes=VMEM_LIMIT),
        name="half_pool",
    )(probs, lse, far_lse, kv, token)


def pad_lanes(width):
    return -(-width // 128) * 128


def stage_body(*refs, layer):
    count = (len(refs) - 3) // 2
    token_ref, sems = refs[-2:]
    copies = []
    for place in range(count):
        copy = pltpu.make_async_copy(refs[place].at[layer], refs[count + 1 + place], sems.at[place])
        copy.start()
        copies.append(copy)
    token_ref[...] = jnp.zeros_like(token_ref)
    for copy in copies:
        copy.wait()


def stage_weights(weights, layer, after):
    held = [pltpu.with_memory_space_constraint(a, pltpu.HBM) for a in weights]
    shapes = [pltpu.VMEM(a.shape[1:], a.dtype) for a in weights]
    size = sum(a.size for a in weights) // ROUNDS
    out = pl.pallas_call(
        functools.partial(stage_body, layer=layer),
        in_specs=[pl.BlockSpec(memory_space=pl.ANY)] * (len(held) + 1),
        out_specs=[pl.BlockSpec(memory_space=pltpu.VMEM)] * (len(shapes) + 1),
        out_shape=shapes + [jax.ShapeDtypeStruct((8, 128), jnp.float32)],
        scratch_shapes=[pltpu.SemaphoreType.DMA((len(held),))],
        compiler_params=pltpu.CompilerParams(vmem_limit_bytes=2 << 20),
        cost_estimate=pl.CostEstimate(flops=0, transcendentals=0, bytes_accessed=4 * size),
        name="stage_weights",
    )(*held, after)
    return out[:-1], out[-1]


def column_tiles(width, tile):
    tile = tile if width % tile == 0 else width
    return [slice(start, start + tile) for start in range(0, width, tile)]


def expand_body(
    near_ref, far_ref, mix_ref, gain_ref, norm_ref, gate_ref, up_ref, token_ref, out_ref,
    scaled_ref, *, layer
):
    del token_ref
    feat, width = gate_ref.shape
    padded = pad_lanes(width)
    edges = sum(mix_ref[kind].astype(jnp.float32) for kind in range(ETYPES))
    inverse = 1.0 / jnp.maximum(jnp.sum(edges, axis=1, keepdims=True), 1.0)
    squares = 0.0
    for span in column_tiles(feat, 512):
        nodes = jnp.concatenate([near_ref[:, span], far_ref[:, span]], axis=0)
        message = 0.0
        for kind in range(ETYPES):
            message += gain_ref[layer, kind : kind + 1, span] * jnp.dot(
                mix_ref[kind], nodes, preferred_element_type=jnp.float32
            )
        pre = nodes.astype(jnp.float32) + message * inverse
        squares += jnp.sum(pre * pre, axis=1, keepdims=True)
        scaled_ref[:, span] = (pre * norm_ref[layer : layer + 1, span]).astype(jnp.bfloat16)
    if padded != width:
        out_ref[...] = jnp.zeros_like(out_ref)
    for place, ref in enumerate((gate_ref, up_ref)):
        for span in column_tiles(width, 256):
            sums = jnp.dot(scaled_ref[...], ref[:, span], preferred_element_type=jnp.float32)
            start = place * padded + span.start
            out_ref[:, start : start + sums.shape[1]] = sums.astype(jnp.bfloat16)
    high = squares.astype(jnp.bfloat16).astype(jnp.float32)
    lane = lax.broadcasted_iota(jnp.int32, (squares.shape[0], 128), 1)
    parts = jnp.where(lane == 0, high, jnp.where(lane == 1, squares - high, 0.0))
    out_ref[:, 2 * padded :] = parts.astype(jnp.bfloat16)


def expand(near, far, mix, gain, norm, gate, up, token, layer):
    half, feat = near.shape
    rows = 2 * half
    columns = 2 * pad_lanes(gate.shape[1]) + 128
    held = [pltpu.with_memory_space_constraint(a, pltpu.VMEM) for a in (gate, up)]
    return pl.pallas_call(
        functools.partial(expand_body, layer=layer),
        in_specs=[pl.BlockSpec(memory_space=pltpu.VMEM)] * 8,
        out_specs=pl.BlockSpec(memory_space=pltpu.VMEM),
        out_shape=jax.ShapeDtypeStruct((rows, columns), jnp.bfloat16),
        scratch_shapes=[pltpu.VMEM((rows, feat), jnp.bfloat16)],
        compiler_params=pltpu.CompilerParams(vmem_limit_bytes=VMEM_LIMIT),
        name="expand",
    )(near, far, mix, gain, norm, *held, token)


def contract_body(near_ref, far_ref, down_ref, keep_ref, give_ref, *, swap):
    rows = near_ref.shape[0]
    width, feat = down_ref.shape
    padded = pad_lanes(width)

    def both(span):
        far = far_ref[:, span].astype(jnp.float32)
        if swap:
            part = rows // 4
            far = jnp.concatenate(
                [far[:part], far[2 * part : 3 * part], far[part : 2 * part], far[3 * part :]], axis=0
            )
        return near_ref[:, span].astype(jnp.float32) + far

    squares = jnp.sum(both(slice(2 * padded, 2 * padded + 128)), axis=1, keepdims=True)
    scale = lax.rsqrt(squares * (1.0 / D) + 1e-05)
    hidden = []
    for span in column_tiles(width, 256):
        gate = both(span) * scale
        up = both(slice(padded + span.start, padded + span.stop)) * scale
        hidden.append((gate * (1.0 / (1.0 + jnp.exp(-gate))) * up).astype(jnp.bfloat16))
    hidden = hidden[0] if len(hidden) == 1 else jnp.concatenate(hidden, axis=1)
    for span in column_tiles(feat, 512):
        total = jnp.dot(hidden, down_ref[:, span], preferred_element_type=jnp.float32)
        keep_ref[:, span] = total[: rows // 2]
        give_ref[:, span] = total[rows // 2 :].astype(jnp.bfloat16)


def contract(near, far, down, swap):
    half, feat = near.shape[0] // 2, down.shape[1]
    held = pltpu.with_memory_space_constraint(down, pltpu.VMEM)
    return pl.pallas_call(
        functools.partial(contract_body, swap=swap),
        in_specs=[pl.BlockSpec(memory_space=pltpu.VMEM)] * 3,
        out_specs=[pl.BlockSpec(memory_space=pltpu.VMEM)] * 2,
        out_shape=[
            jax.ShapeDtypeStruct((half, feat), jnp.float32),
            jax.ShapeDtypeStruct((half, feat), jnp.bfloat16),
        ],
        compiler_params=pltpu.CompilerParams(vmem_limit_bytes=VMEM_LIMIT),
        name="contract",
    )(near, far, held)


def per_device(
    query_vecs,
    key_vecs,
    value_vecs,
    slot_map,
    edge_list,
    edge_types,
    type_gain,
    norm_gain,
    gate_proj,
    up_proj,
    down_proj,
):
    pairs_dev, inst_total, feat_width = query_vecs.shape
    gx_count = lax.axis_size("gx")
    ta_count = lax.axis_size("ta")
    me = lax.axis_index("gx")
    orders = bit_orders(gx_count, ta_count)
    last = len(orders[0]) - 1
    chunks = gx_count // 2
    groups = [list(range(chunks)), list(range(chunks, gx_count))]
    venue_idx = me * pairs_dev // STEPS
    slot_order = lax.dynamic_index_in_dim(slot_map, venue_idx, 0, keepdims=False)

    def picker(pairs):
        rows = pairs * inst_total
        row = lax.broadcasted_iota(jnp.int32, (rows, inst_total), 0)
        inst = (row // pairs % 2 ^ me // chunks) * chunks + row // (2 * pairs)
        hit = inst == lax.broadcasted_iota(jnp.int32, (rows, inst_total), 1)
        slot = jnp.sum(jnp.where(hit, slot_order[None, :], 0), axis=1, keepdims=True)
        line = lax.broadcasted_iota(jnp.int32, (rows, rows), 0)
        source = line % pairs * inst_total + slot
        return (source == lax.broadcasted_iota(jnp.int32, (rows, rows), 1)).astype(jnp.bfloat16)

    whole_venue = pairs_dev == STEPS
    query_pairs = NODE_STEPS if whole_venue else pairs_dev
    rows = pairs_dev * inst_total
    queries = arrange(picker(query_pairs), [query_vecs.reshape(rows, feat_width)], chunks)
    queries = lax.all_to_all(queries, "gx", 0, 0, axis_index_groups=groups, tiled=True)
    queries = queries.reshape(query_pairs * inst_total, feat_width)
    kv = arrange(
        picker(pairs_dev),
        [key_vecs.reshape(rows, feat_width), value_vecs.reshape(rows, feat_width)],
        chunks,
    )
    kv, queries = lax.optimization_barrier((kv, queries))
    if not whole_venue:
        queries = queries.reshape(HALF_VENUES, STEPS // pairs_dev, 2, pairs_dev, feat_width)
        queries = queries[:, (STEPS - NODE_STEPS) // pairs_dev :].transpose(0, 2, 1, 3, 4)
        queries = queries.reshape(2 * ROWS_HALF, feat_width)
    far_queries = swap_stage(queries, orders, last)
    kv = lax.all_to_all(kv, "gx", 0, 0, axis_index_groups=groups, tiled=True)
    kv = kv.reshape(HALF_VENUES, STEPS // pairs_dev, 4, pairs_dev, feat_width)
    kv = kv.transpose(0, 2, 1, 3, 4).reshape(HALF_VENUES, 4, STEPS, feat_width)
    row_total = inst_total * NODE_STEPS
    row = jnp.arange(row_total)
    place = row // NODE_STEPS
    inst_at = [
        me ^ sum((place >> (last - stage) & 1) << bit for stage, bit in enumerate(order))
        for order in orders[:2]
    ]
    inst_at = jnp.where(lax.axis_index("ta") % 2 == 0, inst_at[0], inst_at[1])
    at_source = (edge_list[:, 0][:, None] == inst_at[None, :]).astype(jnp.bfloat16)
    at_target = edge_list[:, 1][:, None] == inst_at[None, :]
    same_step = row[:, None] % NODE_STEPS == row[None, :] % NODE_STEPS
    typed = at_target[None] & (edge_types[None, :] == jnp.arange(ETYPES)[:, None])[:, :, None]
    mix = jnp.einsum(
        "ter,ec->trc", typed.astype(jnp.bfloat16), at_source, preferred_element_type=jnp.float32
    )
    mix = jnp.where(same_step[None], mix, 0.0).astype(jnp.bfloat16)
    kv, mix, type_gain = lax.optimization_barrier((kv, mix, type_gain))
    probs, lse = half_scores(queries, far_queries, kv)
    far_lse = swap_stage(lse, orders, last)
    (gate, up), token = stage_weights([gate_proj, up_proj], 0, lse)
    pooled = half_pool(probs, lse, far_lse, kv, token)
    far_pooled = swap_stage(pooled, orders, last)
    (down,), token = stage_weights([down_proj], 0, pooled)
    far_pooled, token = lax.optimization_barrier((far_pooled, token))
    far_pooled = jnp.concatenate([far_pooled[NODE_STEPS:], far_pooled[:NODE_STEPS]], axis=0)
    pooled = (pooled.astype(jnp.float32) + far_pooled.astype(jnp.float32)).astype(jnp.bfloat16)
    own_rows = pooled[:NODE_STEPS]
    near, far = gather_rows(pooled, orders, last)
    for layer_idx in range(ROUNDS):
        near_sums = expand(near, far, mix, type_gain, norm_gain, gate, up, token, layer_idx)
        if ta_count == 2:
            far_sums = lax.ppermute(near_sums, "ta", [(0, 1), (1, 0)])
        else:
            far_sums = lax.psum(near_sums.astype(jnp.float32), "ta") - near_sums.astype(jnp.float32)
        held, give = contract(near_sums, far_sums, down, ta_count == 2)
        for stage in range(last + 1):
            if stage:
                half = held.shape[0] // 2
                held, give = held[:half], held[half:].astype(jnp.bfloat16)
            taken = swap_stage(give, orders, stage)
            if layer_idx + 1 < ROUNDS and stage < 2:
                if stage == 0:
                    (gate, up), token = stage_weights([gate_proj, up_proj], layer_idx + 1, give)
                else:
                    (down,), token = stage_weights([down_proj], layer_idx + 1, give)
                taken, token = lax.optimization_barrier((taken, token))
            held = held + taken.astype(jnp.float32)
        own_rows = (own_rows.astype(jnp.float32) + held).astype(jnp.bfloat16)
        if layer_idx + 1 < ROUNDS:
            near, far = gather_rows(own_rows, orders, last + 1)
    return own_rows


def solution(mesh):
    placed = (
        P("gx", None, "ta"),
        P("gx", None, "ta"),
        P("gx", None, "ta"),
        P(),
        P(),
        P(),
        P(None, None, "ta"),
        P(None, "ta"),
        P(None, "ta", "gx"),
        P(None, "ta", "gx"),
        P(None, "gx", "ta"),
    )
    return jax.shard_map(
        per_device, mesh=mesh, in_specs=placed, out_specs=P("gx", "ta"), check_vma=False
    )
```

```python
import functools

import jax
import jax.numpy as jnp
from jax import lax
from jax.experimental import pallas as pl
from jax.experimental.pallas import tpu as pltpu
from jax.sharding import PartitionSpec as P

D = 5120
HEAD_DIM = 128
VENUES = 16
STEPS = 16
NODE_STEPS = 8
ROUNDS = 2
ETYPES = 3
HALF_VENUES = VENUES // 2
HEADS_STEP = 5
COLS_STEP = HEADS_STEP * HEAD_DIM
ROWS_HALF = HALF_VENUES * NODE_STEPS
KEYS_HALF = HALF_VENUES * STEPS
LSE_ITEM = 64
VMEM_LIMIT = 8 << 20


def stage_bits(count):
    return list(range(count.bit_length() - 1))


def bit_orders(gx_count, ta_count):
    plain = stage_bits(gx_count)
    if ta_count != 2:
        return [plain] * ta_count
    return [plain, [plain[1], plain[0]] + plain[2:]]


def swap_stage(block, orders, *stages):
    gx_count, ta_count = lax.axis_size("gx"), lax.axis_size("ta")
    flips = [sum(1 << order[stage] for stage in stages) for order in orders]
    pairs = [
        (g * ta_count + t, (g ^ flips[t]) * ta_count + t)
        for g in range(gx_count)
        for t in range(ta_count)
    ]
    return lax.ppermute(block, ("gx", "ta"), pairs)


def gather_rows(held, orders, last):
    for stage in reversed(range(2, last)):
        held = jnp.concatenate([held, swap_stage(held, orders, stage)], axis=0)
    return [
        held,
        swap_stage(held, orders, 1),
        swap_stage(held, orders, 0),
        swap_stage(held, orders, 0, 1),
    ]


def join_pair(mine, orders, last):
    taken = swap_stage(mine, orders, last)
    half = mine.shape[0] // 2
    taken = jnp.concatenate([taken[half:], taken[:half]], axis=0)
    return mine.astype(jnp.float32) + taken.astype(jnp.float32)


def arrange_body(pick_ref, *refs):
    sources, out_ref = refs[:-1], refs[-1]
    chunks, rows, cols = out_ref.shape
    part = rows // len(sources)
    pick = pick_ref[...]
    for side, ref in enumerate(sources):
        moved = jnp.dot(pick, ref[...], preferred_element_type=jnp.float32)
        moved = moved.reshape(chunks, part, cols).astype(jnp.bfloat16)
        out_ref[:, side * part : (side + 1) * part, :] = moved


def arrange(pick, sources, chunks):
    rows = pick.shape[0]
    total, width = sources[0].shape
    per_chunk = len(sources) * rows // chunks
    last = total // rows - 1
    cols = 1280 if width % 1280 == 0 else COLS_STEP
    return pl.pallas_call(
        arrange_body,
        grid=(width // cols,),
        in_specs=[pl.BlockSpec((rows, rows), lambda j: (0, 0))]
        + [pl.BlockSpec((rows, cols), lambda j: (last, j)) for _ in sources],
        out_specs=pl.BlockSpec((chunks, per_chunk, cols), lambda j: (0, 0, j)),
        out_shape=jax.ShapeDtypeStruct((chunks, per_chunk, width), jnp.bfloat16),
        compiler_params=pltpu.CompilerParams(vmem_limit_bytes=VMEM_LIMIT),
        name="arrange",
    )(pick, *sources)


def score_body(own_ref, far_ref, key_ref, probs_ref, lse_ref):
    step = pl.program_id(0)

    @pl.when(step == 0)
    def _():
        lse_ref[...] = jnp.zeros_like(lse_ref)

    shape = (HALF_VENUES, 2, NODE_STEPS, COLS_STEP)
    own = own_ref[...].astype(jnp.float32).reshape(shape)
    far = far_ref[...].astype(jnp.float32).reshape(shape)
    full = (2 * ROWS_HALF, KEYS_HALF)
    query_step = lax.broadcasted_iota(jnp.int32, full, 0) % NODE_STEPS + (STEPS - NODE_STEPS)
    key_step = lax.broadcasted_iota(jnp.int32, full, 1) % STEPS
    allowed = key_step <= query_step
    lane = lax.broadcasted_iota(jnp.int32, lse_ref.shape, 1)
    lse = lse_ref[...]
    for item in range(2):
        queries = jnp.concatenate(
            [
                own[:, item].reshape(ROWS_HALF, COLS_STEP),
                far[:, 1 - item].reshape(ROWS_HALF, COLS_STEP),
            ],
            axis=0,
        ).astype(jnp.bfloat16)
        keys = key_ref[:, item].reshape(KEYS_HALF, COLS_STEP)
        for head in range(HEADS_STEP):
            span = slice(head * HEAD_DIM, (head + 1) * HEAD_DIM)
            scores = lax.dot_general(
                queries[:, span],
                keys[:, span],
                (((1,), (1,)), ((), ())),
                preferred_element_type=jnp.float32,
            ) * (1.0 / HEAD_DIM**0.5)
            scores = jnp.where(allowed, scores, -1e30)
            top = jnp.max(scores, axis=1, keepdims=True)
            expd = jnp.exp(scores - top)
            total = jnp.sum(expd, axis=1, keepdims=True)
            probs_ref[head, item] = (expd * (1.0 / total)).astype(jnp.bfloat16)
            column = step * HEADS_STEP + head + item * LSE_ITEM
            lse = jnp.where(lane == column, top + jnp.log(total), lse)
    lse_ref[...] = lse


def half_scores(own, far, kv):
    width = own.shape[1]
    rows = own.shape[0]
    heads = width // HEAD_DIM
    return pl.pallas_call(
        score_body,
        grid=(width // COLS_STEP,),
        in_specs=[
            pl.BlockSpec((rows, COLS_STEP), lambda j: (0, j)),
            pl.BlockSpec((rows, COLS_STEP), lambda j: (0, j)),
            pl.BlockSpec((HALF_VENUES, 2, STEPS, COLS_STEP), lambda j: (0, 0, 0, j)),
        ],
        out_specs=[
            pl.BlockSpec((HEADS_STEP, 2, 2 * ROWS_HALF, KEYS_HALF), lambda j: (j, 0, 0, 0)),
            pl.BlockSpec((2 * ROWS_HALF, 128), lambda j: (0, 0)),
        ],
        out_shape=[
            jax.ShapeDtypeStruct((heads, 2, 2 * ROWS_HALF, KEYS_HALF), jnp.bfloat16),
            jax.ShapeDtypeStruct((2 * ROWS_HALF, 128), jnp.float32),
        ],
        compiler_params=pltpu.CompilerParams(vmem_limit_bytes=VMEM_LIMIT),
        name="half_scores",
    )(own, far, kv)


def pool_body(probs_ref, lse_ref, far_ref, value_ref, out_ref):
    step = pl.program_id(0)
    far = jnp.concatenate([far_ref[ROWS_HALF:, :], far_ref[:ROWS_HALF, :]], axis=0)
    far = jnp.concatenate([far[:, LSE_ITEM:], far[:, :LSE_ITEM]], axis=1)
    share = 1.0 / (1.0 + jnp.exp(far - lse_ref[...])) * (1.0 / VENUES)
    lane = lax.broadcasted_iota(jnp.int32, lse_ref.shape, 1)
    for head in range(HEADS_STEP):
        span = slice(head * HEAD_DIM, (head + 1) * HEAD_DIM)
        pooled = []
        for item in range(2):
            column = step * HEADS_STEP + head + item * LSE_ITEM
            factor = jnp.sum(jnp.where(lane == column, share, 0.0), axis=1, keepdims=True)
            weights = probs_ref[head, item].astype(jnp.float32) * factor
            weights = jnp.sum(weights.reshape(VENUES, NODE_STEPS, KEYS_HALF), axis=0)
            values = value_ref[:, item, :, span].reshape(KEYS_HALF, HEAD_DIM)
            pooled.append(
                jnp.dot(
                    weights.astype(jnp.bfloat16), values, preferred_element_type=jnp.float32
                )
            )
        out_ref[:, span] = jnp.concatenate(pooled, axis=0).astype(jnp.bfloat16)


def half_pool(probs, lse, far_lse, kv):
    width = kv.shape[3]
    return pl.pallas_call(
        pool_body,
        grid=(width // COLS_STEP,),
        in_specs=[
            pl.BlockSpec((HEADS_STEP, 2, 2 * ROWS_HALF, KEYS_HALF), lambda j: (j, 0, 0, 0)),
            pl.BlockSpec((2 * ROWS_HALF, 128), lambda j: (0, 0)),
            pl.BlockSpec((2 * ROWS_HALF, 128), lambda j: (0, 0)),
            pl.BlockSpec((HALF_VENUES, 2, STEPS, COLS_STEP), lambda j: (0, 1, 0, j)),
        ],
        out_specs=pl.BlockSpec((2 * NODE_STEPS, COLS_STEP), lambda j: (0, j)),
        out_shape=jax.ShapeDtypeStruct((2 * NODE_STEPS, width), jnp.bfloat16),
        compiler_params=pltpu.CompilerParams(vmem_limit_bytes=VMEM_LIMIT),
        name="half_pool",
    )(probs, lse, far_lse, kv)


def pad_lanes(width):
    return -(-width // 128) * 128


def stage_body(*refs, layer, count):
    first = len(refs) - count - 2
    token_ref, sems = refs[-2:]
    copies = []
    for place in range(count):
        copy = pltpu.make_async_copy(refs[place].at[layer], refs[first + place], sems.at[place])
        copy.start()
        copies.append(copy)
    token_ref[...] = jnp.zeros_like(token_ref)
    for copy in copies:
        copy.wait()


def stage_weights(weights, layer, after):
    held = [pltpu.with_memory_space_constraint(a, pltpu.HBM) for a in weights]
    shapes = [pltpu.VMEM(a.shape[1:], a.dtype) for a in weights]
    size = sum(a.size for a in weights) // ROUNDS
    out = pl.pallas_call(
        functools.partial(stage_body, layer=layer, count=len(held)),
        in_specs=[pl.BlockSpec(memory_space=pl.ANY)] * (len(held) + len(after)),
        out_specs=[pl.BlockSpec(memory_space=pltpu.VMEM)] * (len(shapes) + 1),
        out_shape=shapes + [jax.ShapeDtypeStruct((8, 128), jnp.float32)],
        scratch_shapes=[pltpu.SemaphoreType.DMA((len(held),))],
        compiler_params=pltpu.CompilerParams(vmem_limit_bytes=2 << 20),
        cost_estimate=pl.CostEstimate(flops=0, transcendentals=0, bytes_accessed=4 * size),
        name="stage_weights",
    )(*held, *after)
    return out[:-1], out[-1]


def column_tiles(width, tile):
    tile = tile if width % tile == 0 else width
    return [slice(start, start + tile) for start in range(0, width, tile)]


def expand_body(*refs, layer):
    node_refs, refs = refs[:4], refs[4:]
    mix_ref, gain_ref, norm_ref, gate_ref, up_ref, _, out_ref, scaled_ref = refs
    feat, width = gate_ref.shape
    padded = pad_lanes(width)
    edges = sum(mix_ref[kind].astype(jnp.float32) for kind in range(ETYPES))
    inverse = 1.0 / jnp.maximum(jnp.sum(edges, axis=1, keepdims=True), 1.0)
    squares = 0.0
    for span in column_tiles(feat, 512):
        nodes = jnp.concatenate([ref[:, span] for ref in node_refs], axis=0)
        message = 0.0
        for kind in range(ETYPES):
            message += gain_ref[layer, kind : kind + 1, span] * jnp.dot(
                mix_ref[kind], nodes, preferred_element_type=jnp.float32
            )
        pre = nodes.astype(jnp.float32) + message * inverse
        squares += jnp.sum(pre * pre, axis=1, keepdims=True)
        scaled_ref[:, span] = (pre * norm_ref[layer : layer + 1, span]).astype(jnp.bfloat16)
    if padded != width:
        out_ref[...] = jnp.zeros_like(out_ref)
    for place, ref in enumerate((gate_ref, up_ref)):
        for span in column_tiles(width, 256):
            sums = jnp.dot(scaled_ref[...], ref[:, span], preferred_element_type=jnp.float32)
            start = place * padded + span.start
            out_ref[:, start : start + sums.shape[1]] = sums.astype(jnp.bfloat16)
    high = squares.astype(jnp.bfloat16).astype(jnp.float32)
    lane = lax.broadcasted_iota(jnp.int32, (squares.shape[0], 128), 1)
    parts = jnp.where(lane == 0, high, jnp.where(lane == 1, squares - high, 0.0))
    out_ref[:, 2 * padded :] = parts.astype(jnp.bfloat16)


def expand(nodes, mix, gain, norm, gate, up, token, layer):
    part, feat = nodes[0].shape
    rows = len(nodes) * part
    columns = 2 * pad_lanes(gate.shape[1]) + 128
    held = [pltpu.with_memory_space_constraint(a, pltpu.VMEM) for a in (gate, up)]
    operands = [*nodes, mix, gain, norm, *held, token]
    return pl.pallas_call(
        functools.partial(expand_body, layer=layer),
        in_specs=[pl.BlockSpec(memory_space=pltpu.VMEM)] * len(operands),
        out_specs=pl.BlockSpec(memory_space=pltpu.VMEM),
        out_shape=jax.ShapeDtypeStruct((rows, columns), jnp.bfloat16),
        scratch_shapes=[pltpu.VMEM((rows, feat), jnp.bfloat16)],
        compiler_params=pltpu.CompilerParams(vmem_limit_bytes=VMEM_LIMIT),
        name="expand",
    )(*operands)


def contract_body(near_ref, far_ref, down_ref, keep_ref, give_ref, *, swap):
    rows = near_ref.shape[0]
    width, feat = down_ref.shape
    padded = pad_lanes(width)

    def both(span):
        far = far_ref[:, span].astype(jnp.float32)
        if swap:
            part = rows // 4
            far = jnp.concatenate(
                [far[:part], far[2 * part : 3 * part], far[part : 2 * part], far[3 * part :]], axis=0
            )
        return near_ref[:, span].astype(jnp.float32) + far

    squares = jnp.sum(both(slice(2 * padded, 2 * padded + 128)), axis=1, keepdims=True)
    scale = lax.rsqrt(squares * (1.0 / D) + 1e-05)
    hidden = []
    for span in column_tiles(width, 256):
        gate = both(span) * scale
        up = both(slice(padded + span.start, padded + span.stop)) * scale
        hidden.append((gate * (1.0 / (1.0 + jnp.exp(-gate))) * up).astype(jnp.bfloat16))
    hidden = hidden[0] if len(hidden) == 1 else jnp.concatenate(hidden, axis=1)
    for span in column_tiles(feat, 512):
        total = jnp.dot(hidden, down_ref[:, span], preferred_element_type=jnp.float32)
        keep_ref[:, span] = total[: rows // 2]
        give_ref[:, span] = total[rows // 2 :].astype(jnp.bfloat16)


def contract(near, far, down, swap):
    half, feat = near.shape[0] // 2, down.shape[1]
    held = pltpu.with_memory_space_constraint(down, pltpu.VMEM)
    return pl.pallas_call(
        functools.partial(contract_body, swap=swap),
        in_specs=[pl.BlockSpec(memory_space=pltpu.VMEM)] * 3,
        out_specs=[pl.BlockSpec(memory_space=pltpu.VMEM)] * 2,
        out_shape=[
            jax.ShapeDtypeStruct((half, feat), jnp.float32),
            jax.ShapeDtypeStruct((half, feat), jnp.bfloat16),
        ],
        compiler_params=pltpu.CompilerParams(vmem_limit_bytes=VMEM_LIMIT),
        name="contract",
    )(near, far, held)


def per_device(
    query_vecs,
    key_vecs,
    value_vecs,
    slot_map,
    edge_list,
    edge_types,
    type_gain,
    norm_gain,
    gate_proj,
    up_proj,
    down_proj,
):
    pairs_dev, inst_total, feat_width = query_vecs.shape
    gx_count = lax.axis_size("gx")
    ta_count = lax.axis_size("ta")
    me = lax.axis_index("gx")
    orders = bit_orders(gx_count, ta_count)
    last = len(orders[0]) - 1
    chunks = gx_count // 2
    groups = [list(range(chunks)), list(range(chunks, gx_count))]
    venue_idx = me * pairs_dev // STEPS
    slot_order = lax.dynamic_index_in_dim(slot_map, venue_idx, 0, keepdims=False)

    def picker(pairs):
        rows = pairs * inst_total
        row = lax.broadcasted_iota(jnp.int32, (rows, inst_total), 0)
        inst = (row // pairs % 2 ^ me // chunks) * chunks + row // (2 * pairs)
        hit = inst == lax.broadcasted_iota(jnp.int32, (rows, inst_total), 1)
        slot = jnp.sum(jnp.where(hit, slot_order[None, :], 0), axis=1, keepdims=True)
        line = lax.broadcasted_iota(jnp.int32, (rows, rows), 0)
        source = line % pairs * inst_total + slot
        return (source == lax.broadcasted_iota(jnp.int32, (rows, rows), 1)).astype(jnp.bfloat16)

    whole_venue = pairs_dev == STEPS
    query_pairs = NODE_STEPS if whole_venue else pairs_dev
    rows = pairs_dev * inst_total
    queries = arrange(picker(query_pairs), [query_vecs.reshape(rows, feat_width)], chunks)
    queries = lax.all_to_all(queries, "gx", 0, 0, axis_index_groups=groups, tiled=True)
    queries = queries.reshape(query_pairs * inst_total, feat_width)
    kv = arrange(
        picker(pairs_dev),
        [key_vecs.reshape(rows, feat_width), value_vecs.reshape(rows, feat_width)],
        chunks,
    )
    kv, queries = lax.optimization_barrier((kv, queries))
    if not whole_venue:
        queries = queries.reshape(HALF_VENUES, STEPS // pairs_dev, 2, pairs_dev, feat_width)
        queries = queries[:, (STEPS - NODE_STEPS) // pairs_dev :].transpose(0, 2, 1, 3, 4)
        queries = queries.reshape(2 * ROWS_HALF, feat_width)
    far = swap_stage(queries, orders, last)
    kv = lax.all_to_all(kv, "gx", 0, 0, axis_index_groups=groups, tiled=True)
    kv = kv.reshape(HALF_VENUES, STEPS // pairs_dev, 4, pairs_dev, feat_width)
    kv = kv.transpose(0, 2, 1, 3, 4).reshape(HALF_VENUES, 4, STEPS, feat_width)
    row_total = inst_total * NODE_STEPS
    row = jnp.arange(row_total)
    place = row // NODE_STEPS
    inst_at = [
        me ^ sum((place >> (last - stage) & 1) << bit for stage, bit in enumerate(order))
        for order in orders[:2]
    ]
    inst_at = jnp.where(lax.axis_index("ta") % 2 == 0, inst_at[0], inst_at[1])
    at_source = (edge_list[:, 0][:, None] == inst_at[None, :]).astype(jnp.bfloat16)
    at_target = edge_list[:, 1][:, None] == inst_at[None, :]
    same_step = row[:, None] % NODE_STEPS == row[None, :] % NODE_STEPS
    typed = at_target[None] & (edge_types[None, :] == jnp.arange(ETYPES)[:, None])[:, :, None]
    mix = jnp.einsum(
        "ter,ec->trc", typed.astype(jnp.bfloat16), at_source, preferred_element_type=jnp.float32
    )
    mix = jnp.where(same_step[None], mix, 0.0).astype(jnp.bfloat16)
    kv, mix, type_gain = lax.optimization_barrier((kv, mix, type_gain))
    probs, lse = half_scores(queries, far, kv)
    far_lse = swap_stage(lse, orders, last)
    (gate,), token = stage_weights([gate_proj], 0, [lse])
    far_lse, token = lax.optimization_barrier((far_lse, token))
    pooled = half_pool(probs, lse, far_lse, kv)
    (up,), token = stage_weights([up_proj], 0, [pooled, token])
    pooled = join_pair(pooled, orders, last).astype(jnp.bfloat16)
    pooled, token = lax.optimization_barrier((pooled, token))
    (down,), token = stage_weights([down_proj], 0, [token])
    for layer_idx in range(ROUNDS):
        nodes = gather_rows(pooled, orders, last)
        near_sums = expand(nodes, mix, type_gain, norm_gain, gate, up, token, layer_idx)
        if ta_count == 2:
            far_sums = lax.ppermute(near_sums, "ta", [(0, 1), (1, 0)])
        else:
            far_sums = lax.psum(near_sums.astype(jnp.float32), "ta") - near_sums.astype(jnp.float32)
        held, give = contract(near_sums, far_sums, down, ta_count == 2)
        final = layer_idx + 1 == ROUNDS
        for stage in range(last + 1 if final else last):
            if stage:
                half = held.shape[0] // 2
                held, give = held[:half], held[half:].astype(jnp.bfloat16)
            taken = swap_stage(give, orders, stage)
            if not final and stage == 0:
                (gate, up), token = stage_weights([gate_proj, up_proj], layer_idx + 1, [give])
                taken, token = lax.optimization_barrier((taken, token))
            elif not final and stage == 1:
                (down,), token = stage_weights([down_proj], layer_idx + 1, [give])
                taken, token = lax.optimization_barrier((taken, token))
            held = held + taken.astype(jnp.float32)
        if final:
            return (pooled[:NODE_STEPS].astype(jnp.float32) + held).astype(jnp.bfloat16)
        held = join_pair(held.astype(jnp.bfloat16), orders, last)
        pooled = (pooled.astype(jnp.float32) + held).astype(jnp.bfloat16)


def solution(mesh):
    placed = (
        P("gx", None, "ta"),
        P("gx", None, "ta"),
        P("gx", None, "ta"),
        P(),
        P(),
        P(),
        P(None, None, "ta"),
        P(None, "ta"),
        P(None, "ta", "gx"),
        P(None, "ta", "gx"),
        P(None, "gx", "ta"),
    )
    return jax.shard_map(
        per_device, mesh=mesh, in_specs=placed, out_specs=P("gx", "ta"), check_vma=False
    )
```

```python
import functools

import jax
import jax.numpy as jnp
from jax import lax
from jax.experimental import pallas as pl
from jax.experimental.pallas import tpu as pltpu
from jax.sharding import PartitionSpec as P

D = 5120
HEAD_DIM = 128
VENUES = 16
STEPS = 16
NODE_STEPS = 8
ROUNDS = 2
ETYPES = 3
HALF_VENUES = VENUES // 2
HEADS_STEP = 5
COLS_STEP = HEADS_STEP * HEAD_DIM
ROWS_HALF = HALF_VENUES * NODE_STEPS
KEYS_HALF = HALF_VENUES * STEPS
LSE_ITEM = 64
SUM_PARTS = 2
VMEM_LIMIT = 8 << 20


def stage_bits(count):
    return list(range(count.bit_length() - 1))


def bit_orders(gx_count, ta_count):
    plain = stage_bits(gx_count)
    if ta_count != 2:
        return [plain] * ta_count
    return [plain, [plain[1], plain[0]] + plain[2:]]


def swap_stage(block, orders, *stages):
    gx_count, ta_count = lax.axis_size("gx"), lax.axis_size("ta")
    flips = [sum(1 << order[stage] for stage in stages) for order in orders]
    pairs = [
        (g * ta_count + t, (g ^ flips[t]) * ta_count + t)
        for g in range(gx_count)
        for t in range(ta_count)
    ]
    return lax.ppermute(block, ("gx", "ta"), pairs)


def gather_rows(held, orders, last):
    for stage in reversed(range(2, last)):
        held = jnp.concatenate([held, swap_stage(held, orders, stage)], axis=0)
    return [
        held,
        swap_stage(held, orders, 1),
        swap_stage(held, orders, 0),
        swap_stage(held, orders, 0, 1),
    ]


def join_pair(mine, orders, last):
    taken = swap_stage(mine, orders, last)
    half = mine.shape[0] // 2
    taken = jnp.concatenate([taken[half:], taken[:half]], axis=0)
    return mine.astype(jnp.float32) + taken.astype(jnp.float32)


def arrange_body(pick_ref, *refs):
    sources, out_ref = refs[:-1], refs[-1]
    chunks, rows, cols = out_ref.shape
    part = rows // len(sources)
    pick = pick_ref[...]
    for side, ref in enumerate(sources):
        moved = jnp.dot(pick, ref[...], preferred_element_type=jnp.float32)
        moved = moved.reshape(chunks, part, cols).astype(jnp.bfloat16)
        out_ref[:, side * part : (side + 1) * part, :] = moved


def arrange(pick, sources, chunks):
    rows = pick.shape[0]
    total, width = sources[0].shape
    per_chunk = len(sources) * rows // chunks
    last = total // rows - 1
    cols = 1280 if width % 1280 == 0 else COLS_STEP
    return pl.pallas_call(
        arrange_body,
        grid=(width // cols,),
        in_specs=[pl.BlockSpec((rows, rows), lambda j: (0, 0))]
        + [pl.BlockSpec((rows, cols), lambda j: (last, j)) for _ in sources],
        out_specs=pl.BlockSpec((chunks, per_chunk, cols), lambda j: (0, 0, j)),
        out_shape=jax.ShapeDtypeStruct((chunks, per_chunk, width), jnp.bfloat16),
        compiler_params=pltpu.CompilerParams(vmem_limit_bytes=VMEM_LIMIT),
        name="arrange",
    )(pick, *sources)


def score_body(own_ref, far_ref, key_ref, probs_ref, lse_ref):
    step = pl.program_id(0)

    @pl.when(step == 0)
    def _():
        lse_ref[...] = jnp.zeros_like(lse_ref)

    shape = (HALF_VENUES, 2, NODE_STEPS, COLS_STEP)
    own = own_ref[...].astype(jnp.float32).reshape(shape)
    far = far_ref[...].astype(jnp.float32).reshape(shape)
    full = (2 * ROWS_HALF, KEYS_HALF)
    query_step = lax.broadcasted_iota(jnp.int32, full, 0) % NODE_STEPS + (STEPS - NODE_STEPS)
    key_step = lax.broadcasted_iota(jnp.int32, full, 1) % STEPS
    allowed = key_step <= query_step
    lane = lax.broadcasted_iota(jnp.int32, lse_ref.shape, 1)
    lse = lse_ref[...]
    for item in range(2):
        queries = jnp.concatenate(
            [
                own[:, item].reshape(ROWS_HALF, COLS_STEP),
                far[:, 1 - item].reshape(ROWS_HALF, COLS_STEP),
            ],
            axis=0,
        ).astype(jnp.bfloat16)
        keys = key_ref[:, item].reshape(KEYS_HALF, COLS_STEP)
        for head in range(HEADS_STEP):
            span = slice(head * HEAD_DIM, (head + 1) * HEAD_DIM)
            scores = lax.dot_general(
                queries[:, span],
                keys[:, span],
                (((1,), (1,)), ((), ())),
                preferred_element_type=jnp.float32,
            ) * (1.0 / HEAD_DIM**0.5)
            scores = jnp.where(allowed, scores, -1e30)
            top = jnp.max(scores, axis=1, keepdims=True)
            expd = jnp.exp(scores - top)
            total = jnp.sum(expd, axis=1, keepdims=True)
            probs_ref[head, item] = (expd * (1.0 / total)).astype(jnp.bfloat16)
            column = step * HEADS_STEP + head + item * LSE_ITEM
            lse = jnp.where(lane == column, top + jnp.log(total), lse)
    lse_ref[...] = lse


def half_scores(own, far, keys):
    width = own.shape[1]
    rows = own.shape[0]
    heads = width // HEAD_DIM
    return pl.pallas_call(
        score_body,
        grid=(width // COLS_STEP,),
        in_specs=[
            pl.BlockSpec((rows, COLS_STEP), lambda j: (0, j)),
            pl.BlockSpec((rows, COLS_STEP), lambda j: (0, j)),
            pl.BlockSpec((HALF_VENUES, 2, STEPS, COLS_STEP), lambda j: (0, 0, 0, j)),
        ],
        out_specs=[
            pl.BlockSpec((HEADS_STEP, 2, 2 * ROWS_HALF, KEYS_HALF), lambda j: (j, 0, 0, 0)),
            pl.BlockSpec((2 * ROWS_HALF, 128), lambda j: (0, 0)),
        ],
        out_shape=[
            jax.ShapeDtypeStruct((heads, 2, 2 * ROWS_HALF, KEYS_HALF), jnp.bfloat16),
            jax.ShapeDtypeStruct((2 * ROWS_HALF, 128), jnp.float32),
        ],
        compiler_params=pltpu.CompilerParams(vmem_limit_bytes=VMEM_LIMIT),
        name="half_scores",
    )(*[pltpu.with_memory_space_constraint(a, pltpu.HBM) for a in (own, far)], keys)


def weigh_body(probs_ref, lse_ref, far_ref, weights_ref):
    step = pl.program_id(0)
    far = jnp.concatenate([far_ref[ROWS_HALF:, :], far_ref[:ROWS_HALF, :]], axis=0)
    far = jnp.concatenate([far[:, LSE_ITEM:], far[:, :LSE_ITEM]], axis=1)
    share = 1.0 / (1.0 + jnp.exp(far - lse_ref[...])) * (1.0 / VENUES)
    lane = lax.broadcasted_iota(jnp.int32, lse_ref.shape, 1)
    for head in range(HEADS_STEP):
        means = []
        for item in range(2):
            column = step * HEADS_STEP + head + item * LSE_ITEM
            factor = jnp.sum(jnp.where(lane == column, share, 0.0), axis=1, keepdims=True)
            weights = probs_ref[head, item].astype(jnp.float32) * factor
            means.append(jnp.sum(weights.reshape(VENUES, NODE_STEPS, KEYS_HALF), axis=0))
        weights_ref[head] = jnp.concatenate(means, axis=0).astype(jnp.bfloat16)


def mean_weights(probs, lse, far_lse):
    heads = probs.shape[0]
    return pl.pallas_call(
        weigh_body,
        grid=(heads // HEADS_STEP,),
        in_specs=[
            pl.BlockSpec((HEADS_STEP, 2, 2 * ROWS_HALF, KEYS_HALF), lambda j: (j, 0, 0, 0)),
            pl.BlockSpec((2 * ROWS_HALF, 128), lambda j: (0, 0)),
            pl.BlockSpec((2 * ROWS_HALF, 128), lambda j: (0, 0)),
        ],
        out_specs=pl.BlockSpec((HEADS_STEP, 2 * NODE_STEPS, KEYS_HALF), lambda j: (j, 0, 0)),
        out_shape=jax.ShapeDtypeStruct((heads, 2 * NODE_STEPS, KEYS_HALF), jnp.bfloat16),
        compiler_params=pltpu.CompilerParams(vmem_limit_bytes=VMEM_LIMIT),
        name="mean_weights",
    )(probs, lse, far_lse)


def pool_body(weights_ref, value_ref, out_ref):
    row = lax.broadcasted_iota(jnp.int32, (2 * NODE_STEPS, HEAD_DIM), 0)
    for head in range(HEADS_STEP):
        span = slice(head * HEAD_DIM, (head + 1) * HEAD_DIM)
        pooled = [
            jnp.dot(
                weights_ref[head],
                value_ref[:, item, :, span].reshape(KEYS_HALF, HEAD_DIM),
                preferred_element_type=jnp.float32,
            )
            for item in range(2)
        ]
        out_ref[:, span] = jnp.where(row < NODE_STEPS, *pooled).astype(jnp.bfloat16)


def half_pool(weights, values):
    width = values.shape[3]
    return pl.pallas_call(
        pool_body,
        grid=(width // COLS_STEP,),
        in_specs=[
            pl.BlockSpec((HEADS_STEP, 2 * NODE_STEPS, KEYS_HALF), lambda j: (j, 0, 0)),
            pl.BlockSpec((HALF_VENUES, 2, STEPS, COLS_STEP), lambda j: (0, 0, 0, j)),
        ],
        out_specs=pl.BlockSpec((2 * NODE_STEPS, COLS_STEP), lambda j: (0, j)),
        out_shape=jax.ShapeDtypeStruct((2 * NODE_STEPS, width), jnp.bfloat16),
        compiler_params=pltpu.CompilerParams(vmem_limit_bytes=VMEM_LIMIT),
        name="half_pool",
    )(weights, values)


def pad_lanes(width):
    return -(-width // 128) * 128


def stage_body(*refs, layer, count):
    first = len(refs) - count - 2
    token_ref, sems = refs[-2:]
    copies = []
    for place in range(count):
        copy = pltpu.make_async_copy(refs[place].at[layer], refs[first + place], sems.at[place])
        copy.start()
        copies.append(copy)
    token_ref[...] = jnp.zeros_like(token_ref)
    for copy in copies:
        copy.wait()


def stage_weights(weights, layer, after):
    held = [pltpu.with_memory_space_constraint(a, pltpu.HBM) for a in weights]
    shapes = [pltpu.VMEM(a.shape[1:], a.dtype) for a in weights]
    size = sum(a.size for a in weights) // ROUNDS
    out = pl.pallas_call(
        functools.partial(stage_body, layer=layer, count=len(held)),
        in_specs=[pl.BlockSpec(memory_space=pl.ANY)] * (len(held) + len(after)),
        out_specs=[pl.BlockSpec(memory_space=pltpu.VMEM)] * (len(shapes) + 1),
        out_shape=shapes + [jax.ShapeDtypeStruct((8, 128), jnp.float32)],
        scratch_shapes=[pltpu.SemaphoreType.DMA((len(held),))],
        compiler_params=pltpu.CompilerParams(vmem_limit_bytes=2 << 20),
        cost_estimate=pl.CostEstimate(flops=0, transcendentals=0, bytes_accessed=4 * size),
        name="stage_weights",
    )(*held, *after)
    return out[:-1], out[-1]


def column_tiles(width, tile):
    tile = tile if width % tile == 0 else width
    return [slice(start, start + tile) for start in range(0, width, tile)]


def expand_body(*refs, layer):
    node_refs, refs = refs[:4], refs[4:]
    mix_ref, gain_ref, norm_ref, gate_ref, up_ref, _, out_ref, scaled_ref = refs
    feat, width = gate_ref.shape
    padded = pad_lanes(width)
    edges = sum(mix_ref[kind].astype(jnp.float32) for kind in range(ETYPES))
    inverse = 1.0 / jnp.maximum(jnp.sum(edges, axis=1, keepdims=True), 1.0)
    squares = 0.0
    for span in column_tiles(feat, 512):
        nodes = jnp.concatenate([ref[:, span] for ref in node_refs], axis=0)
        message = 0.0
        for kind in range(ETYPES):
            message += gain_ref[layer, kind : kind + 1, span] * jnp.dot(
                mix_ref[kind], nodes, preferred_element_type=jnp.float32
            )
        pre = nodes.astype(jnp.float32) + message * inverse
        squares += jnp.sum(pre * pre, axis=1, keepdims=True)
        scaled_ref[:, span] = (pre * norm_ref[layer : layer + 1, span]).astype(jnp.bfloat16)
    if padded != width:
        out_ref[...] = jnp.zeros_like(out_ref)
    for place, ref in enumerate((gate_ref, up_ref)):
        for span in column_tiles(width, 256):
            sums = jnp.dot(scaled_ref[...], ref[:, span], preferred_element_type=jnp.float32)
            start = place * padded + span.start
            out_ref[:, start : start + sums.shape[1]] = sums.astype(jnp.bfloat16)
    high = squares.astype(jnp.bfloat16).astype(jnp.float32)
    lane = lax.broadcasted_iota(jnp.int32, (squares.shape[0], 128), 1)
    parts = jnp.where(lane == 0, high, jnp.where(lane == 1, squares - high, 0.0))
    out_ref[:, 2 * padded :] = parts.astype(jnp.bfloat16)


def expand(nodes, mix, gain, norm, gate, up, token, layer):
    part, feat = nodes[0].shape
    rows = len(nodes) * part
    columns = 2 * pad_lanes(gate.shape[1]) + 128
    held = [pltpu.with_memory_space_constraint(a, pltpu.VMEM) for a in (gate, up)]
    operands = [*nodes, mix, gain, norm, *held, token]
    return pl.pallas_call(
        functools.partial(expand_body, layer=layer),
        in_specs=[pl.BlockSpec(memory_space=pltpu.VMEM)] * len(operands),
        out_specs=pl.BlockSpec(memory_space=pltpu.VMEM),
        out_shape=jax.ShapeDtypeStruct((rows, columns), jnp.bfloat16),
        scratch_shapes=[pltpu.VMEM((rows, feat), jnp.bfloat16)],
        compiler_params=pltpu.CompilerParams(vmem_limit_bytes=VMEM_LIMIT),
        name="expand",
    )(*operands)


def contract_body(near_ref, far_ref, down_ref, *out_refs, swap):
    rows = near_ref.shape[0]
    width, feat = down_ref.shape
    padded = pad_lanes(width)

    def both(span):
        far = far_ref[:, span].astype(jnp.float32)
        if swap:
            part = rows // 4
            far = jnp.concatenate(
                [far[:part], far[2 * part : 3 * part], far[part : 2 * part], far[3 * part :]], axis=0
            )
        return near_ref[:, span].astype(jnp.float32) + far

    squares = jnp.sum(both(slice(2 * padded, 2 * padded + 128)), axis=1, keepdims=True)
    scale = lax.rsqrt(squares * (1.0 / D) + 1e-05)
    hidden = []
    for span in column_tiles(width, 256):
        gate = both(span) * scale
        up = both(slice(padded + span.start, padded + span.stop)) * scale
        hidden.append((gate * (1.0 / (1.0 + jnp.exp(-gate))) * up).astype(jnp.bfloat16))
    hidden = hidden[0] if len(hidden) == 1 else jnp.concatenate(hidden, axis=1)
    held = feat // (len(out_refs) // 2)
    for span in column_tiles(feat, 640):
        total = jnp.dot(hidden, down_ref[:, span], preferred_element_type=jnp.float32)
        part = span.start // held
        local = slice(span.start % held, span.start % held + span.stop - span.start)
        out_refs[2 * part][:, local] = total[: rows // 2]
        out_refs[2 * part + 1][:, local] = total[rows // 2 :].astype(jnp.bfloat16)


def contract(near, far, down, parts, swap):
    half, feat = near.shape[0] // 2, down.shape[1]
    held = pltpu.with_memory_space_constraint(down, pltpu.VMEM)
    shape = (half, feat // parts)
    out = pl.pallas_call(
        functools.partial(contract_body, swap=swap),
        in_specs=[pl.BlockSpec(memory_space=pltpu.VMEM)] * 3,
        out_specs=[pl.BlockSpec(memory_space=pltpu.VMEM)] * (2 * parts),
        out_shape=[
            jax.ShapeDtypeStruct(shape, jnp.float32),
            jax.ShapeDtypeStruct(shape, jnp.bfloat16),
        ]
        * parts,
        compiler_params=pltpu.CompilerParams(vmem_limit_bytes=VMEM_LIMIT),
        name="contract",
    )(near, far, held)
    return [out[2 * part : 2 * part + 2] for part in range(parts)]


def per_device(
    query_vecs,
    key_vecs,
    value_vecs,
    slot_map,
    edge_list,
    edge_types,
    type_gain,
    norm_gain,
    gate_proj,
    up_proj,
    down_proj,
):
    pairs_dev, inst_total, feat_width = query_vecs.shape
    gx_count = lax.axis_size("gx")
    ta_count = lax.axis_size("ta")
    me = lax.axis_index("gx")
    orders = bit_orders(gx_count, ta_count)
    last = len(orders[0]) - 1
    chunks = gx_count // 2
    groups = [list(range(chunks)), list(range(chunks, gx_count))]
    venue_idx = me * pairs_dev // STEPS
    slot_order = lax.dynamic_index_in_dim(slot_map, venue_idx, 0, keepdims=False)

    def picker(pairs):
        rows = pairs * inst_total
        row = lax.broadcasted_iota(jnp.int32, (rows, inst_total), 0)
        inst = (row // pairs % 2 ^ me // chunks) * chunks + row // (2 * pairs)
        hit = inst == lax.broadcasted_iota(jnp.int32, (rows, inst_total), 1)
        slot = jnp.sum(jnp.where(hit, slot_order[None, :], 0), axis=1, keepdims=True)
        line = lax.broadcasted_iota(jnp.int32, (rows, rows), 0)
        source = line % pairs * inst_total + slot
        return (source == lax.broadcasted_iota(jnp.int32, (rows, rows), 1)).astype(jnp.bfloat16)

    whole_venue = pairs_dev == STEPS
    query_pairs = NODE_STEPS if whole_venue else pairs_dev
    rows = pairs_dev * inst_total
    queries = arrange(picker(query_pairs), [query_vecs.reshape(rows, feat_width)], chunks)
    queries = lax.all_to_all(queries, "gx", 0, 0, axis_index_groups=groups, tiled=True)
    queries = queries.reshape(query_pairs * inst_total, feat_width)
    pick = picker(pairs_dev)
    keys, values = (a.reshape(rows, feat_width) for a in (key_vecs, value_vecs))
    values = arrange(pick, [values], chunks)
    keys = arrange(pick, [keys], chunks)
    keys, queries = lax.optimization_barrier((keys, queries))

    def exchange(block):
        block = lax.all_to_all(block, "gx", 0, 0, axis_index_groups=groups, tiled=True)
        block = block.reshape(HALF_VENUES, STEPS // pairs_dev, 2, pairs_dev, feat_width)
        return block.transpose(0, 2, 1, 3, 4).reshape(HALF_VENUES, 2, STEPS, feat_width)

    if not whole_venue:
        queries = queries.reshape(HALF_VENUES, STEPS // pairs_dev, 2, pairs_dev, feat_width)
        queries = queries[:, (STEPS - NODE_STEPS) // pairs_dev :].transpose(0, 2, 1, 3, 4)
        queries = queries.reshape(2 * ROWS_HALF, feat_width)
    far = swap_stage(queries, orders, last)
    keys = exchange(keys)
    values, keys, far = lax.optimization_barrier((values, keys, far))
    values = exchange(values)
    row_total = inst_total * NODE_STEPS
    row = jnp.arange(row_total)
    place = row // NODE_STEPS
    inst_at = [
        me ^ sum((place >> (last - stage) & 1) << bit for stage, bit in enumerate(order))
        for order in orders[:2]
    ]
    inst_at = jnp.where(lax.axis_index("ta") % 2 == 0, inst_at[0], inst_at[1])
    at_source = (edge_list[:, 0][:, None] == inst_at[None, :]).astype(jnp.bfloat16)
    at_target = edge_list[:, 1][:, None] == inst_at[None, :]
    same_step = row[:, None] % NODE_STEPS == row[None, :] % NODE_STEPS
    typed = at_target[None] & (edge_types[None, :] == jnp.arange(ETYPES)[:, None])[:, :, None]
    mix = jnp.einsum(
        "ter,ec->trc", typed.astype(jnp.bfloat16), at_source, preferred_element_type=jnp.float32
    )
    mix = jnp.where(same_step[None], mix, 0.0).astype(jnp.bfloat16)
    keys, mix, type_gain = lax.optimization_barrier((keys, mix, type_gain))
    probs, lse = half_scores(queries, far, keys)
    far_lse = swap_stage(lse, orders, last)
    pooled = half_pool(mean_weights(probs, lse, far_lse), values)
    (gate,), token = stage_weights([gate_proj], 0, [pooled])
    pooled = join_pair(pooled, orders, last).astype(jnp.bfloat16)
    pooled, token = lax.optimization_barrier((pooled, token))
    (up, down), token = stage_weights([up_proj, down_proj], 0, [token])
    parts = SUM_PARTS if feat_width % (SUM_PARTS * 128) == 0 else 1
    part_width = feat_width // parts
    for layer_idx in range(ROUNDS):
        nodes = gather_rows(pooled, orders, last)
        near_sums = expand(nodes, mix, type_gain, norm_gain, gate, up, token, layer_idx)
        if ta_count == 2:
            far_sums = lax.ppermute(near_sums, "ta", [(0, 1), (1, 0)])
        else:
            far_sums = lax.psum(near_sums.astype(jnp.float32), "ta") - near_sums.astype(jnp.float32)
        sums = contract(near_sums, far_sums, down, parts, ta_count == 2)
        final = layer_idx + 1 == ROUNDS
        settled = []
        for part, (held, give) in enumerate(sums):
            for stage in range(last + 1 if final else last):
                if stage:
                    half = held.shape[0] // 2
                    held, give = held[:half], held[half:].astype(jnp.bfloat16)
                taken = swap_stage(give, orders, stage)
                if not final and part == 0 and stage == 0:
                    (down,), token = stage_weights([down_proj], layer_idx + 1, [give])
                    taken, token = lax.optimization_barrier((taken, token))
                held = held + taken.astype(jnp.float32)
            if not final:
                held = join_pair(held.astype(jnp.bfloat16), orders, last)
            rows_kept = pooled[: held.shape[0], part * part_width : (part + 1) * part_width]
            settled.append((rows_kept.astype(jnp.float32) + held).astype(jnp.bfloat16))
        pooled = jnp.concatenate(settled, axis=1)
        if not final:
            (gate, up), token = stage_weights([gate_proj, up_proj], layer_idx + 1, [pooled, token])
    return pooled


def solution(mesh):
    placed = (
        P("gx", None, "ta"),
        P("gx", None, "ta"),
        P("gx", None, "ta"),
        P(),
        P(),
        P(),
        P(None, None, "ta"),
        P(None, "ta"),
        P(None, "ta", "gx"),
        P(None, "ta", "gx"),
        P(None, "gx", "ta"),
    )
    return jax.shard_map(
        per_device, mesh=mesh, in_specs=placed, out_specs=P("gx", "ta"), check_vma=False
    )
```

```python
import functools

import jax
import jax.numpy as jnp
from jax import lax
from jax.experimental import pallas as pl
from jax.experimental.pallas import tpu as pltpu
from jax.sharding import PartitionSpec as P

D = 5120
HEAD_DIM = 128
VENUES = 16
STEPS = 16
NODE_STEPS = 8
ROUNDS = 2
ETYPES = 3
HALF_VENUES = VENUES // 2
HEADS_STEP = 5
COLS_STEP = HEADS_STEP * HEAD_DIM
ROWS_HALF = HALF_VENUES * NODE_STEPS
KEYS_HALF = HALF_VENUES * STEPS
LSE_ITEM = 64
SUM_PARTS = 2
VMEM_LIMIT = 8 << 20


def stage_bits(count):
    return list(range(count.bit_length() - 1))


def bit_orders(gx_count, ta_count):
    plain = stage_bits(gx_count)
    if ta_count != 2:
        return [plain] * ta_count
    return [plain, [plain[1], plain[0]] + plain[2:]]


def swap_stage(block, orders, *stages):
    gx_count, ta_count = lax.axis_size("gx"), lax.axis_size("ta")
    flips = [sum(1 << order[stage] for stage in stages) for order in orders]
    pairs = [
        (g * ta_count + t, (g ^ flips[t]) * ta_count + t)
        for g in range(gx_count)
        for t in range(ta_count)
    ]
    return lax.ppermute(block, ("gx", "ta"), pairs)


def gather_rows(held, orders, last):
    for stage in reversed(range(2, last)):
        held = jnp.concatenate([held, swap_stage(held, orders, stage)], axis=0)
    return [
        held,
        swap_stage(held, orders, 1),
        swap_stage(held, orders, 0),
        swap_stage(held, orders, 0, 1),
    ]


def join_pair(mine, orders, last):
    taken = swap_stage(mine, orders, last)
    half = mine.shape[0] // 2
    taken = jnp.concatenate([taken[half:], taken[:half]], axis=0)
    return mine.astype(jnp.float32) + taken.astype(jnp.float32)


def arrange_body(pick_ref, source_ref, *out_refs):
    moved = jnp.dot(pick_ref[...], source_ref[...], preferred_element_type=jnp.float32)
    moved = moved.astype(jnp.bfloat16)
    rows = moved.shape[0] // len(out_refs)
    for place, ref in enumerate(out_refs):
        ref[...] = moved[place * rows : (place + 1) * rows]


def arrange(pick, source, pieces=1):
    rows, taken = pick.shape
    total, width = source.shape
    last = total // taken - 1
    cols = 1280 if width % 1280 == 0 else COLS_STEP
    return pl.pallas_call(
        arrange_body,
        grid=(width // cols,),
        in_specs=[
            pl.BlockSpec((rows, taken), lambda j: (0, 0)),
            pl.BlockSpec((taken, cols), lambda j: (last, j)),
        ],
        out_specs=[pl.BlockSpec((rows // pieces, cols), lambda j: (0, j))] * pieces,
        out_shape=[jax.ShapeDtypeStruct((rows // pieces, width), jnp.bfloat16)] * pieces,
        compiler_params=pltpu.CompilerParams(vmem_limit_bytes=VMEM_LIMIT),
        name="arrange",
    )(pick, source)


def score_body(query_ref, *refs):
    key_refs, probs_ref, lse_ref = refs[:HALF_VENUES], refs[-2], refs[-1]
    step = pl.program_id(0)

    @pl.when(step == 0)
    def _():
        lse_ref[...] = jnp.zeros_like(lse_ref)

    shape = (VENUES, 2, NODE_STEPS, COLS_STEP)
    both = query_ref[...].astype(jnp.float32).reshape(shape)
    full = (2 * ROWS_HALF, KEYS_HALF)
    query_step = lax.broadcasted_iota(jnp.int32, full, 0) % NODE_STEPS + (STEPS - NODE_STEPS)
    key_step = lax.broadcasted_iota(jnp.int32, full, 1) % STEPS
    allowed = key_step <= query_step
    lane = lax.broadcasted_iota(jnp.int32, lse_ref.shape, 1)
    lse = lse_ref[...]
    for item in range(2):
        queries = both[:, item].reshape(2 * ROWS_HALF, COLS_STEP).astype(jnp.bfloat16)
        keys = jnp.concatenate(
            [ref[item * STEPS : (item + 1) * STEPS, :] for ref in key_refs], axis=0
        )
        for head in range(HEADS_STEP):
            span = slice(head * HEAD_DIM, (head + 1) * HEAD_DIM)
            scores = lax.dot_general(
                queries[:, span],
                keys[:, span],
                (((1,), (1,)), ((), ())),
                preferred_element_type=jnp.float32,
            ) * (1.0 / HEAD_DIM**0.5)
            scores = jnp.where(allowed, scores, -1e30)
            top = jnp.max(scores, axis=1, keepdims=True)
            expd = jnp.exp(scores - top)
            total = jnp.sum(expd, axis=1, keepdims=True)
            probs_ref[head, item] = (expd * (1.0 / total)).astype(jnp.bfloat16)
            column = step * HEADS_STEP + head + item * LSE_ITEM
            lse = jnp.where(lane == column, top + jnp.log(total), lse)
    lse_ref[...] = lse


def half_scores(queries, keys):
    rows, width = queries.shape
    heads = width // HEAD_DIM
    held = pltpu.with_memory_space_constraint(queries, pltpu.HBM)
    return pl.pallas_call(
        score_body,
        grid=(width // COLS_STEP,),
        in_specs=[pl.BlockSpec((rows, COLS_STEP), lambda j: (0, j))]
        + [pl.BlockSpec((2 * STEPS, COLS_STEP), lambda j: (0, j))] * HALF_VENUES,
        out_specs=[
            pl.BlockSpec((HEADS_STEP, 2, 2 * ROWS_HALF, KEYS_HALF), lambda j: (j, 0, 0, 0)),
            pl.BlockSpec((2 * ROWS_HALF, 128), lambda j: (0, 0)),
        ],
        out_shape=[
            jax.ShapeDtypeStruct((heads, 2, 2 * ROWS_HALF, KEYS_HALF), jnp.bfloat16),
            jax.ShapeDtypeStruct((2 * ROWS_HALF, 128), jnp.float32),
        ],
        compiler_params=pltpu.CompilerParams(vmem_limit_bytes=VMEM_LIMIT),
        name="half_scores",
    )(held, *keys)


def weigh_body(probs_ref, lse_ref, far_ref, weights_ref):
    step = pl.program_id(0)
    far = jnp.concatenate([far_ref[:, LSE_ITEM:], far_ref[:, :LSE_ITEM]], axis=1)
    share = 1.0 / (1.0 + jnp.exp(far - lse_ref[...])) * (1.0 / VENUES)
    lane = lax.broadcasted_iota(jnp.int32, lse_ref.shape, 1)
    for head in range(HEADS_STEP):
        means = []
        for item in range(2):
            column = step * HEADS_STEP + head + item * LSE_ITEM
            factor = jnp.sum(jnp.where(lane == column, share, 0.0), axis=1, keepdims=True)
            weights = probs_ref[head, item].astype(jnp.float32) * factor
            means.append(jnp.sum(weights.reshape(VENUES, NODE_STEPS, KEYS_HALF), axis=0))
        weights_ref[head] = jnp.concatenate(means, axis=0).astype(jnp.bfloat16)


def mean_weights(probs, lse, far_lse):
    heads = probs.shape[0]
    return pl.pallas_call(
        weigh_body,
        grid=(heads // HEADS_STEP,),
        in_specs=[
            pl.BlockSpec((HEADS_STEP, 2, 2 * ROWS_HALF, KEYS_HALF), lambda j: (j, 0, 0, 0)),
            pl.BlockSpec((2 * ROWS_HALF, 128), lambda j: (0, 0)),
            pl.BlockSpec((2 * ROWS_HALF, 128), lambda j: (0, 0)),
        ],
        out_specs=pl.BlockSpec((HEADS_STEP, 2 * NODE_STEPS, KEYS_HALF), lambda j: (j, 0, 0)),
        out_shape=jax.ShapeDtypeStruct((heads, 2 * NODE_STEPS, KEYS_HALF), jnp.bfloat16),
        compiler_params=pltpu.CompilerParams(vmem_limit_bytes=VMEM_LIMIT),
        name="mean_weights",
    )(probs, lse, far_lse)


def pool_body(first_ref, weights_ref, value_ref, out_ref):
    first = first_ref[0]
    row = lax.broadcasted_iota(jnp.int32, (2 * NODE_STEPS, HEAD_DIM), 0)
    for head in range(HEADS_STEP):
        span = slice(head * HEAD_DIM, (head + 1) * HEAD_DIM)
        pooled = [
            jnp.dot(
                weights_ref[head],
                jnp.concatenate(
                    [value_ref[first ^ venue, item, :, span] for venue in range(HALF_VENUES)], axis=0
                ),
                preferred_element_type=jnp.float32,
            )
            for item in range(2)
        ]
        out_ref[:, span] = jnp.where(row < NODE_STEPS, *pooled).astype(jnp.bfloat16)


def half_pool(first, weights, values):
    width = values.shape[3]
    return pl.pallas_call(
        pool_body,
        grid=(width // COLS_STEP,),
        in_specs=[
            pl.BlockSpec(memory_space=pltpu.SMEM),
            pl.BlockSpec((HEADS_STEP, 2 * NODE_STEPS, KEYS_HALF), lambda j: (j, 0, 0)),
            pl.BlockSpec((HALF_VENUES, 2, STEPS, COLS_STEP), lambda j: (0, 0, 0, j)),
        ],
        out_specs=pl.BlockSpec((2 * NODE_STEPS, COLS_STEP), lambda j: (0, j)),
        out_shape=jax.ShapeDtypeStruct((2 * NODE_STEPS, width), jnp.bfloat16),
        compiler_params=pltpu.CompilerParams(vmem_limit_bytes=VMEM_LIMIT),
        name="half_pool",
    )(first, weights, values)


def pad_lanes(width):
    return -(-width // 128) * 128


def stage_body(*refs, layer, count):
    first = len(refs) - count - 2
    token_ref, sems = refs[-2:]
    copies = []
    for place in range(count):
        copy = pltpu.make_async_copy(refs[place].at[layer], refs[first + place], sems.at[place])
        copy.start()
        copies.append(copy)
    token_ref[...] = jnp.zeros_like(token_ref)
    for copy in copies:
        copy.wait()


def stage_weights(weights, layer, after):
    held = [pltpu.with_memory_space_constraint(a, pltpu.HBM) for a in weights]
    shapes = [pltpu.VMEM(a.shape[1:], a.dtype) for a in weights]
    size = sum(a.size for a in weights) // ROUNDS
    out = pl.pallas_call(
        functools.partial(stage_body, layer=layer, count=len(held)),
        in_specs=[pl.BlockSpec(memory_space=pl.ANY)] * (len(held) + len(after)),
        out_specs=[pl.BlockSpec(memory_space=pltpu.VMEM)] * (len(shapes) + 1),
        out_shape=shapes + [jax.ShapeDtypeStruct((8, 128), jnp.float32)],
        scratch_shapes=[pltpu.SemaphoreType.DMA((len(held),))],
        compiler_params=pltpu.CompilerParams(vmem_limit_bytes=2 << 20),
        cost_estimate=pl.CostEstimate(flops=0, transcendentals=0, bytes_accessed=4 * size),
        name="stage_weights",
    )(*held, *after)
    return out[:-1], out[-1]


def column_tiles(width, tile):
    tile = tile if width % tile == 0 else width
    return [slice(start, start + tile) for start in range(0, width, tile)]


def expand_body(*refs, layer):
    node_refs, refs = refs[:4], refs[4:]
    mix_ref, gain_ref, norm_ref, gate_ref, up_ref, _, out_ref, scaled_ref = refs
    feat, width = gate_ref.shape
    padded = pad_lanes(width)
    edges = sum(mix_ref[kind].astype(jnp.float32) for kind in range(ETYPES))
    inverse = 1.0 / jnp.maximum(jnp.sum(edges, axis=1, keepdims=True), 1.0)
    squares = 0.0
    for span in column_tiles(feat, 512):
        nodes = jnp.concatenate([ref[:, span] for ref in node_refs], axis=0)
        message = 0.0
        for kind in range(ETYPES):
            message += gain_ref[layer, kind : kind + 1, span] * jnp.dot(
                mix_ref[kind], nodes, preferred_element_type=jnp.float32
            )
        pre = nodes.astype(jnp.float32) + message * inverse
        squares += jnp.sum(pre * pre, axis=1, keepdims=True)
        scaled_ref[:, span] = (pre * norm_ref[layer : layer + 1, span]).astype(jnp.bfloat16)
    if padded != width:
        out_ref[...] = jnp.zeros_like(out_ref)
    for place, ref in enumerate((gate_ref, up_ref)):
        for span in column_tiles(width, 256):
            sums = jnp.dot(scaled_ref[...], ref[:, span], preferred_element_type=jnp.float32)
            start = place * padded + span.start
            out_ref[:, start : start + sums.shape[1]] = sums.astype(jnp.bfloat16)
    high = squares.astype(jnp.bfloat16).astype(jnp.float32)
    lane = lax.broadcasted_iota(jnp.int32, (squares.shape[0], 128), 1)
    parts = jnp.where(lane == 0, high, jnp.where(lane == 1, squares - high, 0.0))
    out_ref[:, 2 * padded :] = parts.astype(jnp.bfloat16)


def expand(nodes, mix, gain, norm, gate, up, token, layer):
    part, feat = nodes[0].shape
    rows = len(nodes) * part
    columns = 2 * pad_lanes(gate.shape[1]) + 128
    held = [pltpu.with_memory_space_constraint(a, pltpu.VMEM) for a in (gate, up)]
    operands = [*nodes, mix, gain, norm, *held, token]
    return pl.pallas_call(
        functools.partial(expand_body, layer=layer),
        in_specs=[pl.BlockSpec(memory_space=pltpu.VMEM)] * len(operands),
        out_specs=pl.BlockSpec(memory_space=pltpu.VMEM),
        out_shape=jax.ShapeDtypeStruct((rows, columns), jnp.bfloat16),
        scratch_shapes=[pltpu.VMEM((rows, feat), jnp.bfloat16)],
        compiler_params=pltpu.CompilerParams(vmem_limit_bytes=VMEM_LIMIT),
        name="expand",
    )(*operands)


def contract_body(near_ref, far_ref, down_ref, *out_refs, swap):
    rows = near_ref.shape[0]
    width, feat = down_ref.shape
    padded = pad_lanes(width)

    def both(span):
        far = far_ref[:, span].astype(jnp.float32)
        if swap:
            part = rows // 4
            far = jnp.concatenate(
                [far[:part], far[2 * part : 3 * part], far[part : 2 * part], far[3 * part :]], axis=0
            )
        return near_ref[:, span].astype(jnp.float32) + far

    squares = jnp.sum(both(slice(2 * padded, 2 * padded + 128)), axis=1, keepdims=True)
    scale = lax.rsqrt(squares * (1.0 / D) + 1e-05)
    hidden = []
    for span in column_tiles(width, 256):
        gate = both(span) * scale
        up = both(slice(padded + span.start, padded + span.stop)) * scale
        hidden.append((gate * (1.0 / (1.0 + jnp.exp(-gate))) * up).astype(jnp.bfloat16))
    hidden = hidden[0] if len(hidden) == 1 else jnp.concatenate(hidden, axis=1)
    held = feat // (len(out_refs) // 2)
    for span in column_tiles(feat, 640):
        total = jnp.dot(hidden, down_ref[:, span], preferred_element_type=jnp.float32)
        part = span.start // held
        local = slice(span.start % held, span.start % held + span.stop - span.start)
        out_refs[2 * part][:, local] = total[: rows // 2]
        out_refs[2 * part + 1][:, local] = total[rows // 2 :].astype(jnp.bfloat16)


def contract(near, far, down, parts, swap):
    half, feat = near.shape[0] // 2, down.shape[1]
    held = pltpu.with_memory_space_constraint(down, pltpu.VMEM)
    shape = (half, feat // parts)
    out = pl.pallas_call(
        functools.partial(contract_body, swap=swap),
        in_specs=[pl.BlockSpec(memory_space=pltpu.VMEM)] * 3,
        out_specs=[pl.BlockSpec(memory_space=pltpu.VMEM)] * (2 * parts),
        out_shape=[
            jax.ShapeDtypeStruct(shape, jnp.float32),
            jax.ShapeDtypeStruct(shape, jnp.bfloat16),
        ]
        * parts,
        compiler_params=pltpu.CompilerParams(vmem_limit_bytes=VMEM_LIMIT),
        name="contract",
    )(near, far, held)
    return [out[2 * part : 2 * part + 2] for part in range(parts)]


def per_device(
    query_vecs,
    key_vecs,
    value_vecs,
    slot_map,
    edge_list,
    edge_types,
    type_gain,
    norm_gain,
    gate_proj,
    up_proj,
    down_proj,
):
    pairs_dev, inst_total, feat_width = query_vecs.shape
    gx_count = lax.axis_size("gx")
    ta_count = lax.axis_size("ta")
    me = lax.axis_index("gx")
    orders = bit_orders(gx_count, ta_count)
    last = len(orders[0]) - 1
    chunks = gx_count // 2
    groups = [list(range(chunks)), list(range(chunks, gx_count))]
    venue_idx = me * pairs_dev // STEPS
    slot_order = lax.dynamic_index_in_dim(slot_map, venue_idx, 0, keepdims=False)

    def picker(pairs, inst_of, places):
        shape = (places * 2 * pairs, pairs * inst_total)
        row = lax.broadcasted_iota(jnp.int32, (shape[0], inst_total), 0)
        inst = inst_of(row // (2 * pairs), row // pairs % 2)
        hit = inst == lax.broadcasted_iota(jnp.int32, (shape[0], inst_total), 1)
        slot = jnp.sum(jnp.where(hit, slot_order[None, :], 0), axis=1, keepdims=True)
        source = lax.broadcasted_iota(jnp.int32, shape, 0) % pairs * inst_total + slot
        return (source == lax.broadcasted_iota(jnp.int32, shape, 1)).astype(jnp.bfloat16)

    whole_venue = pairs_dev == STEPS
    direct = whole_venue and chunks == HALF_VENUES
    query_pairs = NODE_STEPS if whole_venue else pairs_dev
    rows = pairs_dev * inst_total
    query_vecs, key_vecs, value_vecs = (
        a.reshape(rows, feat_width) for a in (query_vecs, key_vecs, value_vecs)
    )

    def by_venue(block, venues):
        block = block.reshape(venues, -1, 2, rows // inst_total, feat_width)
        return block.transpose(0, 2, 1, 3, 4).reshape(venues, 2, -1, feat_width)

    def in_half(block):
        block = lax.all_to_all(
            block.reshape(chunks, -1, feat_width), "gx", 0, 0, axis_index_groups=groups, tiled=True
        )
        return by_venue(block, HALF_VENUES)

    def own_first(flip):
        return lambda place, item: (item ^ me // chunks) * chunks + (place ^ flip)

    pick = picker(query_pairs, lambda place, item: place ^ item * chunks, gx_count)
    (queries,) = arrange(pick, query_vecs)
    queries = lax.all_to_all(queries.reshape(gx_count, -1, feat_width), "gx", 0, 0, tiled=True)
    if not whole_venue:
        queries = by_venue(queries, VENUES)[:, :, STEPS - NODE_STEPS :]
    queries = queries.reshape(4 * ROWS_HALF, feat_width)
    (values,) = arrange(picker(pairs_dev, own_first(0), chunks), value_vecs)
    if direct:
        first = me % chunks
        pieces = arrange(picker(pairs_dev, own_first(first), chunks), key_vecs, chunks)
        keys = [pieces[0]]
        for flip in range(1, chunks):
            pairs = [(g, g ^ flip) for g in range(gx_count)]
            keys.append(lax.ppermute(pieces[flip], "gx", pairs))
        waited = keys[-7:]
        values, queries, waited = lax.optimization_barrier((values, queries, waited))
        keys[-7:] = waited
    else:
        first = me * 0
        (keys,) = arrange(picker(pairs_dev, own_first(0), chunks), key_vecs)
        keys = in_half(keys)
        keys = [keys[venue].reshape(2 * STEPS, feat_width) for venue in range(HALF_VENUES)]
    first = first[None].astype(jnp.int32)
    values = in_half(values)
    row_total = inst_total * NODE_STEPS
    row = jnp.arange(row_total)
    place = row // NODE_STEPS
    inst_at = [
        me ^ sum((place >> (last - stage) & 1) << bit for stage, bit in enumerate(order))
        for order in orders[:2]
    ]
    inst_at = jnp.where(lax.axis_index("ta") % 2 == 0, inst_at[0], inst_at[1])
    at_source = (edge_list[:, 0][:, None] == inst_at[None, :]).astype(jnp.bfloat16)
    at_target = edge_list[:, 1][:, None] == inst_at[None, :]
    same_step = row[:, None] % NODE_STEPS == row[None, :] % NODE_STEPS
    typed = at_target[None] & (edge_types[None, :] == jnp.arange(ETYPES)[:, None])[:, :, None]
    mix = jnp.einsum(
        "ter,ec->trc", typed.astype(jnp.bfloat16), at_source, preferred_element_type=jnp.float32
    )
    mix = jnp.where(same_step[None], mix, 0.0).astype(jnp.bfloat16)
    keys, mix, type_gain = lax.optimization_barrier((keys, mix, type_gain))
    probs, lse = half_scores(queries, keys)
    far_lse = swap_stage(lse, orders, last)
    pooled = half_pool(first, mean_weights(probs, lse, far_lse), values)
    (gate,), token = stage_weights([gate_proj], 0, [pooled])
    pooled = join_pair(pooled, orders, last).astype(jnp.bfloat16)
    pooled, token = lax.optimization_barrier((pooled, token))
    (up, down), token = stage_weights([up_proj, down_proj], 0, [token])
    parts = SUM_PARTS if feat_width % (SUM_PARTS * 128) == 0 else 1
    part_width = feat_width // parts
    for layer_idx in range(ROUNDS):
        nodes = gather_rows(pooled, orders, last)
        near_sums = expand(nodes, mix, type_gain, norm_gain, gate, up, token, layer_idx)
        if ta_count == 2:
            far_sums = lax.ppermute(near_sums, "ta", [(0, 1), (1, 0)])
        else:
            far_sums = lax.psum(near_sums.astype(jnp.float32), "ta") - near_sums.astype(jnp.float32)
        sums = contract(near_sums, far_sums, down, parts, ta_count == 2)
        final = layer_idx + 1 == ROUNDS
        settled = []
        for part, (held, give) in enumerate(sums):
            for stage in range(last + 1 if final else last):
                if stage:
                    half = held.shape[0] // 2
                    held, give = held[:half], held[half:].astype(jnp.bfloat16)
                taken = swap_stage(give, orders, stage)
                if not final and part == 0 and stage == 0:
                    (down,), token = stage_weights([down_proj], layer_idx + 1, [give])
                    taken, token = lax.optimization_barrier((taken, token))
                held = held + taken.astype(jnp.float32)
            if not final:
                held = join_pair(held.astype(jnp.bfloat16), orders, last)
            rows_kept = pooled[: held.shape[0], part * part_width : (part + 1) * part_width]
            settled.append((rows_kept.astype(jnp.float32) + held).astype(jnp.bfloat16))
        pooled = jnp.concatenate(settled, axis=1)
        if not final:
            (gate, up), token = stage_weights([gate_proj, up_proj], layer_idx + 1, [pooled, token])
    return pooled


def solution(mesh):
    placed = (
        P("gx", None, "ta"),
        P("gx", None, "ta"),
        P("gx", None, "ta"),
        P(),
        P(),
        P(),
        P(None, None, "ta"),
        P(None, "ta"),
        P(None, "ta", "gx"),
        P(None, "ta", "gx"),
        P(None, "gx", "ta"),
    )
    return jax.shard_map(
        per_device, mesh=mesh, in_specs=placed, out_specs=P("gx", "ta"), check_vma=False
    )
```

```python
import functools

import jax
import jax.numpy as jnp
from jax import lax
from jax.experimental import pallas as pl
from jax.experimental.pallas import tpu as pltpu
from jax.sharding import PartitionSpec as P

D = 5120
HEAD_DIM = 128
VENUES = 16
STEPS = 16
NODE_STEPS = 8
ROUNDS = 2
ETYPES = 3
HALF_VENUES = VENUES // 2
HEADS_STEP = 5
COLS_STEP = HEADS_STEP * HEAD_DIM
ROWS_HALF = HALF_VENUES * NODE_STEPS
KEYS_HALF = HALF_VENUES * STEPS
LSE_ITEM = 64
VMEM_LIMIT = 8 << 20


def stage_bits(count):
    return list(range(count.bit_length() - 1))


def bit_orders(gx_count, ta_count):
    plain = stage_bits(gx_count)
    if ta_count != 2:
        return [plain] * ta_count
    return [plain, [plain[1], plain[0]] + plain[2:]]


def swap_stage(block, orders, *stages):
    gx_count, ta_count = lax.axis_size("gx"), lax.axis_size("ta")
    flips = [sum(1 << order[stage] for stage in stages) for order in orders]
    pairs = [
        (g * ta_count + t, (g ^ flips[t]) * ta_count + t)
        for g in range(gx_count)
        for t in range(ta_count)
    ]
    return lax.ppermute(block, ("gx", "ta"), pairs)


def gather_rows(held, orders, last):
    for stage in reversed(range(2, last)):
        held = jnp.concatenate([held, swap_stage(held, orders, stage)], axis=0)
    return [
        held,
        swap_stage(held, orders, 1),
        swap_stage(held, orders, 0),
        swap_stage(held, orders, 0, 1),
    ]


def join_pair(mine, orders, last):
    taken = swap_stage(mine, orders, last)
    half = mine.shape[0] // 2
    taken = jnp.concatenate([taken[half:], taken[:half]], axis=0)
    return mine.astype(jnp.float32) + taken.astype(jnp.float32)


def arrange_body(pick_ref, source_ref, *out_refs):
    moved = jnp.dot(pick_ref[...], source_ref[...], preferred_element_type=jnp.float32)
    moved = moved.astype(jnp.bfloat16)
    rows = moved.shape[0] // len(out_refs)
    for place, ref in enumerate(out_refs):
        ref[...] = moved[place * rows : (place + 1) * rows]


def arrange(pick, source, pieces=1):
    rows, taken = pick.shape
    total, width = source.shape
    last = total // taken - 1
    cols = 1280 if width % 1280 == 0 else COLS_STEP
    return pl.pallas_call(
        arrange_body,
        grid=(width // cols,),
        in_specs=[
            pl.BlockSpec((rows, taken), lambda j: (0, 0)),
            pl.BlockSpec((taken, cols), lambda j: (last, j)),
        ],
        out_specs=[pl.BlockSpec((rows // pieces, cols), lambda j: (0, j))] * pieces,
        out_shape=[jax.ShapeDtypeStruct((rows // pieces, width), jnp.bfloat16)] * pieces,
        compiler_params=pltpu.CompilerParams(vmem_limit_bytes=VMEM_LIMIT),
        name="arrange",
    )(pick, source)


def score_body(query_ref, *refs):
    key_refs, probs_ref, lse_ref = refs[:HALF_VENUES], refs[-2], refs[-1]
    step = pl.program_id(0)

    @pl.when(step == 0)
    def _():
        lse_ref[...] = jnp.zeros_like(lse_ref)

    shape = (VENUES, 2, NODE_STEPS, COLS_STEP)
    both = query_ref[...].astype(jnp.float32).reshape(shape)
    full = (2 * ROWS_HALF, KEYS_HALF)
    query_step = lax.broadcasted_iota(jnp.int32, full, 0) % NODE_STEPS + (STEPS - NODE_STEPS)
    key_step = lax.broadcasted_iota(jnp.int32, full, 1) % STEPS
    allowed = key_step <= query_step
    lane = lax.broadcasted_iota(jnp.int32, lse_ref.shape, 1)
    lse = lse_ref[...]
    for item in range(2):
        queries = both[:, item].reshape(2 * ROWS_HALF, COLS_STEP).astype(jnp.bfloat16)
        keys = jnp.concatenate(
            [ref[item * STEPS : (item + 1) * STEPS, :] for ref in key_refs], axis=0
        )
        for head in range(HEADS_STEP):
            span = slice(head * HEAD_DIM, (head + 1) * HEAD_DIM)
            scores = lax.dot_general(
                queries[:, span],
                keys[:, span],
                (((1,), (1,)), ((), ())),
                preferred_element_type=jnp.float32,
            ) * (1.0 / HEAD_DIM**0.5)
            scores = jnp.where(allowed, scores, -1e30)
            top = jnp.max(scores, axis=1, keepdims=True)
            expd = jnp.exp(scores - top)
            total = jnp.sum(expd, axis=1, keepdims=True)
            probs_ref[head, item] = (expd * (1.0 / total)).astype(jnp.bfloat16)
            column = step * HEADS_STEP + head + item * LSE_ITEM
            lse = jnp.where(lane == column, top + jnp.log(total), lse)
    lse_ref[...] = lse


def half_scores(queries, keys):
    rows, width = queries.shape
    heads = width // HEAD_DIM
    held = pltpu.with_memory_space_constraint(queries, pltpu.HBM)
    return pl.pallas_call(
        score_body,
        grid=(width // COLS_STEP,),
        in_specs=[pl.BlockSpec((rows, COLS_STEP), lambda j: (0, j))]
        + [pl.BlockSpec((2 * STEPS, COLS_STEP), lambda j: (0, j))] * HALF_VENUES,
        out_specs=[
            pl.BlockSpec((HEADS_STEP, 2, 2 * ROWS_HALF, KEYS_HALF), lambda j: (j, 0, 0, 0)),
            pl.BlockSpec((2 * ROWS_HALF, 128), lambda j: (0, 0)),
        ],
        out_shape=[
            jax.ShapeDtypeStruct((heads, 2, 2 * ROWS_HALF, KEYS_HALF), jnp.bfloat16),
            jax.ShapeDtypeStruct((2 * ROWS_HALF, 128), jnp.float32),
        ],
        compiler_params=pltpu.CompilerParams(vmem_limit_bytes=VMEM_LIMIT),
        name="half_scores",
    )(held, *keys)


def weigh_body(probs_ref, lse_ref, far_ref, weights_ref):
    step = pl.program_id(0)
    far = jnp.concatenate([far_ref[:, LSE_ITEM:], far_ref[:, :LSE_ITEM]], axis=1)
    share = 1.0 / (1.0 + jnp.exp(far - lse_ref[...])) * (1.0 / VENUES)
    lane = lax.broadcasted_iota(jnp.int32, lse_ref.shape, 1)
    for head in range(HEADS_STEP):
        means = []
        for item in range(2):
            column = step * HEADS_STEP + head + item * LSE_ITEM
            factor = jnp.sum(jnp.where(lane == column, share, 0.0), axis=1, keepdims=True)
            weights = probs_ref[head, item].astype(jnp.float32) * factor
            means.append(jnp.sum(weights.reshape(VENUES, NODE_STEPS, KEYS_HALF), axis=0))
        weights_ref[head] = jnp.concatenate(means, axis=0).astype(jnp.bfloat16)


def mean_weights(probs, lse, far_lse):
    heads = probs.shape[0]
    return pl.pallas_call(
        weigh_body,
        grid=(heads // HEADS_STEP,),
        in_specs=[
            pl.BlockSpec((HEADS_STEP, 2, 2 * ROWS_HALF, KEYS_HALF), lambda j: (j, 0, 0, 0)),
            pl.BlockSpec((2 * ROWS_HALF, 128), lambda j: (0, 0)),
            pl.BlockSpec((2 * ROWS_HALF, 128), lambda j: (0, 0)),
        ],
        out_specs=pl.BlockSpec((HEADS_STEP, 2 * NODE_STEPS, KEYS_HALF), lambda j: (j, 0, 0)),
        out_shape=jax.ShapeDtypeStruct((heads, 2 * NODE_STEPS, KEYS_HALF), jnp.bfloat16),
        compiler_params=pltpu.CompilerParams(vmem_limit_bytes=VMEM_LIMIT),
        name="mean_weights",
    )(probs, lse, far_lse)


def pool_body(first_ref, weights_ref, value_ref, out_ref):
    first = first_ref[0]
    row = lax.broadcasted_iota(jnp.int32, (2 * NODE_STEPS, HEAD_DIM), 0)
    for head in range(HEADS_STEP):
        span = slice(head * HEAD_DIM, (head + 1) * HEAD_DIM)
        pooled = [
            jnp.dot(
                weights_ref[head],
                jnp.concatenate(
                    [value_ref[first ^ venue, item, :, span] for venue in range(HALF_VENUES)], axis=0
                ),
                preferred_element_type=jnp.float32,
            )
            for item in range(2)
        ]
        out_ref[:, span] = jnp.where(row < NODE_STEPS, *pooled).astype(jnp.bfloat16)


def half_pool(first, weights, values):
    width = values.shape[3]
    return pl.pallas_call(
        pool_body,
        grid=(width // COLS_STEP,),
        in_specs=[
            pl.BlockSpec(memory_space=pltpu.SMEM),
            pl.BlockSpec((HEADS_STEP, 2 * NODE_STEPS, KEYS_HALF), lambda j: (j, 0, 0)),
            pl.BlockSpec((HALF_VENUES, 2, STEPS, COLS_STEP), lambda j: (0, 0, 0, j)),
        ],
        out_specs=pl.BlockSpec((2 * NODE_STEPS, COLS_STEP), lambda j: (0, j)),
        out_shape=jax.ShapeDtypeStruct((2 * NODE_STEPS, width), jnp.bfloat16),
        compiler_params=pltpu.CompilerParams(vmem_limit_bytes=VMEM_LIMIT),
        name="half_pool",
    )(first, weights, values)


def pad_lanes(width):
    return -(-width // 128) * 128


def stage_body(*refs, layer, count):
    first = len(refs) - count - 2
    token_ref, sems = refs[-2:]
    copies = []
    for place in range(count):
        copy = pltpu.make_async_copy(refs[place].at[layer], refs[first + place], sems.at[place])
        copy.start()
        copies.append(copy)
    token_ref[...] = jnp.zeros_like(token_ref)
    for copy in copies:
        copy.wait()


def stage_weights(weights, layer, after):
    held = [pltpu.with_memory_space_constraint(a, pltpu.HBM) for a in weights]
    shapes = [pltpu.VMEM(a.shape[1:], a.dtype) for a in weights]
    size = sum(a.size for a in weights) // ROUNDS
    out = pl.pallas_call(
        functools.partial(stage_body, layer=layer, count=len(held)),
        in_specs=[pl.BlockSpec(memory_space=pl.ANY)] * (len(held) + len(after)),
        out_specs=[pl.BlockSpec(memory_space=pltpu.VMEM)] * (len(shapes) + 1),
        out_shape=shapes + [jax.ShapeDtypeStruct((8, 128), jnp.float32)],
        scratch_shapes=[pltpu.SemaphoreType.DMA((len(held),))],
        compiler_params=pltpu.CompilerParams(vmem_limit_bytes=2 << 20),
        cost_estimate=pl.CostEstimate(flops=0, transcendentals=0, bytes_accessed=4 * size),
        name="stage_weights",
    )(*held, *after)
    return out[:-1], out[-1]


def column_tiles(width, tile):
    tile = tile if width % tile == 0 else width
    return [slice(start, start + tile) for start in range(0, width, tile)]


def expand_body(*refs, layer):
    node_refs, refs = refs[:4], refs[4:]
    mix_ref, gain_ref, norm_ref, gate_ref, up_ref, _, out_ref, scaled_ref = refs
    feat, width = gate_ref.shape
    padded = pad_lanes(width)
    edges = sum(mix_ref[kind].astype(jnp.float32) for kind in range(ETYPES))
    inverse = 1.0 / jnp.maximum(jnp.sum(edges, axis=1, keepdims=True), 1.0)
    squares = 0.0
    for span in column_tiles(feat, 512):
        nodes = jnp.concatenate([ref[:, span] for ref in node_refs], axis=0)
        message = 0.0
        for kind in range(ETYPES):
            message += gain_ref[layer, kind : kind + 1, span] * jnp.dot(
                mix_ref[kind], nodes, preferred_element_type=jnp.float32
            )
        pre = nodes.astype(jnp.float32) + message * inverse
        squares += jnp.sum(pre * pre, axis=1, keepdims=True)
        scaled_ref[:, span] = (pre * norm_ref[layer : layer + 1, span]).astype(jnp.bfloat16)
    if padded != width:
        out_ref[...] = jnp.zeros_like(out_ref)
    for place, ref in enumerate((gate_ref, up_ref)):
        for span in column_tiles(width, 256):
            sums = jnp.dot(scaled_ref[...], ref[:, span], preferred_element_type=jnp.float32)
            start = place * padded + span.start
            out_ref[:, start : start + sums.shape[1]] = sums.astype(jnp.bfloat16)
    high = squares.astype(jnp.bfloat16).astype(jnp.float32)
    lane = lax.broadcasted_iota(jnp.int32, (squares.shape[0], 128), 1)
    parts = jnp.where(lane == 0, high, jnp.where(lane == 1, squares - high, 0.0))
    out_ref[:, 2 * padded :] = parts.astype(jnp.bfloat16)


def expand(nodes, mix, gain, norm, gate, up, token, layer):
    part, feat = nodes[0].shape
    rows = len(nodes) * part
    columns = 2 * pad_lanes(gate.shape[1]) + 128
    held = [pltpu.with_memory_space_constraint(a, pltpu.VMEM) for a in (gate, up)]
    operands = [*nodes, mix, gain, norm, *held, token]
    return pl.pallas_call(
        functools.partial(expand_body, layer=layer),
        in_specs=[pl.BlockSpec(memory_space=pltpu.VMEM)] * len(operands),
        out_specs=pl.BlockSpec(memory_space=pltpu.VMEM),
        out_shape=jax.ShapeDtypeStruct((rows, columns), jnp.bfloat16),
        scratch_shapes=[pltpu.VMEM((rows, feat), jnp.bfloat16)],
        compiler_params=pltpu.CompilerParams(vmem_limit_bytes=VMEM_LIMIT),
        name="expand",
    )(*operands)


def contract_body(near_ref, far_ref, down_ref, *out_refs, swap):
    rows = near_ref.shape[0]
    width, feat = down_ref.shape
    padded = pad_lanes(width)

    def both(span):
        far = far_ref[:, span].astype(jnp.float32)
        if swap:
            part = rows // 4
            far = jnp.concatenate(
                [far[:part], far[2 * part : 3 * part], far[part : 2 * part], far[3 * part :]], axis=0
            )
        return near_ref[:, span].astype(jnp.float32) + far

    squares = jnp.sum(both(slice(2 * padded, 2 * padded + 128)), axis=1, keepdims=True)
    scale = lax.rsqrt(squares * (1.0 / D) + 1e-05)
    hidden = []
    for span in column_tiles(width, 256):
        gate = both(span) * scale
        up = both(slice(padded + span.start, padded + span.stop)) * scale
        hidden.append((gate * (1.0 / (1.0 + jnp.exp(-gate))) * up).astype(jnp.bfloat16))
    hidden = hidden[0] if len(hidden) == 1 else jnp.concatenate(hidden, axis=1)
    part = rows // 4
    for span in column_tiles(feat, 640):
        total = jnp.dot(hidden, down_ref[:, span], preferred_element_type=jnp.float32)
        for place, ref in enumerate(out_refs):
            ref[:, span] = total[place * part : (place + 1) * part].astype(ref.dtype)


def contract(near, far, down, swap):
    shape = (near.shape[0] // 4, down.shape[1])
    held = pltpu.with_memory_space_constraint(down, pltpu.VMEM)
    return pl.pallas_call(
        functools.partial(contract_body, swap=swap),
        in_specs=[pl.BlockSpec(memory_space=pltpu.VMEM)] * 3,
        out_specs=[pl.BlockSpec(memory_space=pltpu.VMEM)] * 4,
        out_shape=[jax.ShapeDtypeStruct(shape, jnp.float32)]
        + [jax.ShapeDtypeStruct(shape, jnp.bfloat16)] * 3,
        compiler_params=pltpu.CompilerParams(vmem_limit_bytes=VMEM_LIMIT),
        name="contract",
    )(near, far, held)


def per_device(
    query_vecs,
    key_vecs,
    value_vecs,
    slot_map,
    edge_list,
    edge_types,
    type_gain,
    norm_gain,
    gate_proj,
    up_proj,
    down_proj,
):
    pairs_dev, inst_total, feat_width = query_vecs.shape
    gx_count = lax.axis_size("gx")
    ta_count = lax.axis_size("ta")
    me = lax.axis_index("gx")
    orders = bit_orders(gx_count, ta_count)
    last = len(orders[0]) - 1
    chunks = gx_count // 2
    groups = [list(range(chunks)), list(range(chunks, gx_count))]
    venue_idx = me * pairs_dev // STEPS
    slot_order = lax.dynamic_index_in_dim(slot_map, venue_idx, 0, keepdims=False)

    def picker(pairs, inst_of, places):
        shape = (places * 2 * pairs, pairs * inst_total)
        row = lax.broadcasted_iota(jnp.int32, (shape[0], inst_total), 0)
        inst = inst_of(row // (2 * pairs), row // pairs % 2)
        hit = inst == lax.broadcasted_iota(jnp.int32, (shape[0], inst_total), 1)
        slot = jnp.sum(jnp.where(hit, slot_order[None, :], 0), axis=1, keepdims=True)
        source = lax.broadcasted_iota(jnp.int32, shape, 0) % pairs * inst_total + slot
        return (source == lax.broadcasted_iota(jnp.int32, shape, 1)).astype(jnp.bfloat16)

    whole_venue = pairs_dev == STEPS
    direct = whole_venue and chunks == HALF_VENUES
    query_pairs = NODE_STEPS if whole_venue else pairs_dev
    rows = pairs_dev * inst_total
    query_vecs, key_vecs, value_vecs = (
        a.reshape(rows, feat_width) for a in (query_vecs, key_vecs, value_vecs)
    )

    def by_venue(block, venues):
        block = block.reshape(venues, -1, 2, rows // inst_total, feat_width)
        return block.transpose(0, 2, 1, 3, 4).reshape(venues, 2, -1, feat_width)

    def in_half(block):
        block = lax.all_to_all(
            block.reshape(chunks, -1, feat_width), "gx", 0, 0, axis_index_groups=groups, tiled=True
        )
        return by_venue(block, HALF_VENUES)

    def own_first(flip):
        return lambda place, item: (item ^ me // chunks) * chunks + (place ^ flip)

    pick = picker(query_pairs, lambda place, item: place ^ item * chunks, gx_count)
    (queries,) = arrange(pick, query_vecs)
    queries = lax.all_to_all(queries.reshape(gx_count, -1, feat_width), "gx", 0, 0, tiled=True)
    if not whole_venue:
        queries = by_venue(queries, VENUES)[:, :, STEPS - NODE_STEPS :]
    queries = queries.reshape(4 * ROWS_HALF, feat_width)
    (values,) = arrange(picker(pairs_dev, own_first(0), chunks), value_vecs)
    if direct:
        first = me % chunks
        pieces = arrange(picker(pairs_dev, own_first(first), chunks), key_vecs, chunks)
        keys = [pieces[0]]
        for flip in range(1, chunks):
            pairs = [(g, g ^ flip) for g in range(gx_count)]
            keys.append(lax.ppermute(pieces[flip], "gx", pairs))
        waited = keys[-7:]
        values, queries, waited = lax.optimization_barrier((values, queries, waited))
        keys[-7:] = waited
    else:
        first = me * 0
        (keys,) = arrange(picker(pairs_dev, own_first(0), chunks), key_vecs)
        keys = in_half(keys)
        keys = [keys[venue].reshape(2 * STEPS, feat_width) for venue in range(HALF_VENUES)]
    first = first[None].astype(jnp.int32)
    values = in_half(values)
    row_total = inst_total * NODE_STEPS
    row = jnp.arange(row_total)
    place = row // NODE_STEPS
    inst_at = [
        me ^ sum((place >> (last - stage) & 1) << bit for stage, bit in enumerate(order))
        for order in orders[:2]
    ]
    inst_at = jnp.where(lax.axis_index("ta") % 2 == 0, inst_at[0], inst_at[1])
    at_source = (edge_list[:, 0][:, None] == inst_at[None, :]).astype(jnp.bfloat16)
    at_target = edge_list[:, 1][:, None] == inst_at[None, :]
    same_step = row[:, None] % NODE_STEPS == row[None, :] % NODE_STEPS
    typed = at_target[None] & (edge_types[None, :] == jnp.arange(ETYPES)[:, None])[:, :, None]
    mix = jnp.einsum(
        "ter,ec->trc", typed.astype(jnp.bfloat16), at_source, preferred_element_type=jnp.float32
    )
    mix = jnp.where(same_step[None], mix, 0.0).astype(jnp.bfloat16)
    keys, mix, type_gain = lax.optimization_barrier((keys, mix, type_gain))
    probs, lse = half_scores(queries, keys)
    far_lse = swap_stage(lse, orders, last)
    pooled = half_pool(first, mean_weights(probs, lse, far_lse), values)
    (gate, up), token = stage_weights([gate_proj, up_proj], 0, [pooled])
    pooled = join_pair(pooled, orders, last).astype(jnp.bfloat16)
    pooled, token = lax.optimization_barrier((pooled, token))
    (down,), token = stage_weights([down_proj], 0, [token])
    for layer_idx in range(ROUNDS):
        nodes = gather_rows(pooled, orders, last)
        near_sums = expand(nodes, mix, type_gain, norm_gain, gate, up, token, layer_idx)
        if ta_count == 2:
            far_sums = lax.ppermute(near_sums, "ta", [(0, 1), (1, 0)])
        else:
            far_sums = lax.psum(near_sums.astype(jnp.float32), "ta") - near_sums.astype(jnp.float32)
        held, *gives = contract(near_sums, far_sums, down, ta_count == 2)
        final = layer_idx + 1 == ROUNDS
        taken = [
            swap_stage(give, orders, *stages)
            for give, stages in zip(gives, ((1,), (0,), (0, 1)))
        ]
        if not final:
            (gate, up), token = stage_weights([gate_proj, up_proj], layer_idx + 1, gives)
            taken, token = lax.optimization_barrier((taken, token))
        for block in taken:
            held = held + block.astype(jnp.float32)
        for stage in range(2, last + 1 if final else last):
            half = held.shape[0] // 2
            held, give = held[:half], held[half:].astype(jnp.bfloat16)
            held = held + swap_stage(give, orders, stage).astype(jnp.float32)
        if not final:
            held = join_pair(held.astype(jnp.bfloat16), orders, last)
        pooled = (pooled[: held.shape[0]].astype(jnp.float32) + held).astype(jnp.bfloat16)
        if not final:
            (down,), token = stage_weights([down_proj], layer_idx + 1, [pooled, token])
    return pooled


def solution(mesh):
    placed = (
        P("gx", None, "ta"),
        P("gx", None, "ta"),
        P("gx", None, "ta"),
        P(),
        P(),
        P(),
        P(None, None, "ta"),
        P(None, "ta"),
        P(None, "ta", "gx"),
        P(None, "ta", "gx"),
        P(None, "gx", "ta"),
    )
    return jax.shard_map(
        per_device, mesh=mesh, in_specs=placed, out_specs=P("gx", "ta"), check_vma=False
    )
```

```python
import functools

import jax
import jax.numpy as jnp
from jax import lax
from jax.experimental import pallas as pl
from jax.experimental.pallas import tpu as pltpu
from jax.sharding import PartitionSpec as P

D = 5120
HEAD_DIM = 128
VENUES = 16
STEPS = 16
NODE_STEPS = 8
ROUNDS = 2
ETYPES = 3
HALF_VENUES = VENUES // 2
HEADS_STEP = 5
COLS_STEP = HEADS_STEP * HEAD_DIM
ROWS_HALF = HALF_VENUES * NODE_STEPS
KEYS_HALF = HALF_VENUES * STEPS
LSE_ITEM = 32
VMEM_LIMIT = 8 << 20


def stage_bits(count):
    return list(range(count.bit_length() - 1))


def bit_orders(gx_count, ta_count):
    plain = stage_bits(gx_count)
    if ta_count != 2:
        return [plain] * ta_count
    return [plain, [plain[1], plain[0]] + plain[2:]]


def swap_stage(block, orders, *stages):
    gx_count, ta_count = lax.axis_size("gx"), lax.axis_size("ta")
    flips = [sum(1 << order[stage] for stage in stages) for order in orders]
    pairs = [
        (g * ta_count + t, (g ^ flips[t]) * ta_count + t)
        for g in range(gx_count)
        for t in range(ta_count)
    ]
    return lax.ppermute(block, ("gx", "ta"), pairs)


def gather_rows(held, orders, last):
    for stage in reversed(range(2, last)):
        held = jnp.concatenate([held, swap_stage(held, orders, stage)], axis=0)
    return [
        held,
        swap_stage(held, orders, 1),
        swap_stage(held, orders, 0),
        swap_stage(held, orders, 0, 1),
    ]


def join_pair(mine, orders, last):
    taken = swap_stage(mine, orders, last)
    half = mine.shape[0] // 2
    taken = jnp.concatenate([taken[half:], taken[:half]], axis=0)
    return mine.astype(jnp.float32) + taken.astype(jnp.float32)


def arrange_body(pick_ref, source_ref, *out_refs):
    moved = jnp.dot(pick_ref[...], source_ref[...], preferred_element_type=jnp.float32)
    moved = moved.astype(jnp.bfloat16)
    rows = moved.shape[0] // len(out_refs)
    for place, ref in enumerate(out_refs):
        ref[...] = moved[place * rows : (place + 1) * rows]


def arrange(pick, source, pieces=1):
    rows, taken = pick.shape
    total, width = source.shape
    last = total // taken - 1
    cols = 1280 if width % 1280 == 0 else COLS_STEP
    return pl.pallas_call(
        arrange_body,
        grid=(width // cols,),
        in_specs=[
            pl.BlockSpec((rows, taken), lambda j: (0, 0)),
            pl.BlockSpec((taken, cols), lambda j: (last, j)),
        ],
        out_specs=[pl.BlockSpec((rows // pieces, cols), lambda j: (0, j))] * pieces,
        out_shape=[jax.ShapeDtypeStruct((rows // pieces, width), jnp.bfloat16)] * pieces,
        compiler_params=pltpu.CompilerParams(vmem_limit_bytes=VMEM_LIMIT),
        name="arrange",
    )(pick, source)


def score_body(query_ref, *refs):
    key_refs = refs[:HALF_VENUES]
    probs_ref, lse_ref, packed_ref = refs[HALF_VENUES:]
    step = pl.program_id(0)

    @pl.when(step == 0)
    def _():
        lse_ref[...] = jnp.zeros_like(lse_ref)

    shape = (VENUES, 2, NODE_STEPS, COLS_STEP)
    both = query_ref[...].astype(jnp.float32).reshape(shape)
    full = (2 * ROWS_HALF, KEYS_HALF)
    query_step = lax.broadcasted_iota(jnp.int32, full, 0) % NODE_STEPS + (STEPS - NODE_STEPS)
    key_step = lax.broadcasted_iota(jnp.int32, full, 1) % STEPS
    allowed = key_step <= query_step
    lane = lax.broadcasted_iota(jnp.int32, lse_ref.shape, 1)
    lse = lse_ref[...]
    for item in range(2):
        queries = both[:, item].reshape(2 * ROWS_HALF, COLS_STEP).astype(jnp.bfloat16)
        keys = jnp.concatenate(
            [ref[item * STEPS : (item + 1) * STEPS, :] for ref in key_refs], axis=0
        )
        for head in range(HEADS_STEP):
            span = slice(head * HEAD_DIM, (head + 1) * HEAD_DIM)
            scores = lax.dot_general(
                queries[:, span],
                keys[:, span],
                (((1,), (1,)), ((), ())),
                preferred_element_type=jnp.float32,
            ) * (1.0 / HEAD_DIM**0.5)
            scores = jnp.where(allowed, scores, -1e30)
            top = jnp.max(scores, axis=1, keepdims=True)
            expd = jnp.exp(scores - top)
            total = jnp.sum(expd, axis=1, keepdims=True)
            probs_ref[head, item] = (expd * (1.0 / total)).astype(jnp.bfloat16)
            column = step * HEADS_STEP + head + item * LSE_ITEM
            lse = jnp.where(lane == column, top + jnp.log(total), lse)
    lse_ref[...] = lse
    low, high = lse[:ROWS_HALF], pltpu.roll(lse[ROWS_HALF:], 2 * LSE_ITEM, 1)
    packed_ref[...] = jnp.where(lane[:ROWS_HALF] < 2 * LSE_ITEM, low, high)


def half_scores(queries, keys):
    rows, width = queries.shape
    heads = width // HEAD_DIM
    held = pltpu.with_memory_space_constraint(queries, pltpu.HBM)
    return pl.pallas_call(
        score_body,
        grid=(width // COLS_STEP,),
        in_specs=[pl.BlockSpec((rows, COLS_STEP), lambda j: (0, j))]
        + [pl.BlockSpec((2 * STEPS, COLS_STEP), lambda j: (0, j))] * HALF_VENUES,
        out_specs=[
            pl.BlockSpec((HEADS_STEP, 2, 2 * ROWS_HALF, KEYS_HALF), lambda j: (j, 0, 0, 0)),
            pl.BlockSpec((2 * ROWS_HALF, 128), lambda j: (0, 0)),
            pl.BlockSpec((ROWS_HALF, 128), lambda j: (0, 0)),
        ],
        out_shape=[
            jax.ShapeDtypeStruct((heads, 2, 2 * ROWS_HALF, KEYS_HALF), jnp.bfloat16),
            jax.ShapeDtypeStruct((2 * ROWS_HALF, 128), jnp.float32),
            jax.ShapeDtypeStruct((ROWS_HALF, 128), jnp.float32),
        ],
        compiler_params=pltpu.CompilerParams(vmem_limit_bytes=VMEM_LIMIT),
        name="half_scores",
    )(held, *keys)


def weigh_body(probs_ref, lse_ref, far_ref, weights_ref):
    step = pl.program_id(0)
    lane = lax.broadcasted_iota(jnp.int32, lse_ref.shape, 1)
    far = jnp.concatenate([far_ref[...], pltpu.roll(far_ref[...], 2 * LSE_ITEM, 1)], axis=0)
    far = jnp.where(
        lane < LSE_ITEM, pltpu.roll(far, 128 - LSE_ITEM, 1), pltpu.roll(far, LSE_ITEM, 1)
    )
    share = 1.0 / (1.0 + jnp.exp(far - lse_ref[...])) * (1.0 / VENUES)
    for head in range(HEADS_STEP):
        means = []
        for item in range(2):
            column = step * HEADS_STEP + head + item * LSE_ITEM
            factor = jnp.sum(jnp.where(lane == column, share, 0.0), axis=1, keepdims=True)
            weights = probs_ref[head, item].astype(jnp.float32) * factor
            means.append(jnp.sum(weights.reshape(VENUES, NODE_STEPS, KEYS_HALF), axis=0))
        weights_ref[head] = jnp.concatenate(means, axis=0).astype(jnp.bfloat16)


def mean_weights(probs, lse, far_lse):
    heads = probs.shape[0]
    return pl.pallas_call(
        weigh_body,
        grid=(heads // HEADS_STEP,),
        in_specs=[
            pl.BlockSpec((HEADS_STEP, 2, 2 * ROWS_HALF, KEYS_HALF), lambda j: (j, 0, 0, 0)),
            pl.BlockSpec((2 * ROWS_HALF, 128), lambda j: (0, 0)),
            pl.BlockSpec((ROWS_HALF, 128), lambda j: (0, 0)),
        ],
        out_specs=pl.BlockSpec((HEADS_STEP, 2 * NODE_STEPS, KEYS_HALF), lambda j: (j, 0, 0)),
        out_shape=jax.ShapeDtypeStruct((heads, 2 * NODE_STEPS, KEYS_HALF), jnp.bfloat16),
        compiler_params=pltpu.CompilerParams(vmem_limit_bytes=VMEM_LIMIT),
        name="mean_weights",
    )(probs, lse, far_lse)


def pool_body(first_ref, weights_ref, value_ref, out_ref):
    first = first_ref[0]
    row = lax.broadcasted_iota(jnp.int32, (2 * NODE_STEPS, HEAD_DIM), 0)
    for head in range(HEADS_STEP):
        span = slice(head * HEAD_DIM, (head + 1) * HEAD_DIM)
        pooled = [
            jnp.dot(
                weights_ref[head],
                jnp.concatenate(
                    [value_ref[first ^ venue, item, :, span] for venue in range(HALF_VENUES)], axis=0
                ),
                preferred_element_type=jnp.float32,
            )
            for item in range(2)
        ]
        out_ref[:, span] = jnp.where(row < NODE_STEPS, *pooled).astype(jnp.bfloat16)


def half_pool(first, weights, values):
    width = values.shape[3]
    return pl.pallas_call(
        pool_body,
        grid=(width // COLS_STEP,),
        in_specs=[
            pl.BlockSpec(memory_space=pltpu.SMEM),
            pl.BlockSpec((HEADS_STEP, 2 * NODE_STEPS, KEYS_HALF), lambda j: (j, 0, 0)),
            pl.BlockSpec((HALF_VENUES, 2, STEPS, COLS_STEP), lambda j: (0, 0, 0, j)),
        ],
        out_specs=pl.BlockSpec((2 * NODE_STEPS, COLS_STEP), lambda j: (0, j)),
        out_shape=jax.ShapeDtypeStruct((2 * NODE_STEPS, width), jnp.bfloat16),
        compiler_params=pltpu.CompilerParams(vmem_limit_bytes=VMEM_LIMIT),
        name="half_pool",
    )(first, weights, values)


def pad_lanes(width):
    return -(-width // 128) * 128


def stage_body(*refs, layer, count):
    first = len(refs) - count - 2
    token_ref, sems = refs[-2:]
    copies = []
    for place in range(count):
        copy = pltpu.make_async_copy(refs[place].at[layer], refs[first + place], sems.at[place])
        copy.start()
        copies.append(copy)
    token_ref[...] = jnp.zeros_like(token_ref)
    for copy in copies:
        copy.wait()


def stage_weights(weights, layer, after):
    held = [pltpu.with_memory_space_constraint(a, pltpu.HBM) for a in weights]
    shapes = [pltpu.VMEM(a.shape[1:], a.dtype) for a in weights]
    size = sum(a.size for a in weights) // ROUNDS
    out = pl.pallas_call(
        functools.partial(stage_body, layer=layer, count=len(held)),
        in_specs=[pl.BlockSpec(memory_space=pl.ANY)] * (len(held) + len(after)),
        out_specs=[pl.BlockSpec(memory_space=pltpu.VMEM)] * (len(shapes) + 1),
        out_shape=shapes + [jax.ShapeDtypeStruct((8, 128), jnp.float32)],
        scratch_shapes=[pltpu.SemaphoreType.DMA((len(held),))],
        compiler_params=pltpu.CompilerParams(vmem_limit_bytes=2 << 20),
        cost_estimate=pl.CostEstimate(flops=0, transcendentals=0, bytes_accessed=4 * size),
        name="stage_weights",
    )(*held, *after)
    return out[:-1], out[-1]


def column_tiles(width, tile):
    tile = tile if width % tile == 0 else width
    return [slice(start, start + tile) for start in range(0, width, tile)]


def expand_body(*refs, layer):
    node_refs, refs = refs[:4], refs[4:]
    mix_ref, gain_ref, norm_ref, gate_ref, up_ref, _, out_ref, scaled_ref = refs
    feat, width = gate_ref.shape
    padded = pad_lanes(width)
    rows = mix_ref.shape[1]
    kinds = [slice(kind * rows, (kind + 1) * rows) for kind in range(ETYPES)]
    edges = sum(mix_ref[kind, :].astype(jnp.float32) for kind in kinds)
    inverse = 1.0 / jnp.maximum(jnp.sum(edges, axis=1, keepdims=True), 1.0)
    squares = 0.0
    for span in column_tiles(feat, 512):
        nodes = jnp.concatenate([ref[:, span] for ref in node_refs], axis=0)
        mixed = jnp.dot(mix_ref[...], nodes, preferred_element_type=jnp.float32)
        message = sum(
            gain_ref[layer, kind : kind + 1, span] * mixed[kinds[kind]] for kind in range(ETYPES)
        )
        pre = nodes.astype(jnp.float32) + message * inverse
        squares += jnp.sum(pre * pre, axis=1, keepdims=True)
        scaled_ref[:, span] = (pre * norm_ref[layer : layer + 1, span]).astype(jnp.bfloat16)
    if padded != width:
        out_ref[...] = jnp.zeros_like(out_ref)
    for place, ref in enumerate((gate_ref, up_ref)):
        for span in column_tiles(width, 256):
            sums = jnp.dot(scaled_ref[...], ref[:, span], preferred_element_type=jnp.float32)
            start = place * padded + span.start
            out_ref[:, start : start + sums.shape[1]] = sums.astype(jnp.bfloat16)
    high = squares.astype(jnp.bfloat16).astype(jnp.float32)
    lane = lax.broadcasted_iota(jnp.int32, (squares.shape[0], 128), 1)
    parts = jnp.where(lane == 0, high, jnp.where(lane == 1, squares - high, 0.0))
    out_ref[:, 2 * padded :] = parts.astype(jnp.bfloat16)


def expand(nodes, mix, gain, norm, gate, up, token, layer):
    part, feat = nodes[0].shape
    rows = len(nodes) * part
    columns = 2 * pad_lanes(gate.shape[1]) + 128
    held = [pltpu.with_memory_space_constraint(a, pltpu.VMEM) for a in (gate, up)]
    operands = [*nodes, mix, gain, norm, *held, token]
    return pl.pallas_call(
        functools.partial(expand_body, layer=layer),
        in_specs=[pl.BlockSpec(memory_space=pltpu.VMEM)] * len(operands),
        out_specs=pl.BlockSpec(memory_space=pltpu.VMEM),
        out_shape=jax.ShapeDtypeStruct((rows, columns), jnp.bfloat16),
        scratch_shapes=[pltpu.VMEM((rows, feat), jnp.bfloat16)],
        compiler_params=pltpu.CompilerParams(vmem_limit_bytes=VMEM_LIMIT),
        name="expand",
    )(*operands)


def contract_body(near_ref, far_ref, down_ref, *out_refs, swap):
    rows = near_ref.shape[0]
    width, feat = down_ref.shape
    padded = pad_lanes(width)

    def both(span):
        far = far_ref[:, span].astype(jnp.float32)
        if swap:
            part = rows // 4
            far = jnp.concatenate(
                [far[:part], far[2 * part : 3 * part], far[part : 2 * part], far[3 * part :]], axis=0
            )
        return near_ref[:, span].astype(jnp.float32) + far

    squares = jnp.sum(both(slice(2 * padded, 2 * padded + 128)), axis=1, keepdims=True)
    scale = lax.rsqrt(squares * (1.0 / D) + 1e-05)
    hidden = []
    for span in column_tiles(width, 256):
        gate = both(span) * scale
        up = both(slice(padded + span.start, padded + span.stop)) * scale
        hidden.append((gate * (1.0 / (1.0 + jnp.exp(-gate))) * up).astype(jnp.bfloat16))
    hidden = hidden[0] if len(hidden) == 1 else jnp.concatenate(hidden, axis=1)
    part = rows // 4
    for span in column_tiles(feat, 640):
        total = jnp.dot(hidden, down_ref[:, span], preferred_element_type=jnp.float32)
        for place, ref in enumerate(out_refs):
            ref[:, span] = total[place * part : (place + 1) * part].astype(ref.dtype)


def contract(near, far, down, swap):
    shape = (near.shape[0] // 4, down.shape[1])
    held = pltpu.with_memory_space_constraint(down, pltpu.VMEM)
    return pl.pallas_call(
        functools.partial(contract_body, swap=swap),
        in_specs=[pl.BlockSpec(memory_space=pltpu.VMEM)] * 3,
        out_specs=[pl.BlockSpec(memory_space=pltpu.VMEM)] * 4,
        out_shape=[jax.ShapeDtypeStruct(shape, jnp.float32)]
        + [jax.ShapeDtypeStruct(shape, jnp.bfloat16)] * 3,
        compiler_params=pltpu.CompilerParams(vmem_limit_bytes=VMEM_LIMIT),
        name="contract",
    )(near, far, held)


def per_device(
    query_vecs,
    key_vecs,
    value_vecs,
    slot_map,
    edge_list,
    edge_types,
    type_gain,
    norm_gain,
    gate_proj,
    up_proj,
    down_proj,
):
    pairs_dev, inst_total, feat_width = query_vecs.shape
    gx_count = lax.axis_size("gx")
    ta_count = lax.axis_size("ta")
    me = lax.axis_index("gx")
    orders = bit_orders(gx_count, ta_count)
    last = len(orders[0]) - 1
    chunks = gx_count // 2
    groups = [list(range(chunks)), list(range(chunks, gx_count))]
    venue_idx = me * pairs_dev // STEPS
    slot_order = lax.dynamic_index_in_dim(slot_map, venue_idx, 0, keepdims=False)

    def picker(pairs, inst_of, places):
        shape = (places * 2 * pairs, pairs * inst_total)
        row = lax.broadcasted_iota(jnp.int32, (shape[0], inst_total), 0)
        inst = inst_of(row // (2 * pairs), row // pairs % 2)
        hit = inst == lax.broadcasted_iota(jnp.int32, (shape[0], inst_total), 1)
        slot = jnp.sum(jnp.where(hit, slot_order[None, :], 0), axis=1, keepdims=True)
        source = lax.broadcasted_iota(jnp.int32, shape, 0) % pairs * inst_total + slot
        return (source == lax.broadcasted_iota(jnp.int32, shape, 1)).astype(jnp.bfloat16)

    whole_venue = pairs_dev == STEPS
    direct = whole_venue and chunks == HALF_VENUES
    query_pairs = NODE_STEPS if whole_venue else pairs_dev
    rows = pairs_dev * inst_total
    query_vecs, key_vecs, value_vecs = (
        a.reshape(rows, feat_width) for a in (query_vecs, key_vecs, value_vecs)
    )

    def by_venue(block, venues):
        block = block.reshape(venues, -1, 2, rows // inst_total, feat_width)
        return block.transpose(0, 2, 1, 3, 4).reshape(venues, 2, -1, feat_width)

    def in_half(block):
        block = lax.all_to_all(
            block.reshape(chunks, -1, feat_width), "gx", 0, 0, axis_index_groups=groups, tiled=True
        )
        return by_venue(block, HALF_VENUES)

    def own_first(flip):
        return lambda place, item: (item ^ me // chunks) * chunks + (place ^ flip)

    pick = picker(query_pairs, lambda place, item: place ^ item * chunks, gx_count)
    (queries,) = arrange(pick, query_vecs)
    queries = lax.all_to_all(queries.reshape(gx_count, -1, feat_width), "gx", 0, 0, tiled=True)
    if not whole_venue:
        queries = by_venue(queries, VENUES)[:, :, STEPS - NODE_STEPS :]
    queries = queries.reshape(4 * ROWS_HALF, feat_width)
    (values,) = arrange(picker(pairs_dev, own_first(0), chunks), value_vecs)
    if direct:
        first = me % chunks
        pieces = arrange(picker(pairs_dev, own_first(first), chunks), key_vecs, chunks)
        keys = [pieces[0]]
        for flip in range(1, chunks):
            pairs = [(g, g ^ flip) for g in range(gx_count)]
            keys.append(lax.ppermute(pieces[flip], "gx", pairs))
        waited = keys[-7:]
        values, queries, waited = lax.optimization_barrier((values, queries, waited))
        keys[-7:] = waited
    else:
        first = me * 0
        (keys,) = arrange(picker(pairs_dev, own_first(0), chunks), key_vecs)
        keys = in_half(keys)
        keys = [keys[venue].reshape(2 * STEPS, feat_width) for venue in range(HALF_VENUES)]
    first = first[None].astype(jnp.int32)
    values = in_half(values)
    row_total = inst_total * NODE_STEPS
    row = jnp.arange(row_total)
    place = row // NODE_STEPS
    inst_at = [
        me ^ sum((place >> (last - stage) & 1) << bit for stage, bit in enumerate(order))
        for order in orders[:2]
    ]
    inst_at = jnp.where(lax.axis_index("ta") % 2 == 0, inst_at[0], inst_at[1])
    at_source = (edge_list[:, 0][:, None] == inst_at[None, :]).astype(jnp.bfloat16)
    at_target = edge_list[:, 1][:, None] == inst_at[None, :]
    same_step = row[:, None] % NODE_STEPS == row[None, :] % NODE_STEPS
    typed = at_target[None] & (edge_types[None, :] == jnp.arange(ETYPES)[:, None])[:, :, None]
    mix = jnp.einsum(
        "ter,ec->trc", typed.astype(jnp.bfloat16), at_source, preferred_element_type=jnp.float32
    )
    mix = jnp.where(same_step[None], mix, 0.0).astype(jnp.bfloat16)
    mix = mix.reshape(ETYPES * row_total, row_total)
    keys, mix, type_gain = lax.optimization_barrier((keys, mix, type_gain))
    probs, lse, packed = half_scores(queries, keys)
    far_lse = swap_stage(packed, orders, last)
    pooled = half_pool(first, mean_weights(probs, lse, far_lse), values)
    (gate, up), token = stage_weights([gate_proj, up_proj], 0, [pooled])
    pooled = join_pair(pooled, orders, last).astype(jnp.bfloat16)
    pooled, token = lax.optimization_barrier((pooled, token))
    (down,), token = stage_weights([down_proj], 0, [token])
    for layer_idx in range(ROUNDS):
        nodes = gather_rows(pooled, orders, last)
        near_sums = expand(nodes, mix, type_gain, norm_gain, gate, up, token, layer_idx)
        if ta_count == 2:
            far_sums = lax.ppermute(near_sums, "ta", [(0, 1), (1, 0)])
        else:
            far_sums = lax.psum(near_sums.astype(jnp.float32), "ta") - near_sums.astype(jnp.float32)
        held, *gives = contract(near_sums, far_sums, down, ta_count == 2)
        final = layer_idx + 1 == ROUNDS
        taken = [
            swap_stage(give, orders, *stages)
            for give, stages in zip(gives, ((1,), (0,), (0, 1)))
        ]
        if not final:
            (gate, up), token = stage_weights([gate_proj, up_proj], layer_idx + 1, gives)
            taken, token = lax.optimization_barrier((taken, token))
        for block in taken:
            held = held + block.astype(jnp.float32)
        for stage in range(2, last + 1 if final else last):
            half = held.shape[0] // 2
            held, give = held[:half], held[half:].astype(jnp.bfloat16)
            held = held + swap_stage(give, orders, stage).astype(jnp.float32)
        if not final:
            held = join_pair(held.astype(jnp.bfloat16), orders, last)
        pooled = (pooled[: held.shape[0]].astype(jnp.float32) + held).astype(jnp.bfloat16)
        if not final:
            (down,), token = stage_weights([down_proj], layer_idx + 1, [pooled, token])
    return pooled


def solution(mesh):
    placed = (
        P("gx", None, "ta"),
        P("gx", None, "ta"),
        P("gx", None, "ta"),
        P(),
        P(),
        P(),
        P(None, None, "ta"),
        P(None, "ta"),
        P(None, "ta", "gx"),
        P(None, "ta", "gx"),
        P(None, "gx", "ta"),
    )
    return jax.shard_map(
        per_device, mesh=mesh, in_specs=placed, out_specs=P("gx", "ta"), check_vma=False
    )
```

```python
import functools

import jax
import jax.numpy as jnp
from jax import lax
from jax.experimental import pallas as pl
from jax.experimental.pallas import tpu as pltpu
from jax.sharding import PartitionSpec as P

D = 5120
HEAD_DIM = 128
VENUES = 16
STEPS = 16
NODE_STEPS = 8
ROUNDS = 2
ETYPES = 3
HALF_VENUES = VENUES // 2
HEADS_STEP = 5
COLS_STEP = HEADS_STEP * HEAD_DIM
ROWS_HALF = HALF_VENUES * NODE_STEPS
KEYS_HALF = HALF_VENUES * STEPS
LSE_ITEM = 32
VMEM_LIMIT = 8 << 20


def stage_bits(count):
    return list(range(count.bit_length() - 1))


def bit_orders(gx_count, ta_count):
    plain = stage_bits(gx_count)
    if ta_count != 2:
        return [plain] * ta_count
    return [plain, [plain[1], plain[0]] + plain[2:]]


def swap_stage(block, orders, *stages):
    gx_count, ta_count = lax.axis_size("gx"), lax.axis_size("ta")
    flips = [sum(1 << order[stage] for stage in stages) for order in orders]
    pairs = [
        (g * ta_count + t, (g ^ flips[t]) * ta_count + t)
        for g in range(gx_count)
        for t in range(ta_count)
    ]
    return lax.ppermute(block, ("gx", "ta"), pairs)


def gather_rows(held, orders, last):
    for stage in reversed(range(2, last)):
        held = jnp.concatenate([held, swap_stage(held, orders, stage)], axis=0)
    return [
        held,
        swap_stage(held, orders, 1),
        swap_stage(held, orders, 0),
        swap_stage(held, orders, 0, 1),
    ]


def join_pair(mine, orders, last):
    taken = swap_stage(mine, orders, last)
    half = mine.shape[0] // 2
    taken = jnp.concatenate([taken[half:], taken[:half]], axis=0)
    return mine.astype(jnp.float32) + taken.astype(jnp.float32)


def arrange_body(pick_ref, source_ref, *out_refs):
    moved = jnp.dot(pick_ref[...], source_ref[...], preferred_element_type=jnp.float32)
    moved = moved.astype(jnp.bfloat16)
    rows = moved.shape[0] // len(out_refs)
    for place, ref in enumerate(out_refs):
        ref[...] = moved[place * rows : (place + 1) * rows]


def arrange(pick, source, pieces=1):
    rows, taken = pick.shape
    total, width = source.shape
    last = total // taken - 1
    cols = 1280 if width % 1280 == 0 else COLS_STEP
    return pl.pallas_call(
        arrange_body,
        grid=(width // cols,),
        in_specs=[
            pl.BlockSpec((rows, taken), lambda j: (0, 0)),
            pl.BlockSpec((taken, cols), lambda j: (last, j)),
        ],
        out_specs=[pl.BlockSpec((rows // pieces, cols), lambda j: (0, j))] * pieces,
        out_shape=[jax.ShapeDtypeStruct((rows // pieces, width), jnp.bfloat16)] * pieces,
        compiler_params=pltpu.CompilerParams(vmem_limit_bytes=VMEM_LIMIT),
        name="arrange",
    )(pick, source)


def score_body(query_ref, *refs):
    key_refs = refs[:HALF_VENUES]
    probs_ref, lse_ref, packed_ref = refs[HALF_VENUES:]
    step = pl.program_id(0)

    @pl.when(step == 0)
    def _():
        lse_ref[...] = jnp.zeros_like(lse_ref)

    shape = (VENUES, 2, NODE_STEPS, COLS_STEP)
    both = query_ref[...].astype(jnp.float32).reshape(shape)
    full = (2 * ROWS_HALF, KEYS_HALF)
    query_step = lax.broadcasted_iota(jnp.int32, full, 0) % NODE_STEPS + (STEPS - NODE_STEPS)
    key_step = lax.broadcasted_iota(jnp.int32, full, 1) % STEPS
    allowed = key_step <= query_step
    lane = lax.broadcasted_iota(jnp.int32, lse_ref.shape, 1)
    lse = lse_ref[...]
    for item in range(2):
        queries = both[:, item].reshape(2 * ROWS_HALF, COLS_STEP).astype(jnp.bfloat16)
        keys = jnp.concatenate(
            [ref[item * STEPS : (item + 1) * STEPS, :] for ref in key_refs], axis=0
        )
        for head in range(HEADS_STEP):
            span = slice(head * HEAD_DIM, (head + 1) * HEAD_DIM)
            scores = lax.dot_general(
                queries[:, span],
                keys[:, span],
                (((1,), (1,)), ((), ())),
                preferred_element_type=jnp.float32,
            ) * (1.0 / HEAD_DIM**0.5)
            scores = jnp.where(allowed, scores, -1e30)
            top = jnp.max(scores, axis=1, keepdims=True)
            expd = jnp.exp(scores - top)
            total = jnp.sum(expd, axis=1, keepdims=True)
            probs_ref[head, item] = (expd * (1.0 / total)).astype(jnp.bfloat16)
            column = step * HEADS_STEP + head + item * LSE_ITEM
            lse = jnp.where(lane == column, top + jnp.log(total), lse)
    lse_ref[...] = lse
    low, high = lse[:ROWS_HALF], pltpu.roll(lse[ROWS_HALF:], 2 * LSE_ITEM, 1)
    packed_ref[...] = jnp.where(lane[:ROWS_HALF] < 2 * LSE_ITEM, low, high)


def half_scores(queries, keys):
    rows, width = queries.shape
    heads = width // HEAD_DIM
    held = pltpu.with_memory_space_constraint(queries, pltpu.HBM)
    return pl.pallas_call(
        score_body,
        grid=(width // COLS_STEP,),
        in_specs=[pl.BlockSpec((rows, COLS_STEP), lambda j: (0, j))]
        + [pl.BlockSpec((2 * STEPS, COLS_STEP), lambda j: (0, j))] * HALF_VENUES,
        out_specs=[
            pl.BlockSpec((HEADS_STEP, 2, 2 * ROWS_HALF, KEYS_HALF), lambda j: (j, 0, 0, 0)),
            pl.BlockSpec((2 * ROWS_HALF, 128), lambda j: (0, 0)),
            pl.BlockSpec((ROWS_HALF, 128), lambda j: (0, 0)),
        ],
        out_shape=[
            jax.ShapeDtypeStruct((heads, 2, 2 * ROWS_HALF, KEYS_HALF), jnp.bfloat16),
            jax.ShapeDtypeStruct((2 * ROWS_HALF, 128), jnp.float32),
            jax.ShapeDtypeStruct((ROWS_HALF, 128), jnp.float32),
        ],
        compiler_params=pltpu.CompilerParams(vmem_limit_bytes=VMEM_LIMIT),
        name="half_scores",
    )(held, *keys)


def weigh_body(probs_ref, lse_ref, far_ref, weights_ref):
    step = pl.program_id(0)
    lane = lax.broadcasted_iota(jnp.int32, lse_ref.shape, 1)
    far = jnp.concatenate([far_ref[...], pltpu.roll(far_ref[...], 2 * LSE_ITEM, 1)], axis=0)
    far = jnp.where(
        lane < LSE_ITEM, pltpu.roll(far, 128 - LSE_ITEM, 1), pltpu.roll(far, LSE_ITEM, 1)
    )
    share = 1.0 / (1.0 + jnp.exp(far - lse_ref[...])) * (1.0 / VENUES)
    for head in range(HEADS_STEP):
        means = []
        for item in range(2):
            column = step * HEADS_STEP + head + item * LSE_ITEM
            factor = jnp.sum(jnp.where(lane == column, share, 0.0), axis=1, keepdims=True)
            weights = probs_ref[head, item].astype(jnp.float32) * factor
            means.append(jnp.sum(weights.reshape(VENUES, NODE_STEPS, KEYS_HALF), axis=0))
        weights_ref[head] = jnp.concatenate(means, axis=0).astype(jnp.bfloat16)


def mean_weights(probs, lse, far_lse):
    heads = probs.shape[0]
    return pl.pallas_call(
        weigh_body,
        grid=(heads // HEADS_STEP,),
        in_specs=[
            pl.BlockSpec((HEADS_STEP, 2, 2 * ROWS_HALF, KEYS_HALF), lambda j: (j, 0, 0, 0)),
            pl.BlockSpec((2 * ROWS_HALF, 128), lambda j: (0, 0)),
            pl.BlockSpec((ROWS_HALF, 128), lambda j: (0, 0)),
        ],
        out_specs=pl.BlockSpec((HEADS_STEP, 2 * NODE_STEPS, KEYS_HALF), lambda j: (j, 0, 0)),
        out_shape=jax.ShapeDtypeStruct((heads, 2 * NODE_STEPS, KEYS_HALF), jnp.bfloat16),
        compiler_params=pltpu.CompilerParams(vmem_limit_bytes=VMEM_LIMIT),
        name="mean_weights",
    )(probs, lse, far_lse)


def pool_body(first_ref, weights_ref, value_ref, out_ref):
    first = first_ref[0]
    row = lax.broadcasted_iota(jnp.int32, (2 * NODE_STEPS, HEAD_DIM), 0)
    for head in range(HEADS_STEP):
        span = slice(head * HEAD_DIM, (head + 1) * HEAD_DIM)
        pooled = [
            jnp.dot(
                weights_ref[head],
                jnp.concatenate(
                    [value_ref[first ^ venue, item, :, span] for venue in range(HALF_VENUES)], axis=0
                ),
                preferred_element_type=jnp.float32,
            )
            for item in range(2)
        ]
        out_ref[:, span] = jnp.where(row < NODE_STEPS, *pooled).astype(jnp.bfloat16)


def half_pool(first, weights, values):
    width = values.shape[3]
    return pl.pallas_call(
        pool_body,
        grid=(width // COLS_STEP,),
        in_specs=[
            pl.BlockSpec(memory_space=pltpu.SMEM),
            pl.BlockSpec((HEADS_STEP, 2 * NODE_STEPS, KEYS_HALF), lambda j: (j, 0, 0)),
            pl.BlockSpec((HALF_VENUES, 2, STEPS, COLS_STEP), lambda j: (0, 0, 0, j)),
        ],
        out_specs=pl.BlockSpec((2 * NODE_STEPS, COLS_STEP), lambda j: (0, j)),
        out_shape=jax.ShapeDtypeStruct((2 * NODE_STEPS, width), jnp.bfloat16),
        compiler_params=pltpu.CompilerParams(vmem_limit_bytes=VMEM_LIMIT),
        name="half_pool",
    )(first, weights, values)


def pad_lanes(width):
    return -(-width // 128) * 128


def stage_body(*refs, layer, count):
    first = len(refs) - count - 2
    token_ref, sems = refs[-2:]
    copies = []
    for place in range(count):
        copy = pltpu.make_async_copy(refs[place].at[layer], refs[first + place], sems.at[place])
        copy.start()
        copies.append(copy)
    token_ref[...] = jnp.zeros_like(token_ref)
    for copy in copies:
        copy.wait()


def stage_weights(weights, layer, after):
    held = [pltpu.with_memory_space_constraint(a, pltpu.HBM) for a in weights]
    shapes = [pltpu.VMEM(a.shape[1:], a.dtype) for a in weights]
    size = sum(a.size for a in weights) // ROUNDS
    out = pl.pallas_call(
        functools.partial(stage_body, layer=layer, count=len(held)),
        in_specs=[pl.BlockSpec(memory_space=pl.ANY)] * (len(held) + len(after)),
        out_specs=[pl.BlockSpec(memory_space=pltpu.VMEM)] * (len(shapes) + 1),
        out_shape=shapes + [jax.ShapeDtypeStruct((8, 128), jnp.float32)],
        scratch_shapes=[pltpu.SemaphoreType.DMA((len(held),))],
        compiler_params=pltpu.CompilerParams(vmem_limit_bytes=2 << 20),
        cost_estimate=pl.CostEstimate(flops=0, transcendentals=0, bytes_accessed=4 * size),
        name="stage_weights",
    )(*held, *after)
    return out[:-1], out[-1]


def column_tiles(width, tile):
    tile = tile if width % tile == 0 else width
    return [slice(start, start + tile) for start in range(0, width, tile)]


def expand_body(*refs, layer):
    node_refs, refs = refs[:4], refs[4:]
    mix_ref, gain_ref, norm_ref, gate_ref, up_ref, _, out_ref, scaled_ref = refs
    feat, width = gate_ref.shape
    padded = pad_lanes(width)
    rows = mix_ref.shape[1]
    kinds = [slice(kind * rows, (kind + 1) * rows) for kind in range(ETYPES)]
    edges = sum(mix_ref[kind, :].astype(jnp.float32) for kind in kinds)
    inverse = 1.0 / jnp.maximum(jnp.sum(edges, axis=1, keepdims=True), 1.0)
    squares = 0.0
    for span in column_tiles(feat, 512):
        nodes = jnp.concatenate([ref[:, span] for ref in node_refs], axis=0)
        mixed = jnp.dot(mix_ref[...], nodes, preferred_element_type=jnp.float32)
        message = sum(
            gain_ref[layer, kind : kind + 1, span] * mixed[kinds[kind]] for kind in range(ETYPES)
        )
        pre = nodes.astype(jnp.float32) + message * inverse
        squares += jnp.sum(pre * pre, axis=1, keepdims=True)
        scaled_ref[:, span] = (pre * norm_ref[layer : layer + 1, span]).astype(jnp.bfloat16)
    if padded != width:
        out_ref[...] = jnp.zeros_like(out_ref)
    for place, ref in enumerate((gate_ref, up_ref)):
        for span in column_tiles(width, 256):
            sums = jnp.dot(scaled_ref[...], ref[:, span], preferred_element_type=jnp.float32)
            start = place * padded + span.start
            out_ref[:, start : start + sums.shape[1]] = sums.astype(jnp.bfloat16)
    high = squares.astype(jnp.bfloat16).astype(jnp.float32)
    lane = lax.broadcasted_iota(jnp.int32, (squares.shape[0], 128), 1)
    parts = jnp.where(lane == 0, high, jnp.where(lane == 1, squares - high, 0.0))
    out_ref[:, 2 * padded :] = parts.astype(jnp.bfloat16)


def expand(nodes, mix, gain, norm, gate, up, token, layer):
    part, feat = nodes[0].shape
    rows = len(nodes) * part
    columns = 2 * pad_lanes(gate.shape[1]) + 128
    held = [pltpu.with_memory_space_constraint(a, pltpu.VMEM) for a in (gate, up)]
    operands = [*nodes, mix, gain, norm, *held, token]
    return pl.pallas_call(
        functools.partial(expand_body, layer=layer),
        in_specs=[pl.BlockSpec(memory_space=pltpu.VMEM)] * len(operands),
        out_specs=pl.BlockSpec(memory_space=pltpu.VMEM),
        out_shape=jax.ShapeDtypeStruct((rows, columns), jnp.bfloat16),
        scratch_shapes=[pltpu.VMEM((rows, feat), jnp.bfloat16)],
        compiler_params=pltpu.CompilerParams(vmem_limit_bytes=VMEM_LIMIT),
        name="expand",
    )(*operands)


def contract_body(near_ref, far_ref, down_ref, *out_refs, swap):
    rows = near_ref.shape[0]
    width, feat = down_ref.shape
    padded = pad_lanes(width)

    def both(span):
        far = far_ref[:, span].astype(jnp.float32)
        if swap:
            part = rows // 4
            far = jnp.concatenate(
                [far[:part], far[2 * part : 3 * part], far[part : 2 * part], far[3 * part :]], axis=0
            )
        return near_ref[:, span].astype(jnp.float32) + far

    squares = jnp.sum(both(slice(2 * padded, 2 * padded + 128)), axis=1, keepdims=True)
    scale = lax.rsqrt(squares * (1.0 / D) + 1e-05)
    hidden = []
    for span in column_tiles(width, 256):
        gate = both(span) * scale
        up = both(slice(padded + span.start, padded + span.stop)) * scale
        hidden.append((gate * (1.0 / (1.0 + jnp.exp(-gate))) * up).astype(jnp.bfloat16))
    hidden = hidden[0] if len(hidden) == 1 else jnp.concatenate(hidden, axis=1)
    part = rows // len(out_refs)
    for span in column_tiles(feat, 640):
        total = jnp.dot(hidden, down_ref[:, span], preferred_element_type=jnp.float32)
        for place, ref in enumerate(out_refs):
            ref[:, span] = total[place * part : (place + 1) * part].astype(ref.dtype)


def contract(near, far, down, swap):
    shape = (near.shape[0] // 8, down.shape[1])
    held = pltpu.with_memory_space_constraint(down, pltpu.VMEM)
    return pl.pallas_call(
        functools.partial(contract_body, swap=swap),
        in_specs=[pl.BlockSpec(memory_space=pltpu.VMEM)] * 3,
        out_specs=[pl.BlockSpec(memory_space=pltpu.VMEM)] * 8,
        out_shape=[jax.ShapeDtypeStruct(shape, jnp.float32)]
        + [jax.ShapeDtypeStruct(shape, jnp.bfloat16)] * 7,
        compiler_params=pltpu.CompilerParams(vmem_limit_bytes=VMEM_LIMIT),
        name="contract",
    )(near, far, held)


def per_device(
    query_vecs,
    key_vecs,
    value_vecs,
    slot_map,
    edge_list,
    edge_types,
    type_gain,
    norm_gain,
    gate_proj,
    up_proj,
    down_proj,
):
    pairs_dev, inst_total, feat_width = query_vecs.shape
    gx_count = lax.axis_size("gx")
    ta_count = lax.axis_size("ta")
    me = lax.axis_index("gx")
    orders = bit_orders(gx_count, ta_count)
    last = len(orders[0]) - 1
    chunks = gx_count // 2
    groups = [list(range(chunks)), list(range(chunks, gx_count))]
    venue_idx = me * pairs_dev // STEPS
    slot_order = lax.dynamic_index_in_dim(slot_map, venue_idx, 0, keepdims=False)

    def picker(pairs, inst_of, places):
        shape = (places * 2 * pairs, pairs * inst_total)
        row = lax.broadcasted_iota(jnp.int32, (shape[0], inst_total), 0)
        inst = inst_of(row // (2 * pairs), row // pairs % 2)
        hit = inst == lax.broadcasted_iota(jnp.int32, (shape[0], inst_total), 1)
        slot = jnp.sum(jnp.where(hit, slot_order[None, :], 0), axis=1, keepdims=True)
        source = lax.broadcasted_iota(jnp.int32, shape, 0) % pairs * inst_total + slot
        return (source == lax.broadcasted_iota(jnp.int32, shape, 1)).astype(jnp.bfloat16)

    whole_venue = pairs_dev == STEPS
    direct = whole_venue and chunks == HALF_VENUES
    query_pairs = NODE_STEPS if whole_venue else pairs_dev
    rows = pairs_dev * inst_total
    query_vecs, key_vecs, value_vecs = (
        a.reshape(rows, feat_width) for a in (query_vecs, key_vecs, value_vecs)
    )

    def by_venue(block, venues):
        block = block.reshape(venues, -1, 2, rows // inst_total, feat_width)
        return block.transpose(0, 2, 1, 3, 4).reshape(venues, 2, -1, feat_width)

    def in_half(block):
        block = lax.all_to_all(
            block.reshape(chunks, -1, feat_width), "gx", 0, 0, axis_index_groups=groups, tiled=True
        )
        return by_venue(block, HALF_VENUES)

    def own_first(flip):
        return lambda place, item: (item ^ me // chunks) * chunks + (place ^ flip)

    pick = picker(query_pairs, lambda place, item: place ^ item * chunks, gx_count)
    (queries,) = arrange(pick, query_vecs)
    queries = lax.all_to_all(queries.reshape(gx_count, -1, feat_width), "gx", 0, 0, tiled=True)
    if not whole_venue:
        queries = by_venue(queries, VENUES)[:, :, STEPS - NODE_STEPS :]
    queries = queries.reshape(4 * ROWS_HALF, feat_width)
    (values,) = arrange(picker(pairs_dev, own_first(0), chunks), value_vecs)
    if direct:
        first = me % chunks
        pieces = arrange(picker(pairs_dev, own_first(first), chunks), key_vecs, chunks)
        keys = [pieces[0]]
        for flip in range(1, chunks):
            pairs = [(g, g ^ flip) for g in range(gx_count)]
            keys.append(lax.ppermute(pieces[flip], "gx", pairs))
        waited = keys[-7:]
        values, queries, waited = lax.optimization_barrier((values, queries, waited))
        keys[-7:] = waited
    else:
        first = me * 0
        (keys,) = arrange(picker(pairs_dev, own_first(0), chunks), key_vecs)
        keys = in_half(keys)
        keys = [keys[venue].reshape(2 * STEPS, feat_width) for venue in range(HALF_VENUES)]
    first = first[None].astype(jnp.int32)
    values = in_half(values)
    row_total = inst_total * NODE_STEPS
    row = jnp.arange(row_total)
    place = row // NODE_STEPS
    inst_at = [
        me ^ sum((place >> (last - stage) & 1) << bit for stage, bit in enumerate(order))
        for order in orders[:2]
    ]
    inst_at = jnp.where(lax.axis_index("ta") % 2 == 0, inst_at[0], inst_at[1])
    at_source = (edge_list[:, 0][:, None] == inst_at[None, :]).astype(jnp.bfloat16)
    at_target = edge_list[:, 1][:, None] == inst_at[None, :]
    same_step = row[:, None] % NODE_STEPS == row[None, :] % NODE_STEPS
    typed = at_target[None] & (edge_types[None, :] == jnp.arange(ETYPES)[:, None])[:, :, None]
    mix = jnp.einsum(
        "ter,ec->trc", typed.astype(jnp.bfloat16), at_source, preferred_element_type=jnp.float32
    )
    mix = jnp.where(same_step[None], mix, 0.0).astype(jnp.bfloat16)
    mix = mix.reshape(ETYPES * row_total, row_total)
    keys, mix, type_gain = lax.optimization_barrier((keys, mix, type_gain))
    probs, lse, packed = half_scores(queries, keys)
    far_lse = swap_stage(packed, orders, last)
    pooled = half_pool(first, mean_weights(probs, lse, far_lse), values)
    (gate, up), token = stage_weights([gate_proj, up_proj], 0, [pooled])
    pooled = join_pair(pooled, orders, last).astype(jnp.bfloat16)
    pooled, token = lax.optimization_barrier((pooled, token))
    (down,), token = stage_weights([down_proj], 0, [token])
    for layer_idx in range(ROUNDS):
        nodes = gather_rows(pooled, orders, last)
        near_sums = expand(nodes, mix, type_gain, norm_gain, gate, up, token, layer_idx)
        if ta_count == 2:
            far_sums = lax.ppermute(near_sums, "ta", [(0, 1), (1, 0)])
        else:
            far_sums = lax.psum(near_sums.astype(jnp.float32), "ta") - near_sums.astype(jnp.float32)
        held, *gives = contract(near_sums, far_sums, down, ta_count == 2)
        final = layer_idx + 1 == ROUNDS
        taken = [
            swap_stage(give, orders, *[stage for stage in range(3) if place >> (2 - stage) & 1])
            for place, give in enumerate(gives, 1)
        ]
        if not final:
            (gate,), token = stage_weights([gate_proj], layer_idx + 1, gives)
            taken, token = lax.optimization_barrier((taken, token))
        for block in taken:
            held = held + block.astype(jnp.float32)
        for stage in range(3, last + 1 if final else last):
            half = held.shape[0] // 2
            held, give = held[:half], held[half:].astype(jnp.bfloat16)
            held = held + swap_stage(give, orders, stage).astype(jnp.float32)
        if not final:
            held = join_pair(held.astype(jnp.bfloat16), orders, last)
        pooled = (pooled[: held.shape[0]].astype(jnp.float32) + held).astype(jnp.bfloat16)
        if not final:
            (up, down), token = stage_weights([up_proj, down_proj], layer_idx + 1, [pooled, token])
    return pooled


def solution(mesh):
    placed = (
        P("gx", None, "ta"),
        P("gx", None, "ta"),
        P("gx", None, "ta"),
        P(),
        P(),
        P(),
        P(None, None, "ta"),
        P(None, "ta"),
        P(None, "ta", "gx"),
        P(None, "ta", "gx"),
        P(None, "gx", "ta"),
    )
    return jax.shard_map(
        per_device, mesh=mesh, in_specs=placed, out_specs=P("gx", "ta"), check_vma=False
    )
```

```python
import functools

import jax
import jax.numpy as jnp
from jax import lax
from jax.experimental import pallas as pl
from jax.experimental.pallas import tpu as pltpu
from jax.sharding import PartitionSpec as P

D = 5120
HEAD_DIM = 128
VENUES = 16
STEPS = 16
NODE_STEPS = 8
ROUNDS = 2
ETYPES = 3
HALF_VENUES = VENUES // 2
HEADS_STEP = 5
COLS_STEP = HEADS_STEP * HEAD_DIM
ROWS_HALF = HALF_VENUES * NODE_STEPS
KEYS_HALF = HALF_VENUES * STEPS
LSE_ITEM = 32
VMEM_LIMIT = 8 << 20


def stage_bits(count):
    return list(range(count.bit_length() - 1))


def bit_orders(gx_count, ta_count):
    plain = stage_bits(gx_count)
    if ta_count != 2:
        return [plain] * ta_count
    return [plain, [plain[1], plain[0]] + plain[2:]]


def swap_stage(block, orders, *stages):
    gx_count, ta_count = lax.axis_size("gx"), lax.axis_size("ta")
    flips = [sum(1 << order[stage] for stage in stages) for order in orders]
    pairs = [
        (g * ta_count + t, (g ^ flips[t]) * ta_count + t)
        for g in range(gx_count)
        for t in range(ta_count)
    ]
    return lax.ppermute(block, ("gx", "ta"), pairs)


def gather_rows(held, orders, last):
    for stage in reversed(range(2, last)):
        held = jnp.concatenate([held, swap_stage(held, orders, stage)], axis=0)
    return [
        held,
        swap_stage(held, orders, 1),
        swap_stage(held, orders, 0),
        swap_stage(held, orders, 0, 1),
    ]


def join_pair(mine, orders, last):
    taken = swap_stage(mine, orders, last)
    half = mine.shape[0] // 2
    taken = jnp.concatenate([taken[half:], taken[:half]], axis=0)
    return mine.astype(jnp.float32) + taken.astype(jnp.float32)


def arrange_body(pick_ref, source_ref, *out_refs):
    moved = jnp.dot(pick_ref[...], source_ref[...], preferred_element_type=jnp.float32)
    moved = moved.astype(jnp.bfloat16)
    rows = moved.shape[0] // len(out_refs)
    for place, ref in enumerate(out_refs):
        ref[...] = moved[place * rows : (place + 1) * rows]


def arrange(pick, source, pieces=1):
    rows, taken = pick.shape
    total, width = source.shape
    last = total // taken - 1
    cols = 1280 if width % 1280 == 0 else COLS_STEP
    return pl.pallas_call(
        arrange_body,
        grid=(width // cols,),
        in_specs=[
            pl.BlockSpec((rows, taken), lambda j: (0, 0)),
            pl.BlockSpec((taken, cols), lambda j: (last, j)),
        ],
        out_specs=[pl.BlockSpec((rows // pieces, cols), lambda j: (0, j))] * pieces,
        out_shape=[jax.ShapeDtypeStruct((rows // pieces, width), jnp.bfloat16)] * pieces,
        compiler_params=pltpu.CompilerParams(vmem_limit_bytes=VMEM_LIMIT),
        name="arrange",
    )(pick, source)


def score_body(query_ref, *refs):
    key_refs = refs[:HALF_VENUES]
    probs_ref, lse_ref, packed_ref = refs[HALF_VENUES:]
    step = pl.program_id(0)

    @pl.when(step == 0)
    def _():
        lse_ref[...] = jnp.zeros_like(lse_ref)

    shape = (VENUES, 2, NODE_STEPS, COLS_STEP)
    both = query_ref[...].astype(jnp.float32).reshape(shape)
    full = (2 * ROWS_HALF, KEYS_HALF)
    query_step = lax.broadcasted_iota(jnp.int32, full, 0) % NODE_STEPS + (STEPS - NODE_STEPS)
    key_step = lax.broadcasted_iota(jnp.int32, full, 1) % STEPS
    allowed = key_step <= query_step
    lane = lax.broadcasted_iota(jnp.int32, lse_ref.shape, 1)
    lse = lse_ref[...]
    for item in range(2):
        queries = both[:, item].reshape(2 * ROWS_HALF, COLS_STEP).astype(jnp.bfloat16)
        keys = jnp.concatenate(
            [ref[item * STEPS : (item + 1) * STEPS, :] for ref in key_refs], axis=0
        )
        for head in range(HEADS_STEP):
            span = slice(head * HEAD_DIM, (head + 1) * HEAD_DIM)
            scores = lax.dot_general(
                queries[:, span],
                keys[:, span],
                (((1,), (1,)), ((), ())),
                preferred_element_type=jnp.float32,
            ) * (1.0 / HEAD_DIM**0.5)
            scores = jnp.where(allowed, scores, -1e30)
            top = jnp.max(scores, axis=1, keepdims=True)
            expd = jnp.exp(scores - top)
            total = jnp.sum(expd, axis=1, keepdims=True)
            probs_ref[head, item] = (expd * (1.0 / total)).astype(jnp.bfloat16)
            column = step * HEADS_STEP + head + item * LSE_ITEM
            lse = jnp.where(lane == column, top + jnp.log(total), lse)
    lse_ref[...] = lse
    low, high = lse[:ROWS_HALF], pltpu.roll(lse[ROWS_HALF:], 2 * LSE_ITEM, 1)
    packed_ref[...] = jnp.where(lane[:ROWS_HALF] < 2 * LSE_ITEM, low, high)


def half_scores(queries, keys):
    rows, width = queries.shape
    heads = width // HEAD_DIM
    held = pltpu.with_memory_space_constraint(queries, pltpu.HBM)
    return pl.pallas_call(
        score_body,
        grid=(width // COLS_STEP,),
        in_specs=[pl.BlockSpec((rows, COLS_STEP), lambda j: (0, j))]
        + [pl.BlockSpec((2 * STEPS, COLS_STEP), lambda j: (0, j))] * HALF_VENUES,
        out_specs=[
            pl.BlockSpec((HEADS_STEP, 2, 2 * ROWS_HALF, KEYS_HALF), lambda j: (j, 0, 0, 0)),
            pl.BlockSpec((2 * ROWS_HALF, 128), lambda j: (0, 0)),
            pl.BlockSpec((ROWS_HALF, 128), lambda j: (0, 0)),
        ],
        out_shape=[
            jax.ShapeDtypeStruct((heads, 2, 2 * ROWS_HALF, KEYS_HALF), jnp.bfloat16),
            jax.ShapeDtypeStruct((2 * ROWS_HALF, 128), jnp.float32),
            jax.ShapeDtypeStruct((ROWS_HALF, 128), jnp.float32),
        ],
        compiler_params=pltpu.CompilerParams(vmem_limit_bytes=VMEM_LIMIT),
        name="half_scores",
    )(held, *keys)


def heads_held(heads):
    return 2 * HEADS_STEP if heads % (2 * HEADS_STEP) == 0 else HEADS_STEP


def weigh_body(probs_ref, lse_ref, far_ref, weights_ref):
    step = pl.program_id(0)
    lane = lax.broadcasted_iota(jnp.int32, lse_ref.shape, 1)
    far = jnp.concatenate([far_ref[...], pltpu.roll(far_ref[...], 2 * LSE_ITEM, 1)], axis=0)
    far = jnp.where(
        lane < LSE_ITEM, pltpu.roll(far, 128 - LSE_ITEM, 1), pltpu.roll(far, LSE_ITEM, 1)
    )
    share = 1.0 / (1.0 + jnp.exp(far - lse_ref[...])) * (1.0 / VENUES)
    held = probs_ref.shape[0]
    for head in range(held):
        means = []
        for item in range(2):
            column = step * held + head + item * LSE_ITEM
            factor = jnp.sum(jnp.where(lane == column, share, 0.0), axis=1, keepdims=True)
            weights = probs_ref[head, item].astype(jnp.float32) * factor
            means.append(jnp.sum(weights.reshape(VENUES, NODE_STEPS, KEYS_HALF), axis=0))
        weights_ref[head] = jnp.concatenate(means, axis=0).astype(jnp.bfloat16)


def mean_weights(probs, lse, far_lse):
    heads = probs.shape[0]
    held = heads_held(heads)
    return pl.pallas_call(
        weigh_body,
        grid=(heads // held,),
        in_specs=[
            pl.BlockSpec((held, 2, 2 * ROWS_HALF, KEYS_HALF), lambda j: (j, 0, 0, 0)),
            pl.BlockSpec((2 * ROWS_HALF, 128), lambda j: (0, 0)),
            pl.BlockSpec((ROWS_HALF, 128), lambda j: (0, 0)),
        ],
        out_specs=pl.BlockSpec((held, 2 * NODE_STEPS, KEYS_HALF), lambda j: (j, 0, 0)),
        out_shape=jax.ShapeDtypeStruct((heads, 2 * NODE_STEPS, KEYS_HALF), jnp.bfloat16),
        compiler_params=pltpu.CompilerParams(vmem_limit_bytes=VMEM_LIMIT),
        name="mean_weights",
    )(probs, lse, far_lse)


def pool_body(first_ref, weights_ref, value_ref, out_ref):
    first = first_ref[0]
    row = lax.broadcasted_iota(jnp.int32, (2 * NODE_STEPS, HEAD_DIM), 0)
    for head in range(weights_ref.shape[0]):
        span = slice(head * HEAD_DIM, (head + 1) * HEAD_DIM)
        pooled = [
            jnp.dot(
                weights_ref[head],
                jnp.concatenate(
                    [value_ref[first ^ venue, item, :, span] for venue in range(HALF_VENUES)], axis=0
                ),
                preferred_element_type=jnp.float32,
            )
            for item in range(2)
        ]
        out_ref[:, span] = jnp.where(row < NODE_STEPS, *pooled).astype(jnp.bfloat16)


def half_pool(first, weights, values):
    width = values.shape[3]
    held = heads_held(width // HEAD_DIM)
    cols = held * HEAD_DIM
    return pl.pallas_call(
        pool_body,
        grid=(width // cols,),
        in_specs=[
            pl.BlockSpec(memory_space=pltpu.SMEM),
            pl.BlockSpec((held, 2 * NODE_STEPS, KEYS_HALF), lambda j: (j, 0, 0)),
            pl.BlockSpec((HALF_VENUES, 2, STEPS, cols), lambda j: (0, 0, 0, j)),
        ],
        out_specs=pl.BlockSpec((2 * NODE_STEPS, cols), lambda j: (0, j)),
        out_shape=jax.ShapeDtypeStruct((2 * NODE_STEPS, width), jnp.bfloat16),
        compiler_params=pltpu.CompilerParams(vmem_limit_bytes=VMEM_LIMIT),
        name="half_pool",
    )(first, weights, values)


def pad_lanes(width):
    return -(-width // 128) * 128


def stage_body(*refs, layer, count):
    first = len(refs) - count - 2
    token_ref, sems = refs[-2:]
    copies = []
    for place in range(count):
        copy = pltpu.make_async_copy(refs[place].at[layer], refs[first + place], sems.at[place])
        copy.start()
        copies.append(copy)
    token_ref[...] = jnp.zeros_like(token_ref)
    for copy in copies:
        copy.wait()


def stage_weights(weights, layer, after):
    held = [pltpu.with_memory_space_constraint(a, pltpu.HBM) for a in weights]
    shapes = [pltpu.VMEM(a.shape[1:], a.dtype) for a in weights]
    size = sum(a.size for a in weights) // ROUNDS
    out = pl.pallas_call(
        functools.partial(stage_body, layer=layer, count=len(held)),
        in_specs=[pl.BlockSpec(memory_space=pl.ANY)] * (len(held) + len(after)),
        out_specs=[pl.BlockSpec(memory_space=pltpu.VMEM)] * (len(shapes) + 1),
        out_shape=shapes + [jax.ShapeDtypeStruct((8, 128), jnp.float32)],
        scratch_shapes=[pltpu.SemaphoreType.DMA((len(held),))],
        compiler_params=pltpu.CompilerParams(vmem_limit_bytes=2 << 20),
        cost_estimate=pl.CostEstimate(flops=0, transcendentals=0, bytes_accessed=4 * size),
        name="stage_weights",
    )(*held, *after)
    return out[:-1], out[-1]


def column_tiles(width, tile):
    tile = tile if width % tile == 0 else width
    return [slice(start, start + tile) for start in range(0, width, tile)]


def expand_body(*refs, layer):
    node_refs, refs = refs[:4], refs[4:]
    mix_ref, gain_ref, norm_ref, gate_ref, up_ref, _, out_ref, scaled_ref = refs
    feat, width = gate_ref.shape
    padded = pad_lanes(width)
    rows = mix_ref.shape[1]
    kinds = [slice(kind * rows, (kind + 1) * rows) for kind in range(ETYPES)]
    edges = sum(mix_ref[kind, :].astype(jnp.float32) for kind in kinds)
    inverse = 1.0 / jnp.maximum(jnp.sum(edges, axis=1, keepdims=True), 1.0)
    squares = 0.0
    for span in column_tiles(feat, 512):
        nodes = jnp.concatenate([ref[:, span] for ref in node_refs], axis=0)
        mixed = jnp.dot(mix_ref[...], nodes, preferred_element_type=jnp.float32)
        message = sum(
            gain_ref[layer, kind : kind + 1, span] * mixed[kinds[kind]] for kind in range(ETYPES)
        )
        pre = nodes.astype(jnp.float32) + message * inverse
        squares += jnp.sum(pre * pre, axis=1, keepdims=True)
        scaled_ref[:, span] = (pre * norm_ref[layer : layer + 1, span]).astype(jnp.bfloat16)
    if padded != width:
        out_ref[...] = jnp.zeros_like(out_ref)
    for place, ref in enumerate((gate_ref, up_ref)):
        for span in column_tiles(width, 256):
            sums = jnp.dot(scaled_ref[...], ref[:, span], preferred_element_type=jnp.float32)
            start = place * padded + span.start
            out_ref[:, start : start + sums.shape[1]] = sums.astype(jnp.bfloat16)
    high = squares.astype(jnp.bfloat16).astype(jnp.float32)
    lane = lax.broadcasted_iota(jnp.int32, (squares.shape[0], 128), 1)
    parts = jnp.where(lane == 0, high, jnp.where(lane == 1, squares - high, 0.0))
    out_ref[:, 2 * padded :] = parts.astype(jnp.bfloat16)


def expand(nodes, mix, gain, norm, gate, up, token, layer):
    part, feat = nodes[0].shape
    rows = len(nodes) * part
    columns = 2 * pad_lanes(gate.shape[1]) + 128
    held = [pltpu.with_memory_space_constraint(a, pltpu.VMEM) for a in (gate, up)]
    operands = [*nodes, mix, gain, norm, *held, token]
    return pl.pallas_call(
        functools.partial(expand_body, layer=layer),
        in_specs=[pl.BlockSpec(memory_space=pltpu.VMEM)] * len(operands),
        out_specs=pl.BlockSpec(memory_space=pltpu.VMEM),
        out_shape=jax.ShapeDtypeStruct((rows, columns), jnp.bfloat16),
        scratch_shapes=[pltpu.VMEM((rows, feat), jnp.bfloat16)],
        compiler_params=pltpu.CompilerParams(vmem_limit_bytes=VMEM_LIMIT),
        name="expand",
    )(*operands)


def contract_body(near_ref, far_ref, down_ref, *out_refs, swap):
    rows = near_ref.shape[0]
    width, feat = down_ref.shape
    padded = pad_lanes(width)

    def both(span):
        far = far_ref[:, span].astype(jnp.float32)
        if swap:
            part = rows // 4
            far = jnp.concatenate(
                [far[:part], far[2 * part : 3 * part], far[part : 2 * part], far[3 * part :]], axis=0
            )
        return near_ref[:, span].astype(jnp.float32) + far

    squares = jnp.sum(both(slice(2 * padded, 2 * padded + 128)), axis=1, keepdims=True)
    scale = lax.rsqrt(squares * (1.0 / D) + 1e-05)
    hidden = []
    for span in column_tiles(width, 256):
        gate = both(span) * scale
        up = both(slice(padded + span.start, padded + span.stop)) * scale
        hidden.append((gate * (1.0 / (1.0 + jnp.exp(-gate))) * up).astype(jnp.bfloat16))
    hidden = hidden[0] if len(hidden) == 1 else jnp.concatenate(hidden, axis=1)
    part = rows // len(out_refs)
    for span in column_tiles(feat, 640):
        total = jnp.dot(hidden, down_ref[:, span], preferred_element_type=jnp.float32)
        for place, ref in enumerate(out_refs):
            ref[:, span] = total[place * part : (place + 1) * part].astype(ref.dtype)


def contract(near, far, down, swap):
    shape = (near.shape[0] // 8, down.shape[1])
    held = pltpu.with_memory_space_constraint(down, pltpu.VMEM)
    return pl.pallas_call(
        functools.partial(contract_body, swap=swap),
        in_specs=[pl.BlockSpec(memory_space=pltpu.VMEM)] * 3,
        out_specs=[pl.BlockSpec(memory_space=pltpu.VMEM)] * 8,
        out_shape=[jax.ShapeDtypeStruct(shape, jnp.float32)]
        + [jax.ShapeDtypeStruct(shape, jnp.bfloat16)] * 7,
        compiler_params=pltpu.CompilerParams(vmem_limit_bytes=VMEM_LIMIT),
        name="contract",
    )(near, far, held)


def per_device(
    query_vecs,
    key_vecs,
    value_vecs,
    slot_map,
    edge_list,
    edge_types,
    type_gain,
    norm_gain,
    gate_proj,
    up_proj,
    down_proj,
):
    pairs_dev, inst_total, feat_width = query_vecs.shape
    gx_count = lax.axis_size("gx")
    ta_count = lax.axis_size("ta")
    me = lax.axis_index("gx")
    orders = bit_orders(gx_count, ta_count)
    last = len(orders[0]) - 1
    chunks = gx_count // 2
    groups = [list(range(chunks)), list(range(chunks, gx_count))]
    venue_idx = me * pairs_dev // STEPS
    slot_order = lax.dynamic_index_in_dim(slot_map, venue_idx, 0, keepdims=False)

    def picker(pairs, inst_of, places):
        shape = (places * 2 * pairs, pairs * inst_total)
        row = lax.broadcasted_iota(jnp.int32, (shape[0], inst_total), 0)
        inst = inst_of(row // (2 * pairs), row // pairs % 2)
        hit = inst == lax.broadcasted_iota(jnp.int32, (shape[0], inst_total), 1)
        slot = jnp.sum(jnp.where(hit, slot_order[None, :], 0), axis=1, keepdims=True)
        source = lax.broadcasted_iota(jnp.int32, shape, 0) % pairs * inst_total + slot
        return (source == lax.broadcasted_iota(jnp.int32, shape, 1)).astype(jnp.bfloat16)

    whole_venue = pairs_dev == STEPS
    direct = whole_venue and chunks == HALF_VENUES
    query_pairs = NODE_STEPS if whole_venue else pairs_dev
    rows = pairs_dev * inst_total
    query_vecs, key_vecs, value_vecs = (
        a.reshape(rows, feat_width) for a in (query_vecs, key_vecs, value_vecs)
    )

    def by_venue(block, venues):
        block = block.reshape(venues, -1, 2, rows // inst_total, feat_width)
        return block.transpose(0, 2, 1, 3, 4).reshape(venues, 2, -1, feat_width)

    def in_half(block):
        block = lax.all_to_all(
            block.reshape(chunks, -1, feat_width), "gx", 0, 0, axis_index_groups=groups, tiled=True
        )
        return by_venue(block, HALF_VENUES)

    def own_first(flip):
        return lambda place, item: (item ^ me // chunks) * chunks + (place ^ flip)

    pick = picker(query_pairs, lambda place, item: place ^ item * chunks, gx_count)
    (queries,) = arrange(pick, query_vecs)
    queries = lax.all_to_all(queries.reshape(gx_count, -1, feat_width), "gx", 0, 0, tiled=True)
    if not whole_venue:
        queries = by_venue(queries, VENUES)[:, :, STEPS - NODE_STEPS :]
    queries = queries.reshape(4 * ROWS_HALF, feat_width)
    (values,) = arrange(picker(pairs_dev, own_first(0), chunks), value_vecs)
    if direct:
        first = me % chunks
        pieces = arrange(picker(pairs_dev, own_first(first), chunks), key_vecs, chunks)
        keys = [pieces[0]]
        for flip in range(1, chunks):
            pairs = [(g, g ^ flip) for g in range(gx_count)]
            keys.append(lax.ppermute(pieces[flip], "gx", pairs))
        waited = keys[-7:]
        values, queries, waited = lax.optimization_barrier((values, queries, waited))
        keys[-7:] = waited
    else:
        first = me * 0
        (keys,) = arrange(picker(pairs_dev, own_first(0), chunks), key_vecs)
        keys = in_half(keys)
        keys = [keys[venue].reshape(2 * STEPS, feat_width) for venue in range(HALF_VENUES)]
    first = first[None].astype(jnp.int32)
    values = in_half(values)
    row_total = inst_total * NODE_STEPS
    row = jnp.arange(row_total)
    place = row // NODE_STEPS
    inst_at = [
        me ^ sum((place >> (last - stage) & 1) << bit for stage, bit in enumerate(order))
        for order in orders[:2]
    ]
    inst_at = jnp.where(lax.axis_index("ta") % 2 == 0, inst_at[0], inst_at[1])
    at_source = (edge_list[:, 0][:, None] == inst_at[None, :]).astype(jnp.bfloat16)
    at_target = edge_list[:, 1][:, None] == inst_at[None, :]
    same_step = row[:, None] % NODE_STEPS == row[None, :] % NODE_STEPS
    typed = at_target[None] & (edge_types[None, :] == jnp.arange(ETYPES)[:, None])[:, :, None]
    mix = jnp.einsum(
        "ter,ec->trc", typed.astype(jnp.bfloat16), at_source, preferred_element_type=jnp.float32
    )
    mix = jnp.where(same_step[None], mix, 0.0).astype(jnp.bfloat16)
    mix = mix.reshape(ETYPES * row_total, row_total)
    keys, mix, type_gain = lax.optimization_barrier((keys, mix, type_gain))
    probs, lse, packed = half_scores(queries, keys)
    far_lse = swap_stage(packed, orders, last)
    pooled = half_pool(first, mean_weights(probs, lse, far_lse), values)
    (gate, up), token = stage_weights([gate_proj, up_proj], 0, [pooled])
    pooled = join_pair(pooled, orders, last).astype(jnp.bfloat16)
    pooled, token = lax.optimization_barrier((pooled, token))
    (down,), token = stage_weights([down_proj], 0, [token])
    for layer_idx in range(ROUNDS):
        nodes = gather_rows(pooled, orders, last)
        near_sums = expand(nodes, mix, type_gain, norm_gain, gate, up, token, layer_idx)
        if ta_count == 2:
            far_sums = lax.ppermute(near_sums, "ta", [(0, 1), (1, 0)])
        else:
            far_sums = lax.psum(near_sums.astype(jnp.float32), "ta") - near_sums.astype(jnp.float32)
        held, *gives = contract(near_sums, far_sums, down, ta_count == 2)
        final = layer_idx + 1 == ROUNDS
        taken = [
            swap_stage(give, orders, *[stage for stage in range(3) if place >> (2 - stage) & 1])
            for place, give in enumerate(gives, 1)
        ]
        if not final:
            (gate,), token = stage_weights([gate_proj], layer_idx + 1, gives)
            taken, token = lax.optimization_barrier((taken, token))
        for block in taken:
            held = held + block.astype(jnp.float32)
        for stage in range(3, last + 1 if final else last):
            half = held.shape[0] // 2
            held, give = held[:half], held[half:].astype(jnp.bfloat16)
            held = held + swap_stage(give, orders, stage).astype(jnp.float32)
        if not final:
            held = join_pair(held.astype(jnp.bfloat16), orders, last)
        pooled = (pooled[: held.shape[0]].astype(jnp.float32) + held).astype(jnp.bfloat16)
        if not final:
            (up, down), token = stage_weights([up_proj, down_proj], layer_idx + 1, [pooled, token])
    return pooled


def solution(mesh):
    placed = (
        P("gx", None, "ta"),
        P("gx", None, "ta"),
        P("gx", None, "ta"),
        P(),
        P(),
        P(),
        P(None, None, "ta"),
        P(None, "ta"),
        P(None, "ta", "gx"),
        P(None, "ta", "gx"),
        P(None, "gx", "ta"),
    )
    return jax.shard_map(
        per_device, mesh=mesh, in_specs=placed, out_specs=P("gx", "ta"), check_vma=False
    )
```
